512 devices in a mesh: dom: 512 (over x, z, y, core).
Axes of the slice: x: 4, y: 4, z: 16, core: 2. Of those that a mesh axis runs over, the one named last changes fastest.
Arguments:
- x_block: float32 [16, 16, 65536], P(None, None, 'dom'), may hold values from -37 to 37
- p_block: float32 [16, 16, 65536], P(None, None, 'dom'), may hold values from -46 to 46
- f_own: float32 [4, 16, 16, 65536], P(None, None, None, 'dom'), may hold values from -0.75 to 0.75
- f_other: float32 [4, 16, 16, 65536], P(None, None, None, 'dom'), may hold values from -0.75 to 0.75
- node_mass: float32 [16, 65536], P(None, 'dom'), may hold values from 0.5 to 6
- block_cols: int32 [4, 65536], P(None, 'dom'), may hold values from 0 to 159, as said below
- degree: int32 [65536], P('dom'), may hold values from 1 to 4, as said below
- send_list: int32 [16384], P('dom'), may hold values from 0 to 127, as said below
- pair_list: int32 [16384], P('dom'), may hold values from 0 to 127, as said below
- partner: int32 [65536], P('dom'), may hold values from 0 to 159, as said below
Outputs:
- precond: float32 [16, 16, 65536], P(None, None, 'dom')
- gram_a: float32 [48, 48], replicated
- gram_b: float32 [48, 48], replicated
The draws below stay inside these ranges and needn't reach their ends.
Inputs may be any that keep to these rules, and one draw needn't show every extreme that they name: `block_cols`: per partition, slot 0 is live on every row; entries never name the row itself; every extended index from 128 to 159 is named by some slot 0 of each partition. `degree`: some row of every partition has all 4 slots live. `send_list`: per partition 2 * 16 distinct local nodes. `pair_list`: per partition 2 * 16 distinct local nodes. Pairing is symmetric and covers every node once: a local partner's partner is the node itself, node pair_list[j] of a partition has partner 128 + j, and the lower neighbour's pair_list[16 + i] is paired with this partition's pair_list[i].
All inputs are finite; a program needn't handle non-finite values.
Results may differ from the reference program's by a relative error of at most 0.0003.
Values sent between devices are 32-bit elements; how exact they have to be, the bound alone decides.
A program may use at most 64 MiB of HBM per device.

```python
import math
import jax
import jax.numpy as jnp
from jax import lax

S = 16
C = 16
K = 4
NODES_DEV = 128
HALO = 16
PAIRS = 16
N_NODES = 65536
HALO_ALL = 16384
PAIR_ALL = 16384
N_DOM = 512


def graph_parts(key):
    devices = N_NODES // NODES_DEV
    device_keys = jax.random.split(key, devices)

    def one_device(device_key):
        key_send, key_pair, key_degree, key_target, key_first, key_halo, key_pick = jax.random.split(device_key, 7)
        order_send = jax.random.permutation(key_send, NODES_DEV).astype(jnp.int32)
        order_pair = jax.random.permutation(key_pair, NODES_DEV).astype(jnp.int32)
        send_nodes = order_send[:2 * HALO]
        pair_nodes = order_pair[:2 * PAIRS]
        remaining = order_pair[2 * PAIRS:].reshape(-1, 2)
        partners = jnp.zeros((NODES_DEV,), jnp.int32)
        partners = partners.at[remaining[:, 0]].set(remaining[:, 1])
        partners = partners.at[remaining[:, 1]].set(remaining[:, 0])
        partners = partners.at[pair_nodes].set(NODES_DEV + jnp.arange(2 * PAIRS, dtype=jnp.int32))
        degrees = jax.random.randint(key_degree, (NODES_DEV,), 1, K + 1).astype(jnp.int32)
        degrees = degrees.at[order_send[NODES_DEV - 1]].set(K)
        row_index = jnp.arange(NODES_DEV, dtype=jnp.int32)
        local_targets = jax.random.randint(key_target, (K, NODES_DEV), 0, NODES_DEV - 1).astype(jnp.int32)
        local_targets = jnp.where(local_targets >= row_index[None, :], local_targets + 1, local_targets)
        halo_targets = jax.random.randint(key_halo, (K, NODES_DEV), NODES_DEV, NODES_DEV + 2 * HALO).astype(jnp.int32)
        pick = jax.random.randint(key_pick, (K, NODES_DEV), 0, 10).astype(jnp.int32)
        targets = jnp.where(pick == 0, halo_targets, local_targets)
        order_first = jax.random.permutation(key_first, NODES_DEV).astype(jnp.int32)
        first_slot = targets[0].at[order_first[:2 * HALO]].set(NODES_DEV + jnp.arange(2 * HALO, dtype=jnp.int32))
        targets = targets.at[0].set(first_slot)
        return (send_nodes, pair_nodes, partners, degrees, targets)
    return jax.vmap(one_device)(device_keys)


def node_position():
    devices = N_NODES // NODES_DEV
    index = (jnp.arange(N_NODES, dtype=jnp.int32) // NODES_DEV).astype(jnp.float32)
    return index / max(devices - 1, 1)


def draw_block_cols(key, part):
    shared = graph_parts(key)
    return jnp.moveaxis(shared[4], 0, 1).reshape(K, N_NODES)


def draw_degree(key, part):
    shared = graph_parts(key)
    return shared[3].reshape(N_NODES)


def draw_send_list(key, part):
    shared = graph_parts(key)
    return shared[0].reshape(HALO_ALL)


def draw_pair_list(key, part):
    shared = graph_parts(key)
    return shared[1].reshape(PAIR_ALL)


def draw_partner(key, part):
    shared = graph_parts(key)
    return shared[2].reshape(N_NODES)


def draw_x_block(key, part):
    key = jax.random.fold_in(key, 11)
    key_values, key_rows, key_cols = jax.random.split(key, 3)
    trend = jnp.exp((node_position() - 0.5) * math.log(3.0))
    values = jnp.clip(jax.random.normal(key_values, (S, C, N_NODES), jnp.float32), -5.0, 5.0)
    row_scale = jnp.exp(jax.random.uniform(key_rows, (N_NODES,), jnp.float32, math.log(0.3), math.log(3.0)))
    col_scale = jax.random.uniform(key_cols, (C,), jnp.float32, 0.7, 1.4)
    return values * (row_scale * trend)[None, None, :] * col_scale[None, :, None]


def draw_p_block(key, part):
    key = jax.random.fold_in(key, 12)
    key_values, key_rows, key_cols = jax.random.split(key, 3)
    values = jnp.clip(jax.random.normal(key_values, (S, C, N_NODES), jnp.float32), -5.0, 5.0)
    row_scale = jnp.exp(jax.random.uniform(key_rows, (N_NODES,), jnp.float32, math.log(0.3), math.log(3.0)))
    col_scale = jnp.exp(jax.random.uniform(key_cols, (C,), jnp.float32, math.log(0.3), math.log(3.0)))
    return values * row_scale[None, None, :] * col_scale[None, :, None]


def draw_node_mass(key, part):
    key = jax.random.fold_in(key, 13)
    trend = 1.0 + 2.0 * node_position()
    base = jnp.exp(jax.random.uniform(key, (S, N_NODES), jnp.float32, math.log(0.5), math.log(2.0)))
    return base * trend[None, :]


def steps_of(stream_key, shape, cuts, smallest, largest):
    factor_of = 1.0
    for dim, parts in cuts:
        heights = jax.random.uniform(jax.random.fold_in(jax.random.fold_in(stream_key, 6), dim), (parts,), jnp.float32, smallest / len(cuts), largest / len(cuts))
        factor_of = factor_of * jnp.repeat(jnp.exp(heights), shape[dim] // parts).reshape((-1,) + (1,) * (len(shape) - 1 - dim))
    return factor_of


def scatter_about(key, dims, spread, most, shards=(), kind=jnp.bfloat16):
    drawn = spread * jax.random.normal(key, dims, jnp.float32)
    if shards:
        drawn = drawn * steps_of(key, dims, shards, -0.22, 0.18)
    return jnp.clip(drawn, -most, most).astype(kind)


def setup_inputs(seed: int = 0) -> dict:
    key_of = jax.random.split(jax.random.key(seed), 11)
    x_block = draw_x_block(jax.random.fold_in(key_of[10], 71), 0)
    p_block = draw_p_block(jax.random.fold_in(key_of[10], 71), 0)
    f_own = scatter_about(key_of[2], (K, S, S, N_NODES), (4 * S) ** -0.5, 0.75, ((3, 512),), jnp.float32)
    f_other = scatter_about(key_of[3], (K, S, S, N_NODES), (4 * S) ** -0.5, 0.75, ((3, 512),), jnp.float32)
    node_mass = draw_node_mass(jax.random.fold_in(key_of[10], 71), 0)
    block_cols = draw_block_cols(jax.random.fold_in(key_of[10], 71), 0)
    degree = draw_degree(jax.random.fold_in(key_of[10], 71), 0)
    send_list = draw_send_list(jax.random.fold_in(key_of[10], 71), 0)
    pair_list = draw_pair_list(jax.random.fold_in(key_of[10], 71), 0)
    partner = draw_partner(jax.random.fold_in(key_of[10], 71), 0)
    return {"x_block": x_block, "p_block": p_block, "f_own": f_own, "f_other": f_other, "node_mass": node_mass, "block_cols": block_cols, "degree": degree, "send_list": send_list, "pair_list": pair_list, "partner": partner}


smooth_weight = 0.5
coarse_weight = 0.5
highest = lax.Precision.HIGHEST

def slot_mask(block_cols, degree):
    slot_index = lax.broadcasted_iota(jnp.int32, block_cols.shape, 0)
    return (slot_index < degree[None, :]).astype(jnp.float32)

def edge_terms(extended, local_vec, f_own, f_other, block_cols, live_slots):
    remote = jnp.take(extended, block_cols, axis=2)
    mismatch = jnp.einsum('kabn,bwn->kawn', f_own, local_vec, precision=highest) - jnp.einsum('kabn,bwkn->kawn', f_other, remote, precision=highest)
    mismatch = mismatch * live_slots[:, None, None, :]
    own_part = jnp.einsum('kabn,kawn->bwn', f_own, mismatch, precision=highest)
    far_part = jnp.einsum('kabn,kawn->bwkn', f_other, mismatch, precision=highest)
    node_count = local_vec.shape[2]
    gathered = jnp.zeros(extended.shape, jnp.float32).at[:, :, block_cols].add(-far_part)
    return (own_part + gathered[:, :, :node_count], gathered[:, :, node_count:])

def diagonal_terms(f_own, f_other, block_cols, live_slots, extended_len):
    own_square = jnp.einsum('kabn,kn->bn', f_own * f_own, live_slots, precision=highest)
    far_square = jnp.einsum('kabn,kn->bkn', f_other * f_other, live_slots, precision=highest)
    node_count = block_cols.shape[1]
    gathered = jnp.zeros((far_square.shape[0], extended_len), jnp.float32).at[:, block_cols].add(far_square)
    return (own_square + gathered[:, :node_count], gathered[:, node_count:])

def solve_spd(matrix, rhs_matrix):
    factor = jnp.linalg.cholesky(matrix)
    middle = lax.linalg.triangular_solve(factor, rhs_matrix, left_side=True, lower=True)
    return lax.linalg.triangular_solve(factor, middle, left_side=True, lower=True, transpose_a=True)

def to_devices(array, devices):
    leading = array.shape[:-1]
    reshaped = array.reshape(leading + (devices, array.shape[-1] // devices))
    return jnp.moveaxis(reshaped, -2, 0)

def from_devices(array):
    restored = jnp.moveaxis(array, 0, -2)
    return restored.reshape(restored.shape[:-2] + (restored.shape[-2] * restored.shape[-1],))

def pick_last(values, indices):
    return jnp.take(values, indices, axis=-1)

def add_last(values, indices, updates):
    return values.at[..., indices].add(updates)

def reference(x_block, p_block, f_own, f_other, node_mass, block_cols, degree, send_list, pair_list, partner):
    devices = N_DOM
    x_dev = to_devices(x_block, devices)
    p_dev = to_devices(p_block, devices)
    own_dev = to_devices(f_own, devices)
    other_dev = to_devices(f_other, devices)
    mass_dev = to_devices(node_mass, devices)
    cols_dev = to_devices(block_cols, devices)
    degree_dev = degree.reshape(devices, -1)
    sends = send_list.reshape(devices, -1)
    pairs_dev = pair_list.reshape(devices, -1)
    partner_dev = partner.reshape(devices, -1)
    live_dev = jax.vmap(slot_mask)(cols_dev, degree_dev)
    half_halo = sends.shape[1] // 2
    half_pair = pairs_dev.shape[1] // 2
    node_count = x_dev.shape[3]
    stalk_size = x_dev.shape[1]
    columns = x_dev.shape[2]
    norm_scale = 1.0 / (devices * node_count * stalk_size)

    def neighbours(packed, half_size):
        lower = jnp.roll(packed, 1, axis=0)[..., half_size:]
        upper = jnp.roll(packed, -1, axis=0)[..., :half_size]
        return jnp.concatenate([lower, upper], axis=-1)

    def operator(vectors):
        packed = jax.vmap(pick_last)(vectors, sends)
        extended = jnp.concatenate([vectors, neighbours(packed, half_halo)], axis=-1)

        def one_device(device_item):
            return edge_terms(device_item[0], device_item[1], device_item[2], device_item[3], device_item[4], device_item[5])
        inner_part, outgoing = lax.map(one_device, (extended, vectors, own_dev, other_dev, cols_dev, live_dev))
        result = inner_part + mass_dev[:, :, None, :] * vectors
        return jax.vmap(add_last)(result, sends, neighbours(outgoing, half_halo))

    def diag_device(device_item):
        return diagonal_terms(device_item[0], device_item[1], device_item[2], device_item[3], node_count + 2 * half_halo)
    diag_inner, diag_out = lax.map(diag_device, (own_dev, other_dev, cols_dev, live_dev))
    diagonal = jax.vmap(add_last)(mass_dev + diag_inner, sends, neighbours(diag_out, half_halo))

    def partner_sum(vectors):
        packed = jax.vmap(pick_last)(vectors, pairs_dev)
        extended = jnp.concatenate([vectors, neighbours(packed, half_pair)], axis=-1)
        return vectors + jax.vmap(pick_last)(extended, partner_dev)

    def gram_block(left, right):
        return jnp.einsum('dscn,dsen->ce', left, right, precision=highest) * norm_scale
    image_x = operator(x_dev)
    image_p = operator(p_dev)
    gram_xx = gram_block(x_dev, x_dev)
    gram_xa = gram_block(x_dev, image_x)
    quotient = solve_spd(gram_xx, gram_xa)
    residual = image_x - jnp.einsum('dscn,ce->dsen', x_dev, quotient, precision=highest)
    inverse = 1.0 / diagonal[:, :, None, :]
    correction = smooth_weight * residual * inverse
    correction = correction + smooth_weight * (residual - operator(correction)) * inverse
    leftover = residual - operator(correction)
    coarse_rhs = partner_sum(leftover)
    coarse_diag = partner_sum(diagonal[:, :, None, :])
    coarse = coarse_weight * coarse_rhs / coarse_diag
    coarse = coarse + coarse_weight * (coarse_rhs - partner_sum(operator(coarse))) / coarse_diag
    correction = correction + coarse
    correction = correction + smooth_weight * (residual - operator(correction)) * inverse
    correction = correction + smooth_weight * (residual - operator(correction)) * inverse
    precond = correction
    image_w = operator(precond)
    basis = jnp.concatenate([x_dev, precond, p_dev], axis=2)
    images = jnp.concatenate([image_x, image_w, image_p], axis=2)
    gram_a = gram_block(basis, images)
    gram_b = gram_block(basis, basis)
    return (from_devices(precond), gram_a, gram_b)
```

```python
import functools

import jax
import jax.numpy as jnp
from jax import lax
from jax.experimental import pallas as pl
from jax.experimental.pallas import tpu as pltpu
from jax.sharding import PartitionSpec as P

MESH = pl.DeviceIdType.MESH
f32 = jnp.float32
bf16 = jnp.bfloat16
S = 16
C = 16
K = 4
N = 128
H = 32
T = 2
LAST = 8


def iota(shape, dim):
    return lax.broadcasted_iota(jnp.int32, shape, dim)


def one_hot(mask):
    return jnp.where(mask, 1.0, 0.0).astype(f32)


def split(value):
    terms = []
    for t in range(T):
        term = value.astype(bf16)
        terms.append(term)
        if t + 1 < T:
            value = value - term.astype(f32)
    return terms


def dot_nn(a, b):
    return jnp.dot(a, b, preferred_element_type=f32)


def dot_nt(a, b):
    return lax.dot_general(a, b, (((1,), (1,)), ((), ())), preferred_element_type=f32)


def dot_tn(a, b):
    return lax.dot_general(a, b, (((0,), (0,)), ((), ())), preferred_element_type=f32)


class Groups:
    def __init__(self, me, dims):
        self.me, self.dims = me, dims
        self.size = 1
        for _, g in dims:
            self.size *= g
        self.pos = 0
        self.base = me
        for s, g in dims:
            p = lax.rem(lax.div(me, s), g)
            self.pos = self.pos * g + p
            self.base = self.base - p * s

    def device(self, pos):
        d = self.base
        for s, g in reversed(self.dims):
            d = d + lax.rem(pos, g) * s
            pos = lax.div(pos, g)
        return d

    def peer(self, t):
        return lax.rem(self.pos + t, self.size)


def kernel(
    n_dom, ar_dims,
    x_ref, p_ref, own_ref, oth_ref, mass_ref, cols_ref, deg_ref, send_ref, pair_ref, part_ref,
    out_ref, ga_ref, gb_ref,
    B, D, hd, hdc, diag, v, y, e, acc, vv, w_ref, qb, gram1, gram2,
    vcat, wcat, rr, Gl, GH, GHs, ST, Pn, Pr, PPn, Ql, Qh,
    sndh, rcvh, sndc, rcvc, sndd, rcvd, ar_bufs,
    hs, hr, cs, cr, ds, dr, ar_ss, ar_rs,
):
    me = lax.axis_index("dom")
    lower = lax.rem(me + n_dom - 1, n_dom)
    upper = lax.rem(me + 1, n_dom)
    groups = [[Groups(me, dims) for dims in stages] for stages in ar_dims]
    bar_groups = groups[1]

    barrier = pltpu.get_barrier_semaphore()
    for d in (lower, upper):
        pl.semaphore_signal(barrier, inc=1, device_id=(d,), device_id_type=MESH)
    n_bar = 2
    for g in bar_groups:
        n_bar += g.size - 1

        def greet(t, _, g=g):
            pl.semaphore_signal(barrier, inc=1, device_id=(g.device(g.peer(t)),), device_id_type=MESH)
            return 0

        lax.fori_loop(1, g.size, greet, 0)

    def pair_copies(snd, rcv, ss, rs, idx):
        out = []
        for side, (src, dst, dev) in enumerate(((0, 16, lower), (16, 0, upper))):
            out.append(
                pltpu.make_async_remote_copy(
                    snd.at[idx + (pl.ds(src, 16),)],
                    rcv.at[idx + (pl.ds(dst, 16),)],
                    ss.at[idx + (side,)],
                    rs.at[idx + (side,)],
                    device_id=(dev,),
                    device_id_type=MESH,
                )
            )
        return out

    def start(*args):
        for c in pair_copies(*args):
            c.start()

    def wait_recv(*args):
        for c in pair_copies(*args):
            c.wait_recv()

    def wait_send(*args):
        for c in pair_copies(*args):
            c.wait_send()

    def ar_copy(slot, stage, t, receive):
        g = groups[slot][stage]
        peer = g.peer(t)
        buf = ar_bufs[slot][stage]
        at = peer if receive else g.pos
        return pltpu.make_async_remote_copy(
            buf.at[g.pos],
            buf.at[at],
            ar_ss[slot][stage].at[peer],
            ar_rs[slot][stage].at[at],
            device_id=(g.device(peer),),
            device_id_type=MESH,
        )

    def ar_start(slot, stage, value):
        g = groups[slot][stage]
        ar_bufs[slot][stage][g.pos] = value

        def go(t, _):
            ar_copy(slot, stage, t, False).start()
            return 0

        lax.fori_loop(1, g.size, go, 0)

    def ar_finish(slot, stage):
        g = groups[slot][stage]

        def go(t, _):
            ar_copy(slot, stage, t, True).wait_recv()
            return 0

        lax.fori_loop(1, g.size, go, 0)
        buf = ar_bufs[slot][stage]
        total = buf[0]
        for j in range(1, g.size):
            total = total + buf[j]
        return total

    def ar_drain(slot, stage):
        g = groups[slot][stage]

        def go(t, _):
            ar_copy(slot, stage, t, False).wait_send()
            return 0

        lax.fori_loop(1, g.size, go, 0)

    for k in range(K):
        at_k = pl.ds(k * N, N)
        hot = one_hot(iota((N, N), 0) == cols_ref[k : k + 1, :])
        hot_t = hot.T.astype(bf16)
        halo = one_hot(iota((H, N), 0) + N == cols_ref[k : k + 1, :]).astype(bf16)
        hot = hot.astype(bf16)
        for t in range(T):
            Gl[pl.ds(t * N, N), at_k] = hot
            ST[pl.ds((t * K + k) * N, N), :] = hot_t
            GH[:, pl.ds((t * K + k) * N, N)] = halo
            GHs[pl.ds(t * H, H), at_k] = halo
    hot = one_hot(iota((N, N), 0) == part_ref[...]).astype(bf16)
    halo = one_hot(iota((H, N), 0) + N == part_ref[...]).astype(bf16)
    for t in range(T):
        Ql[pl.ds(t * N, N), :] = hot
        Qh[pl.ds(t * H, H), :] = halo

    def column(ref):
        square = jnp.where(iota((H, H), 0) == iota((H, H), 1), ref[...].astype(f32), 0.0)
        return jnp.sum(square, axis=1, keepdims=True)

    lanes = iota((H, N), 1).astype(f32)
    sel = one_hot(lanes == column(send_ref)).astype(bf16)
    psel = one_hot(lanes == column(pair_ref)).astype(bf16)
    for t in range(T):
        Pn[:, pl.ds(t * N, N)] = sel
        Pr[pl.ds(t * H, H), :] = sel
        PPn[:, pl.ds(t * N, N)] = psel

    def bcast_rows(ref, idx, r):
        return ref[idx + (slice(r, r + 1), slice(None))]

    def store_split_w(k, b, value):
        for t, term in enumerate(split(value)):
            wcat[pl.ds(b * C, C), pl.ds(pl.multiple_of(t * K * N + k * N, N), N)] = term

    def store_split_v(ref):
        for b in range(S):
            for t, term in enumerate(split(ref[b])):
                vcat[pl.ds(b * C, C), pl.ds(t * N, N)] = term

    def scatter_halo():
        return dot_nt(GH[...], wcat[...])

    def scatter_local():
        return dot_nn(wcat[...], ST[...])

    def from_halo(rows, matrix):
        return dot_tn(jnp.concatenate(split(rows), axis=0), matrix[...])

    def reverse(ref):
        def body(k, _):
            for half in range(2):
                total = [jnp.zeros((C, N), f32)] * 8
                for a in range(S):
                    value = ref[a]
                    for j in range(8):
                        total[j] = total[j] + bcast_rows(B, (k, a), half * 8 + j) * value
                for j in range(8):
                    store_split_w(k, half * 8 + j, total[j])
            return 0

        lax.fori_loop(0, K, body, 0)

    def far(src):
        def body(k, total):
            total = list(total)
            for b in range(S):
                value = src[k, b]
                for a in range(S):
                    total[a] = total[a] + bcast_rows(B, (k, a), b) * value
            return tuple(total)

        return lax.fori_loop(0, K, body, tuple(jnp.zeros((C, N), f32) for _ in range(S)))

    def own(ref, factor=None):
        total = [jnp.zeros((C, N), f32)] * S
        for b in range(S):
            value = ref[b]
            for a in range(S):
                total[a] = total[a] + bcast_rows(D, (a,), b) * value
        return total

    def gather_local(dst):
        rows = dot_nn(vcat[...], Gl[...])
        for k in range(K):
            dst[k] = rows[:, k * N : (k + 1) * N].reshape(S, C, N)

    def gather_halo(rows, dst):
        got = from_halo(rows, GHs)
        for k in range(K):
            dst[k] = dst[k] + got[:, k * N : (k + 1) * N].reshape(S, C, N)

    def a_start(i, ch, with_own=True):
        src = v.at[ch]
        store_split_v(src)
        sndh[i, ch] = dot_nt(Pn[...], vcat[...])
        start(sndh, rcvh, hs, hr, (i, ch))
        reverse(src)
        sndc[i, ch] = scatter_halo()
        start(sndc, rcvc, cs, cr, (i, ch))
        back = scatter_local().reshape(S, C, N)
        gather_local(vv.at[ch])
        if with_own:
            total = own(src)
            for a in range(S):
                acc[ch, a] = total[a] - back[a]
        else:
            acc[ch] = -back

    def a_finish(i, ch):
        wait_recv(sndh, rcvh, hs, hr, (i, ch))
        gather_halo(rcvh[i, ch], vv.at[ch])
        total = far(vv.at[ch])
        wait_recv(sndc, rcvc, cs, cr, (i, ch))
        got = from_halo(rcvc[i, ch], Pr).reshape(S, C, N)
        for a in range(S):
            y[ch, a] = y[ch, a] - acc[ch, a] + total[a] + got[a]

    def q_start(i, ch):
        store_split_v(y.at[ch])
        sndh[i, ch] = dot_nt(PPn[...], vcat[...])
        start(sndh, rcvh, hs, hr, (i, ch))
        acc[ch] = y[ch] + dot_nn(vcat[...], Ql[...]).reshape(S, C, N)

    def q_finish(i, ch):
        wait_recv(sndh, rcvh, hs, hr, (i, ch))
        got = from_halo(rcvh[i, ch], Qh).reshape(S, C, N)
        for b in range(S):
            value = (acc[ch, b] + got[b]) * hdc[b : b + 1, :]
            v[ch, b] = value
            e[ch, b] = e[ch, b] + value

    def smooth(ch):
        for b in range(S):
            value = y[ch, b] * hd[b : b + 1, :]
            v[ch, b] = value
            e[ch, b] = e[ch, b] + value

    def rr_store(row, ref, sign=1.0):
        for b in range(S):
            for t, term in enumerate(split(sign * ref[b])):
                rr[pl.ds(t * 128 + row, C), pl.ds(b * N, N)] = term

    live = [jnp.where(deg_ref[...] > k, 1.0, 0.0).astype(f32) for k in range(K)]

    def outer(left, right, k):
        def body(s, total):
            value = right[k, s]
            return tuple(total[a] + left[k, s, a : a + 1, :] * value for a in range(S))

        return lax.fori_loop(0, S, body, tuple(jnp.zeros((S, N), f32) for _ in range(S)), unroll=4)

    rr[...] = jnp.zeros_like(rr)
    for k in range(K):
        for a, value in enumerate(outer(oth_ref, oth_ref, k)):
            store_split_w(k, a, value * live[k])
    sndc[LAST, 0] = scatter_halo()
    D[...] = scatter_local().reshape(S, S, N)
    for k in range(K):
        for a, value in enumerate(outer(own_ref, own_ref, k)):
            D[a] = D[a] + value * live[k]
        for a, value in enumerate(outer(own_ref, oth_ref, k)):
            B[k, a] = value * live[k]
    for b in range(S):
        D[b, b : b + 1, :] = D[b, b : b + 1, :] + mass_ref[b : b + 1, :]
    e[...] = jnp.zeros_like(e)
    y[...] = jnp.zeros_like(y)
    v[0] = p_ref[...]
    v[1] = x_ref[...]
    rr_store(0, x_ref)
    rr_store(16, p_ref)

    pl.semaphore_wait(barrier, n_bar)

    start(sndc, rcvc, cs, cr, (LAST, 0))
    a_start(0, 1, False)
    a_start(0, 0, False)

    wait_recv(sndc, rcvc, cs, cr, (LAST, 0))
    D[...] = D[...] + from_halo(rcvc[LAST, 0], Pr).reshape(S, S, N)
    for b in range(S):
        diag[b : b + 1, :] = D[b, b : b + 1, :]
    hd[...] = 0.5 / diag[...]
    dcat = jnp.concatenate(split(diag[...]), axis=1)
    sndd[...] = jnp.zeros_like(sndd)
    sndd[:, 0:S] = dot_nt(PPn[...], dcat)
    start(sndd, rcvd, ds, dr, ())
    for ch in (1, 0):
        total = own(v.at[ch])
        for a in range(S):
            acc[ch, a] = acc[ch, a] + total[a]

    def event(g, _):
        i = 1 + lax.div(g, 2)
        ch = 1 - lax.rem(g, 2)
        coarse_end = (i == 4) | (i == 6)
        coarse_start = (i == 3) | (i == 5)

        @pl.when(jnp.logical_not(coarse_end))
        def _():
            a_finish(i - 1, ch)

        @pl.when((i == 1) & (ch == 1))
        def _():
            rr_store(32, y.at[1], -1.0)

        @pl.when((i == 1) & (ch == 0))
        def _():
            rr_store(48, y.at[0], -1.0)
            y[0] = x_ref[...]

        @pl.when(coarse_end)
        def _():
            q_finish(i - 1, ch)

        @pl.when(jnp.logical_not(coarse_end | coarse_start))
        def _():
            smooth(ch)

        @pl.when(coarse_start)
        def _():
            q_start(i, ch)

        @pl.when(jnp.logical_not(coarse_start))
        def _():
            a_start(i, ch)

        late = ch == 0

        @pl.when(late & (i == 1))
        def _():
            left = jnp.concatenate([rr[0:32, :], rr[128:160, :]], axis=0)
            parts = dot_nt(left, rr[...])
            parts = parts[:, 0:128] + parts[:, 128:256]
            parts = (parts[0:32] + parts[32:64]) * (1.0 / (N * S * n_dom))
            rolled = pltpu.roll(parts[16:32], 64, 1)
            ar_start(0, 0, jnp.where(iota((C, 128), 1) < 64, parts[0:16], rolled))

        @pl.when(late & (i == 2))
        def _():
            wait_recv(sndd, rcvd, ds, dr, ())
            dcat = jnp.concatenate(split(diag[...]), axis=1)
            far_diag = from_halo(rcvd[...], Qh)[0:S]
            hdc[...] = 0.5 / (diag[...] + dot_nn(dcat, Ql[...]) + far_diag)

        stages = len(groups[0])
        for s in range(stages):

            @pl.when(late & (i == (2 + s if s + 1 < stages else 3 + s)))
            def _(s=s):
                total = ar_finish(0, s)
                if s + 1 < stages:
                    ar_start(0, s + 1, total)
                else:
                    gram1[...] = total
                    lane = iota((C, 128), 1)
                    work = jnp.where(lane < 16, total, jnp.where(lane < 32, pltpu.roll(total, 112, 1), 0.0))
                    for j in range(C):
                        col = jnp.sum(jnp.where(lane == j, work, 0.0), axis=1, keepdims=True)
                        row = work[j : j + 1, :] / col[j : j + 1, :]
                        unit = jnp.where(iota((C, 1), 0) == j, 1.0, 0.0)
                        work = work - (col - unit) * row
                    square = jnp.concatenate([work, jnp.zeros((128 - C, 128), f32)], axis=0).T
                    quot_t = square[16:32, :]
                    for j in range(C):
                        col = jnp.sum(jnp.where(lane == j, quot_t, 0.0), axis=1, keepdims=True)
                        qb[j] = jnp.broadcast_to(col, (C, 128))

        return 0

    lax.fori_loop(0, 2 * (LAST - 1), event, 0)

    def last_event(g, _):
        ch = g
        a_finish(LAST - 1, ch)
        for b in range(S):
            e[ch, b] = e[ch, b] + y[ch, b] * hd[b : b + 1, :]
        return 0

    lax.fori_loop(0, 2, last_event, 0)

    def combine(b, _):
        total = -e[1, b]
        for j in range(C):
            total = total - qb[j] * e[0, b, j : j + 1, :]
        w_ref[b] = total
        out_ref[b] = total
        return 0

    lax.fori_loop(0, S, combine, 0)

    store_split_v(w_ref)
    sndh[LAST, 0] = dot_nt(Pn[...], vcat[...])
    start(sndh, rcvh, hs, hr, (LAST, 0))
    rr_store(64, w_ref)
    left = jnp.concatenate([rr[64:80, :], rr[192:208, :]], axis=0)
    parts = dot_nt(left, rr[...])
    parts = parts[:, 0:128] + parts[:, 128:256]
    scale = 1.0 / (N * S * n_dom)
    ar_start(1, 0, (parts[0:16] + parts[16:32]) * scale)
    gather_local(vv.at[0])
    total = own(w_ref)
    for a in range(S):
        acc[0, a] = 0.5 * total[a]
    wait_recv(sndh, rcvh, hs, hr, (LAST, 0))
    gather_halo(rcvh[LAST, 0], vv.at[0])
    total = far(vv.at[0])
    for a in range(S):
        v[0, a] = acc[0, a] - total[a]
    rr_store(80, v.at[0])
    images = jnp.concatenate([rr[80:96, :], rr[208:224, :]], axis=0)
    parts = dot_nt(jnp.concatenate([left, images], axis=0), rr[...])
    parts = parts[:, 0:128] + parts[:, 128:256]
    first = pltpu.roll(parts[0:16] + parts[16:32], 128 - 80, 1)
    second = pltpu.roll(parts[32:48] + parts[48:64], 128 - 64, 1)
    lane = iota((C, 128), 1)
    both = jnp.where(lane < 16, first + second, 0.0) * scale
    small = both[0:8] + pltpu.roll(both[8:16], 16, 1)
    gram2[...] = ar_finish(1, 0)
    ar_start(1, 1, gram2[...])
    ar_start(2, 0, small)

    small = ar_finish(2, 0)
    ar_start(2, 1, small)
    gram2[...] = ar_finish(1, 1)

    def place(value, source, target):
        shift = (target - source) % 128
        moved = pltpu.roll(value, shift, 1) if shift else value
        return jnp.where((lane >= target) & (lane < target + 16), moved, 0.0)

    g1, g2 = gram1[...], gram2[...]
    turned = jnp.concatenate([g2, jnp.zeros((128 - C, 128), f32)], axis=0).T
    xw, pw, xaw, paw = [turned[16 * j : 16 * j + 16, :] for j in range(4)]
    gb_ref[0:16, :] = (place(g1, 0, 0) + place(xw, 0, 16) + place(g1, 16, 32))[:, 0:48]
    gb_ref[16:32, :] = (place(g2, 0, 0) + place(g2, 64, 16) + place(g2, 16, 32))[:, 0:48]
    gb_ref[32:48, :] = (place(g1, 64, 0) + place(pw, 0, 16) + place(g1, 80, 32))[:, 0:48]
    ga_ref[0:16, :] = (place(g1, 32, 0) + place(xaw, 0, 16) + place(g1, 48, 32))[:, 0:48]
    ga_ref[32:48, :] = (place(g1, 96, 0) + place(paw, 0, 16) + place(g1, 112, 32))[:, 0:48]
    wide = place(g2, 32, 0) + place(g2, 48, 32)
    small = ar_finish(2, 1)
    ww = jnp.concatenate([small, pltpu.roll(small, 128 - 16, 1)], axis=0)
    ga_ref[16:32, :] = (wide + place(ww, 0, 16))[:, 0:48]

    def drain(g, _):
        i, ch = lax.div(g, 2), lax.rem(g, 2)
        wait_send(sndh, rcvh, hs, hr, (i, ch))

        @pl.when((i != 3) & (i != 5))
        def _():
            wait_send(sndc, rcvc, cs, cr, (i, ch))

        return 0

    lax.fori_loop(0, 2 * LAST, drain, 0)
    wait_send(sndh, rcvh, hs, hr, (LAST, 0))
    wait_send(sndc, rcvc, cs, cr, (LAST, 0))
    wait_send(sndd, rcvd, ds, dr, ())
    for slot in range(3):
        for s in range(len(groups[slot])):
            ar_drain(slot, s)


def shards(n_dom, ar_dims, x, p, f_own, f_other, mass, cols, degree, send, pair, partner):
    vm = pltpu.VMEM
    dma = pltpu.SemaphoreType.DMA

    def size(dims):
        total = 1
        for _, g in dims:
            total *= g
        return total

    rows = (16, 16, 8)
    scratch = [
        vm((K, S, S, N), f32),
        vm((S, S, N), f32),
        vm((S, N), f32),
        vm((S, N), f32),
        vm((S, N), f32),
        vm((2, S, C, N), f32),
        vm((2, S, C, N), f32),
        vm((2, S, C, N), f32),
        vm((2, S, C, N), f32),
        vm((2, K, S, C, N), f32),
        vm((S, C, N), f32),
        vm((C, C, 128), f32),
        vm((C, 128), f32),
        vm((C, 128), f32),
        vm((S * C, T * N), bf16),
        vm((S * C, T * K * N), bf16),
        vm((256, S * N), bf16),
        vm((T * N, K * N), bf16),
        vm((H, T * K * N), bf16),
        vm((T * H, K * N), bf16),
        vm((T * K * N, N), bf16),
        vm((H, T * N), bf16),
        vm((T * H, N), bf16),
        vm((H, T * N), bf16),
        vm((T * N, N), bf16),
        vm((T * H, N), bf16),
        vm((LAST + 1, 2, H, S * C), f32),
        vm((LAST + 1, 2, H, S * C), f32),
        vm((LAST + 1, 2, H, S * C), f32),
        vm((LAST + 1, 2, H, S * C), f32),
        vm((H, 128), f32),
        vm((H, 128), f32),
        [[vm((size(d), rows[j], 128), f32) for d in st] for j, st in enumerate(ar_dims)],
        dma((LAST + 1, 2, 2)),
        dma((LAST + 1, 2, 2)),
        dma((LAST + 1, 2, 2)),
        dma((LAST + 1, 2, 2)),
        dma((2,)),
        dma((2,)),
        [[dma((size(d),)) for d in st] for st in ar_dims],
        [[dma((size(d),)) for d in st] for st in ar_dims],
    ]
    whole = pl.BlockSpec(memory_space=pltpu.VMEM)
    return pl.pallas_call(
        functools.partial(kernel, n_dom, ar_dims),
        out_shape=(
            jax.ShapeDtypeStruct((S, C, N), f32),
            jax.ShapeDtypeStruct((3 * C, 3 * C), f32),
            jax.ShapeDtypeStruct((3 * C, 3 * C), f32),
        ),
        in_specs=[whole] * 10,
        out_specs=(whole, whole, whole),
        scratch_shapes=scratch,
        compiler_params=pltpu.CompilerParams(
            collective_id=0, has_side_effects=True, vmem_limit_bytes=48 * 1024 * 1024
        ),
    )(
        x, p, f_own, f_other, mass, cols,
        degree.reshape(1, N), send.reshape(1, H), pair.reshape(1, H), partner.reshape(1, N),
    )


def solution(mesh):
    n_dom = mesh.shape["dom"]
    if n_dom == 512:
        near = [[(1, 8)], [(128, 4)], [(8, 4)], [(32, 4)]]
        quick = [[(128, 4), (1, 8)], [(8, 16)]]
    else:
        near = [[(1, 2)], [(2, n_dom // 2)]]
        quick = [[(1, 2)], [(2, n_dom // 2)]]
    row = P(None, "dom")
    return jax.shard_map(
        functools.partial(shards, n_dom, (near, quick, quick)),
        mesh=mesh,
        in_specs=(
            P(None, None, "dom"),
            P(None, None, "dom"),
            P(None, None, None, "dom"),
            P(None, None, None, "dom"),
            row, row, P("dom"), P("dom"), P("dom"), P("dom"),
        ),
        out_specs=(P(None, None, "dom"), P(), P()),
        check_vma=False,
    )
```

```python
import functools

import jax
import jax.numpy as jnp
from jax import lax
from jax.experimental import pallas as pl
from jax.experimental.pallas import tpu as pltpu
from jax.sharding import PartitionSpec as P

MESH = pl.DeviceIdType.MESH
f32 = jnp.float32
bf16 = jnp.bfloat16
S = 16
C = 16
K = 4
N = 128
H = 32
T = 2
LAST = 8


def iota(shape, dim):
    return lax.broadcasted_iota(jnp.int32, shape, dim)


def one_hot(mask):
    return jnp.where(mask, 1.0, 0.0).astype(f32)


def split(value):
    terms = []
    for t in range(T):
        term = value.astype(bf16)
        terms.append(term)
        if t + 1 < T:
            value = value - term.astype(f32)
    return terms


def dot_nn(a, b):
    return jnp.dot(a, b, preferred_element_type=f32)


def dot_nt(a, b):
    return lax.dot_general(a, b, (((1,), (1,)), ((), ())), preferred_element_type=f32)


def dot_tn(a, b):
    return lax.dot_general(a, b, (((0,), (0,)), ((), ())), preferred_element_type=f32)


class Groups:
    def __init__(self, me, dims):
        self.me, self.dims = me, dims
        self.size = 1
        for _, g in dims:
            self.size *= g
        self.pos = 0
        self.base = me
        for s, g in dims:
            p = lax.rem(lax.div(me, s), g)
            self.pos = self.pos * g + p
            self.base = self.base - p * s

    def device(self, pos):
        d = self.base
        for s, g in reversed(self.dims):
            d = d + lax.rem(pos, g) * s
            pos = lax.div(pos, g)
        return d

    def peer(self, t):
        return lax.rem(self.pos + t, self.size)


def kernel(
    n_dom, ar_dims,
    x_in, p_in, own_in, oth_in, mass_in, cols_in, deg_in, send_in, pair_in, part_in,
    out_ref, ga_ref, gb_ref,
    x_ref, p_ref, own_ref, oth_ref, mass_ref, cols_ref, deg_ref, send_ref, pair_ref, part_ref, in_sems,
    B, D, hd, hdc, diag, v, y, e, acc, vv, w_ref, qb, gram1, gram2,
    vcat, wcat, rr, Gl, GS, GHs, Pn, Pr, Ql, Qh, raw,
    sndh, rcvh, sndc, rcvc, sndd, rcvd, ar_bufs,
    hs, hr, cs, cr, ds, dr, ar_ss, ar_rs, vouched,
):
    me = lax.axis_index("dom")
    lower = lax.rem(me + n_dom - 1, n_dom)
    upper = lax.rem(me + 1, n_dom)
    groups = [[Groups(me, dims) for dims in stages] for stages in ar_dims]
    bar_groups = groups[1]

    barrier = pltpu.get_barrier_semaphore()
    for d in (lower, upper):
        pl.semaphore_signal(barrier, inc=1, device_id=(d,), device_id_type=MESH)
    wide, ring = bar_groups
    reach = 4
    n_bar = 2 + wide.size - 1 + 2 * reach

    def greet(g, t):
        pl.semaphore_signal(barrier, inc=1, device_id=(g.device(g.peer(t)),), device_id_type=MESH)

    def greet_wide(t, _):
        greet(wide, t)
        return 0

    for t in range(reach, 0, -1):
        greet(ring, t)
        greet(ring, ring.size - t)
    lax.fori_loop(1, wide.size, greet_wide, 0)

    def vouch():
        for j, t in enumerate((reach, ring.size - reach)):
            pl.semaphore_signal(
                vouched.at[j], inc=1, device_id=(ring.device(ring.peer(t)),), device_id_type=MESH
            )

    def fetch(j):
        src = (x_in, p_in, own_in, oth_in, mass_in, cols_in, deg_in, send_in, pair_in, part_in)[j]
        dst = (x_ref, p_ref, own_ref, oth_ref, mass_ref, cols_ref, deg_ref, send_ref, pair_ref, part_ref)[j]
        return pltpu.make_async_copy(src, dst, in_sems.at[j])

    for j in (5, 9, 7, 8, 6, 3, 2, 0, 1, 4):
        fetch(j).start()

    def pair_copies(snd, rcv, ss, rs, idx):
        out = []
        for side, (src, dst, dev) in enumerate(((0, 16, lower), (16, 0, upper))):
            out.append(
                pltpu.make_async_remote_copy(
                    snd.at[idx + (pl.ds(src, 16),)],
                    rcv.at[idx + (pl.ds(dst, 16),)],
                    ss.at[idx + (side,)],
                    rs.at[idx + (side,)],
                    device_id=(dev,),
                    device_id_type=MESH,
                )
            )
        return out

    def start(*args):
        for c in pair_copies(*args):
            c.start()

    def wait_recv(*args):
        for c in pair_copies(*args):
            c.wait_recv()

    def wait_send(*args):
        for c in pair_copies(*args):
            c.wait_send()

    def ar_copy(slot, stage, t, receive):
        g = groups[slot][stage]
        peer = g.peer(t)
        buf = ar_bufs[slot][stage]
        at = peer if receive else g.pos
        return pltpu.make_async_remote_copy(
            buf.at[g.pos],
            buf.at[at],
            ar_ss[slot][stage].at[peer],
            ar_rs[slot][stage].at[at],
            device_id=(g.device(peer),),
            device_id_type=MESH,
        )

    def ar_start(slot, stage, value):
        g = groups[slot][stage]
        ar_bufs[slot][stage][g.pos] = value

        def go(t, _):
            ar_copy(slot, stage, t, False).start()
            return 0

        lax.fori_loop(1, g.size, go, 0)

    def ar_finish(slot, stage):
        g = groups[slot][stage]

        def go(t, _):
            ar_copy(slot, stage, t, True).wait_recv()
            return 0

        lax.fori_loop(1, g.size, go, 0)
        buf = ar_bufs[slot][stage]
        total = buf[0]
        for j in range(1, g.size):
            total = total + buf[j]
        return total

    def ar_drain(slot, stage):
        g = groups[slot][stage]

        def go(t, _):
            ar_copy(slot, stage, t, False).wait_send()
            return 0

        lax.fori_loop(1, g.size, go, 0)

    for j in (5, 9, 7, 8, 6):
        fetch(j).wait()
    for k in range(K):
        at_k = pl.ds(k * N, N)
        hot = one_hot(iota((N, N), 0) == cols_ref[k : k + 1, :]).astype(bf16)
        halo = one_hot(iota((H, N), 0) + N == cols_ref[k : k + 1, :]).astype(bf16)
        for t in range(T):
            Gl[pl.ds(t * N, N), at_k] = hot
            GS[0:N, pl.ds((k * T + t) * N, N)] = hot
            GS[N : N + H, pl.ds((k * T + t) * N, N)] = halo
            GHs[pl.ds(t * H, H), at_k] = halo
    hot = one_hot(iota((N, N), 0) == part_ref[...]).astype(bf16)
    halo = one_hot(iota((H, N), 0) + N == part_ref[...]).astype(bf16)
    for t in range(T):
        Ql[pl.ds(t * N, N), :] = hot
        Qh[pl.ds(t * H, H), :] = halo

    def column(ref):
        square = jnp.where(iota((H, H), 0) == iota((H, H), 1), ref[...].astype(f32), 0.0)
        return jnp.sum(square, axis=1, keepdims=True)

    lanes = iota((H, N), 1).astype(f32)
    sel = one_hot(lanes == column(send_ref)).astype(bf16)
    psel = one_hot(lanes == column(pair_ref)).astype(bf16)
    for t in range(T):
        Pn[0, :, pl.ds(t * N, N)] = sel
        Pn[1, :, pl.ds(t * N, N)] = psel
        Pr[pl.ds(t * H, H), :] = sel

    def bcast_rows(ref, idx, r):
        return ref[idx + (slice(r, r + 1), slice(None))]

    def store_split_w(k, b, value):
        for t, term in enumerate(split(value)):
            wcat[pl.ds(b * C, C), pl.ds((k * T + t) * N, N)] = term

    def store_split_v(ref):
        for b in range(S):
            for t, term in enumerate(split(ref[b])):
                vcat[pl.ds(b * C, C), pl.ds(t * N, N)] = term

    def scatter_slot(k, total):
        at_k = slice(k * T * N, (k + 1) * T * N)
        part = dot_nt(GS[:, at_k], wcat[:, at_k])
        return part if total is None else total + part

    def turned_rows(rows):
        return jnp.concatenate([rows[0:N, 0:N].T, rows[0:N, N : 2 * N].T], axis=0).reshape(S, C, N)

    def from_halo(rows, matrix):
        return dot_tn(jnp.concatenate(split(rows), axis=0), matrix[...])

    def reverse(ref):
        rows = None
        for k in range(K):
            for half in range(2):
                total = [jnp.zeros((C, N), f32)] * 8
                for a in range(S):
                    value = ref[a]
                    for j in range(8):
                        total[j] = total[j] + bcast_rows(B, (k, a), half * 8 + j) * value
                for j in range(8):
                    store_split_w(k, half * 8 + j, total[j])
            rows = scatter_slot(k, rows)
        return rows

    def far(near, rows, half_way=None):
        rows = jnp.concatenate(split(rows), axis=0).T
        total = [jnp.zeros((C, N), f32)] * S
        for k in range(K):
            if k % 2 == 0:
                got = dot_nn(rows, GHs[:, k * N : (k + 2) * N])
            if k == 2 and half_way is not None:
                half_way()
            part = got[:, (k % 2) * N : (k % 2 + 1) * N].reshape(S, C, N)
            near[k] = near[k] + part
            for b in range(S):
                value = near[k, b]
                for a in range(S):
                    total[a] = total[a] + bcast_rows(B, (k, a), b) * value
        return total

    def own(ref, D):
        total = [jnp.zeros((C, N), f32)] * S
        for b in range(S):
            value = ref[b]
            for a in range(S):
                total[a] = total[a] + bcast_rows(D, (a,), b) * value
        return total

    def gather_local(dst):
        rows = dot_nn(vcat[...], Gl[...])
        for k in range(K):
            dst[k] = rows[:, k * N : (k + 1) * N].reshape(S, C, N)

    def send_rows(i, ch, which):
        sndh[i, ch] = dot_nt(Pn[which], vcat[...])
        start(sndh, rcvh, hs, hr, (i, ch))

    def a_rest(i, ch, enter=None):
        src = v.at[ch]
        rows = reverse(src)
        sndc[i, ch] = rows[N : N + H]
        if enter is not None:
            enter()
        start(sndc, rcvc, cs, cr, (i, ch))
        gather_local(vv.at[ch])
        back = turned_rows(rows)
        total = own(src, D)
        for a in range(S):
            acc[ch, a] = total[a] - back[a]

    def a_finish(i, ch):
        wait_recv(sndh, rcvh, hs, hr, (i, ch))
        total = far(
            vv.at[ch], rcvh[i, ch], lambda: wait_recv(sndc, rcvc, cs, cr, (i, ch))
        )
        got = from_halo(rcvc[i, ch], Pr).reshape(S, C, N)
        return [y[ch, a] - acc[ch, a] + got[a] + total[a] for a in range(S)]

    def split_pair(b, value):
        for t, term in enumerate(split(value)):
            vcat[pl.ds(b * C, C), pl.ds(t * N, N)] = term

    def after_a(i, ch, coarse_start):
        first = i == 1
        which = coarse_start.astype(jnp.int32)
        scale = jnp.where(coarse_start, 1.0, hd[...])
        keep = jnp.where(coarse_start, 0.0, 1.0)
        for b, value in enumerate(a_finish(i - 1, ch)):
            raw[b] = value
            value = jnp.where(first & (ch == 0), x_ref[b], value)
            y[ch, b] = value
            value = value * scale[b : b + 1, :]
            v[ch, b] = value
            e[ch, b] = e[ch, b] + keep * value
            split_pair(b, value)
        send_rows(i, ch, which)

    def after_q(i, ch):
        wait_recv(sndh, rcvh, hs, hr, (i - 1, ch))
        got = from_halo(rcvh[i - 1, ch], Qh).reshape(S, C, N)
        for b in range(S):
            value = (acc[ch, b] + got[b]) * hdc[b : b + 1, :]
            v[ch, b] = value
            e[ch, b] = e[ch, b] + value
            split_pair(b, value)
        send_rows(i, ch, 0)

    def q_rest(ch):
        acc[ch] = y[ch] + dot_nn(vcat[...], Ql[...]).reshape(S, C, N)

    def rr_store(row, ref, sign=1.0):
        for b in range(S):
            for t, term in enumerate(split(sign * ref[b])):
                rr[pl.ds(t * 128 + row, C), pl.ds(b * N, N)] = term

    live = [jnp.where(deg_ref[...] > k, 1.0, 0.0).astype(f32) for k in range(K)]

    def outer(left, right, k):
        def body(s, total):
            value = right[k, s]
            return tuple(total[a] + left[k, s, a : a + 1, :] * value for a in range(S))

        return lax.fori_loop(0, S, body, tuple(jnp.zeros((S, N), f32) for _ in range(S)), unroll=4)

    rr[...] = jnp.zeros_like(rr)
    e[...] = jnp.zeros_like(e)
    y[...] = jnp.zeros_like(y)
    fetch(3).wait()
    rows = None
    for k in range(K):
        for a, value in enumerate(outer(oth_ref, oth_ref, k)):
            store_split_w(k, a, value * live[k])
        rows = scatter_slot(k, rows)
    sndc[LAST, 0] = rows[N : N + H]
    D[...] = turned_rows(rows)
    fetch(2).wait()
    for k in range(K):
        for a, value in enumerate(outer(own_ref, oth_ref, k)):
            B[k, a] = value * live[k]
    fetch(0).wait()
    v[1] = x_ref[...]

    def enter():
        pl.semaphore_wait(barrier, n_bar)
        vouch()
        start(sndc, rcvc, cs, cr, (LAST, 0))

    for k in range(K):
        for a, value in enumerate(outer(own_ref, own_ref, k)):
            D[a] = D[a] + value * live[k]
    fetch(4).wait()
    for b in range(S):
        D[b, b : b + 1, :] = D[b, b : b + 1, :] + mass_ref[b : b + 1, :]
    store_split_v(x_ref)
    sndh[0, 1] = dot_nt(Pn[0], vcat[...])

    def enter_and_send():
        enter()
        start(sndh, rcvh, hs, hr, (0, 1))

    a_rest(0, 1, enter_and_send)
    fetch(1).wait()
    v[0] = p_ref[...]
    store_split_v(p_ref)
    send_rows(0, 0, 0)
    a_rest(0, 0)
    rr_store(0, x_ref)
    rr_store(16, p_ref)

    wait_recv(sndc, rcvc, cs, cr, (LAST, 0))
    w_ref[...] = from_halo(rcvc[LAST, 0], Pr).reshape(S, S, N)
    for ch in (1, 0):
        total = own(v.at[ch], w_ref)
        for a in range(S):
            acc[ch, a] = acc[ch, a] + total[a]
    D[...] = D[...] + w_ref[...]
    for b in range(S):
        diag[b : b + 1, :] = D[b, b : b + 1, :]
    hd[...] = 0.5 / diag[...]
    dcat = jnp.concatenate(split(diag[...]), axis=1)
    sndd[...] = jnp.zeros_like(sndd)
    sndd[:, 0:S] = dot_nt(Pn[1], dcat)
    start(sndd, rcvd, ds, dr, ())

    def event(g, _):
        i = 1 + lax.div(g, 2)
        ch = 1 - lax.rem(g, 2)
        coarse_end = (i == 4) | (i == 6)
        coarse_start = (i == 3) | (i == 5)

        @pl.when(jnp.logical_not(coarse_end))
        def _():
            after_a(i, ch, coarse_start)

        @pl.when(coarse_end)
        def _():
            after_q(i, ch)

        @pl.when(coarse_start)
        def _():
            q_rest(ch)

        @pl.when(jnp.logical_not(coarse_start))
        def _():
            a_rest(i, ch)

        @pl.when((i == 1) & (ch == 1))
        def _():
            rr_store(32, raw, -1.0)

        @pl.when((i == 1) & (ch == 0))
        def _():
            rr_store(48, raw, -1.0)

        late = ch == 0

        @pl.when(late & (i == 1))
        def _():
            left = jnp.concatenate([rr[0:32, :], rr[128:160, :]], axis=0)
            parts = dot_nt(left, rr[...])
            parts = parts[:, 0:128] + parts[:, 128:256]
            parts = (parts[0:32] + parts[32:64]) * (1.0 / (N * S * n_dom))
            rolled = pltpu.roll(parts[16:32], 64, 1)
            ar_start(0, 0, jnp.where(iota((C, 128), 1) < 64, parts[0:16], rolled))
            for j in range(2):
                pl.semaphore_wait(vouched.at[j], 1)

        @pl.when(late & (i == 2))
        def _():
            wait_recv(sndd, rcvd, ds, dr, ())
            dcat = jnp.concatenate(split(diag[...]), axis=1)
            far_diag = from_halo(rcvd[...], Qh)[0:S]
            hdc[...] = 0.5 / (diag[...] + dot_nn(dcat, Ql[...]) + far_diag)

        stages = len(groups[0])
        for s in range(stages):

            @pl.when(late & (i == (2 + s if s + 1 < stages else 3 + s)))
            def _(s=s):
                total = ar_finish(0, s)
                if s + 1 < stages:
                    ar_start(0, s + 1, total)
                else:
                    gram1[...] = total
                    lane = iota((C, 128), 1)
                    work = jnp.where(lane < 16, total, jnp.where(lane < 32, pltpu.roll(total, 112, 1), 0.0))
                    for j in range(C):
                        col = jnp.sum(jnp.where(lane == j, work, 0.0), axis=1, keepdims=True)
                        row = work[j : j + 1, :] / col[j : j + 1, :]
                        unit = jnp.where(iota((C, 1), 0) == j, 1.0, 0.0)
                        work = work - (col - unit) * row
                    square = jnp.concatenate([work, jnp.zeros((128 - C, 128), f32)], axis=0).T
                    quot_t = square[16:32, :]
                    for j in range(C):
                        col = jnp.sum(jnp.where(lane == j, quot_t, 0.0), axis=1, keepdims=True)
                        qb[j] = jnp.broadcast_to(col, (C, 128))

        return 0

    lax.fori_loop(0, 2 * (LAST - 1), event, 0)

    def last_event(g, _):
        ch = g
        for b, value in enumerate(a_finish(LAST - 1, ch)):
            e[ch, b] = e[ch, b] + value * hd[b : b + 1, :]
        return 0

    lax.fori_loop(0, 2, last_event, 0)

    def combine(b, _):
        total = -e[1, b]
        for j in range(C):
            total = total - qb[j] * e[0, b, j : j + 1, :]
        w_ref[b] = total
        return 0

    lax.fori_loop(0, S, combine, 0)

    result = pltpu.make_async_copy(w_ref, out_ref, in_sems.at[10])
    result.start()
    store_split_v(w_ref)
    sndh[LAST, 0] = dot_nt(Pn[0], vcat[...])
    start(sndh, rcvh, hs, hr, (LAST, 0))
    rr_store(64, w_ref)
    lane = iota((C, 128), 1)
    scale = 1.0 / (N * S * n_dom)
    left = jnp.concatenate([rr[64:80, :], rr[192:208, :]], axis=0)
    parts = dot_nt(left, rr[...])
    parts = (parts[0:16, 0:128] + parts[0:16, 128:256] + parts[16:32, 0:128] + parts[16:32, 128:256]) * scale
    low = jnp.where(lane < 64, parts, 0.0)
    ar_start(1, 0, low[0:8] + pltpu.roll(low[8:16], 64, 1))

    diagonal = lax.div(lane, 16) == lax.rem(iota((C, 128), 0), 8)

    def pack_block(block):
        for shift in (16, 32, 64):
            block = block + pltpu.roll(block, shift, 1)
        block = jnp.where(diagonal, block, 0.0)
        top = jnp.sum(block[0:8], axis=0, keepdims=True)
        return jnp.concatenate([top, jnp.sum(block[8:16], axis=0, keepdims=True)], axis=0)

    def unpack_block(pair):
        wide = jnp.concatenate(
            [jnp.broadcast_to(pair[0:1], (8, 128)), jnp.broadcast_to(pair[1:2], (8, 128))], axis=0
        )
        wide = jnp.where(diagonal, wide, 0.0)
        for shift in (16, 32, 64):
            wide = wide + pltpu.roll(wide, shift, 1)
        return wide

    def lanes_from(value, source):
        return jnp.where(lane < 16, pltpu.roll(value, 128 - source, 1), 0.0)

    gram2[0:2, :] = pack_block(lanes_from(parts, 64))
    gather_local(vv.at[0])
    total = own(w_ref, D)
    for a in range(S):
        acc[0, a] = 0.5 * total[a]
    wait_recv(sndh, rcvh, hs, hr, (LAST, 0))
    total = far(vv.at[0], rcvh[LAST, 0])
    for a in range(S):
        v[0, a] = acc[0, a] - total[a]
    rr_store(80, v.at[0])
    images = jnp.concatenate([rr[80:96, :], rr[208:224, :]], axis=0)
    left = jnp.concatenate([rr[64:80, :], rr[192:208, :]], axis=0)
    parts = dot_nt(jnp.concatenate([left, images], axis=0), rr[...])
    parts = parts[:, 0:128] + parts[:, 128:256]
    both = lanes_from(parts[0:16] + parts[16:32], 80) + lanes_from(parts[32:48] + parts[48:64], 64)
    ar_start(2, 0, jnp.concatenate([pack_block(both * scale), gram2[0:2, :]], axis=0))

    def drain(g, _):
        i, ch = lax.div(g, 2), lax.rem(g, 2)
        wait_send(sndh, rcvh, hs, hr, (i, ch))

        @pl.when((i != 3) & (i != 5))
        def _():
            wait_send(sndc, rcvc, cs, cr, (i, ch))

        return 0

    ar_start(1, 1, ar_finish(1, 0))
    lax.fori_loop(0, 2 * LAST, drain, 0)
    wait_send(sndh, rcvh, hs, hr, (LAST, 0))
    wait_send(sndc, rcvc, cs, cr, (LAST, 0))
    wait_send(sndd, rcvd, ds, dr, ())
    ar_start(2, 1, ar_finish(2, 0))
    for s in range(len(groups[0])):
        ar_drain(0, s)
    ar_drain(1, 0)
    ar_drain(2, 0)
    half = ar_finish(1, 1)
    high = pltpu.roll(half, 64, 1)
    g2 = jnp.where(lane < 64, jnp.concatenate([half, high], axis=0), 0.0)

    def place(value, source, target):
        shift = (target - source) % 128
        moved = pltpu.roll(value, shift, 1) if shift else value
        return jnp.where((lane >= target) & (lane < target + 16), moved, 0.0)

    g1 = gram1[...]
    turned = jnp.concatenate([g2, jnp.zeros((128 - C, 128), f32)], axis=0).T
    xw, pw, xaw, paw = [turned[16 * j : 16 * j + 16, :] for j in range(4)]
    gb_ref[0:16, :] = (place(g1, 0, 0) + place(xw, 0, 16) + place(g1, 16, 32))[:, 0:48]
    gb_ref[32:48, :] = (place(g1, 64, 0) + place(pw, 0, 16) + place(g1, 80, 32))[:, 0:48]
    ga_ref[0:16, :] = (place(g1, 32, 0) + place(xaw, 0, 16) + place(g1, 48, 32))[:, 0:48]
    ga_ref[32:48, :] = (place(g1, 96, 0) + place(paw, 0, 16) + place(g1, 112, 32))[:, 0:48]
    wide_a = place(g2, 32, 0) + place(g2, 48, 32)
    wide_b = place(g2, 0, 0) + place(g2, 16, 32)
    ar_drain(1, 1)
    last = ar_finish(2, 1)
    ga_ref[16:32, :] = (wide_a + place(unpack_block(last[0:2]), 16, 16))[:, 0:48]
    gb_ref[16:32, :] = (wide_b + place(unpack_block(last[2:4]), 16, 16))[:, 0:48]
    ar_drain(2, 1)
    result.wait()


def shards(n_dom, ar_dims, x, p, f_own, f_other, mass, cols, degree, send, pair, partner):
    vm = pltpu.VMEM
    dma = pltpu.SemaphoreType.DMA

    def size(dims):
        total = 1
        for _, g in dims:
            total *= g
        return total

    rows = (16, 8, 4)
    i32 = jnp.int32
    scratch = [
        vm((S, C, N), f32),
        vm((S, C, N), f32),
        vm((K, S, S, N), f32),
        vm((K, S, S, N), f32),
        vm((S, N), f32),
        vm((K, N), i32),
        vm((1, N), i32),
        vm((1, H), i32),
        vm((1, H), i32),
        vm((1, N), i32),
        dma((11,)),
        vm((K, S, S, N), f32),
        vm((S, S, N), f32),
        vm((S, N), f32),
        vm((S, N), f32),
        vm((S, N), f32),
        vm((2, S, C, N), f32),
        vm((2, S, C, N), f32),
        vm((2, S, C, N), f32),
        vm((2, S, C, N), f32),
        vm((2, K, S, C, N), f32),
        vm((S, C, N), f32),
        vm((C, C, 128), f32),
        vm((C, 128), f32),
        vm((C, 128), f32),
        vm((S * C, T * N), bf16),
        vm((S * C, T * K * N), bf16),
        vm((256, S * N), bf16),
        vm((T * N, K * N), bf16),
        vm((N + H, T * K * N), bf16),
        vm((T * H, K * N), bf16),
        vm((2, H, T * N), bf16),
        vm((T * H, N), bf16),
        vm((T * N, N), bf16),
        vm((T * H, N), bf16),
        vm((S, C, N), f32),
        vm((LAST + 1, 2, H, S * C), f32),
        vm((LAST + 1, 2, H, S * C), f32),
        vm((LAST + 1, 2, H, S * C), f32),
        vm((LAST + 1, 2, H, S * C), f32),
        vm((H, 128), f32),
        vm((H, 128), f32),
        [[vm((size(d), rows[j], 128), f32) for d in st] for j, st in enumerate(ar_dims)],
        dma((LAST + 1, 2, 2)),
        dma((LAST + 1, 2, 2)),
        dma((LAST + 1, 2, 2)),
        dma((LAST + 1, 2, 2)),
        dma((2,)),
        dma((2,)),
        [[dma((size(d),)) for d in st] for st in ar_dims],
        [[dma((size(d),)) for d in st] for st in ar_dims],
        pltpu.SemaphoreType.REGULAR((2,)),
    ]
    whole = pl.BlockSpec(memory_space=pltpu.VMEM)
    return pl.pallas_call(
        functools.partial(kernel, n_dom, ar_dims),
        out_shape=(
            jax.ShapeDtypeStruct((S, C, N), f32),
            jax.ShapeDtypeStruct((3 * C, 3 * C), f32),
            jax.ShapeDtypeStruct((3 * C, 3 * C), f32),
        ),
        in_specs=[pl.BlockSpec(memory_space=pl.ANY)] * 10,
        out_specs=(pl.BlockSpec(memory_space=pl.ANY), whole, whole),
        scratch_shapes=scratch,
        compiler_params=pltpu.CompilerParams(
            collective_id=0, has_side_effects=True, vmem_limit_bytes=56 * 1024 * 1024
        ),
    )(
        x, p, f_own, f_other, mass, cols,
        degree.reshape(1, N), send.reshape(1, H), pair.reshape(1, H), partner.reshape(1, N),
    )


def solution(mesh):
    n_dom = mesh.shape["dom"]
    if n_dom == 512:
        near = [[(1, 8)], [(128, 4)], [(8, 4)], [(32, 4)]]
        quick = [[(128, 4), (1, 8)], [(8, 16)]]
    else:
        near = [[(1, 2)], [(2, n_dom // 2)]]
        quick = [[(1, 2)], [(2, n_dom // 2)]]
    row = P(None, "dom")
    return jax.shard_map(
        functools.partial(shards, n_dom, (near, quick, quick)),
        mesh=mesh,
        in_specs=(
            P(None, None, "dom"),
            P(None, None, "dom"),
            P(None, None, None, "dom"),
            P(None, None, None, "dom"),
            row, row, P("dom"), P("dom"), P("dom"), P("dom"),
        ),
        out_specs=(P(None, None, "dom"), P(), P()),
        check_vma=False,
    )
```

```python
import functools

import jax
import jax.numpy as jnp
from jax import lax
from jax.experimental import pallas as pl
from jax.experimental.pallas import tpu as pltpu
from jax.sharding import PartitionSpec as P

MESH = pl.DeviceIdType.MESH
f32 = jnp.float32
bf16 = jnp.bfloat16
S = 16
C = 16
K = 4
N = 128
H = 32
T = 2
LAST = 6


def iota(shape, dim):
    return lax.broadcasted_iota(jnp.int32, shape, dim)


def one_hot(mask):
    return jnp.where(mask, 1.0, 0.0).astype(f32)


def split(value):
    terms = []
    for t in range(T):
        term = value.astype(bf16)
        terms.append(term)
        if t + 1 < T:
            value = value - term.astype(f32)
    return terms


def dot_nn(a, b):
    return jnp.dot(a, b, preferred_element_type=f32)


def dot_nt(a, b):
    return lax.dot_general(a, b, (((1,), (1,)), ((), ())), preferred_element_type=f32)


def dot_tn(a, b):
    return lax.dot_general(a, b, (((0,), (0,)), ((), ())), preferred_element_type=f32)


class Groups:
    def __init__(self, me, dims):
        self.me, self.dims = me, dims
        self.size = 1
        for _, g in dims:
            self.size *= g
        self.pos = 0
        self.base = me
        for s, g in dims:
            p = lax.rem(lax.div(me, s), g)
            self.pos = self.pos * g + p
            self.base = self.base - p * s

    def device(self, pos):
        d = self.base
        for s, g in reversed(self.dims):
            d = d + lax.rem(pos, g) * s
            pos = lax.div(pos, g)
        return d

    def peer(self, t):
        return lax.rem(self.pos + t, self.size)


def kernel(
    n_dom, ar_dims,
    x_in, p_in, own_in, oth_in, mass_in, cols_in, deg_in, send_in, pair_in, part_in,
    out_ref, ga_ref, gb_ref,
    x_ref, p_ref, own_ref, oth_ref, mass_ref, cols_ref, deg_ref, send_ref, pair_ref, part_ref, in_sems,
    B, D, hd, hdc, diag, v, y, e, acc, vv, w_ref, qb, gram1, gram2,
    vcat, wcat, rr, Gl, GS, GHs, Pn, Pr, Ql, Qh, raw, PK, GH2, REP, BP, hdcT, TG, SEL, repv, wcat2,
    sndh, rcvh, sndc, rcvc, sndd, rcvd, sndk, rcvk, rcvq, sndm, rcvm, ar_bufs,
    hs, hr, cs, cr, ds, dr, ks, kr, qs, qr, ms, mr, bs, br, ts, tr, ar_ss, ar_rs, vouched,
):
    me = lax.axis_index("dom")
    lower = lax.rem(me + n_dom - 1, n_dom)
    upper = lax.rem(me + 1, n_dom)
    lower2 = lax.rem(me + n_dom - 2, n_dom)
    upper2 = lax.rem(me + 2, n_dom)
    groups = [[Groups(me, dims) for dims in stages] for stages in ar_dims]
    bar_groups = groups[1]

    barrier = pltpu.get_barrier_semaphore()
    for d in (lower, upper, lower2, upper2):
        pl.semaphore_signal(barrier, inc=1, device_id=(d,), device_id_type=MESH)
    wide, ring = bar_groups
    reach = 4
    n_bar = 4 + wide.size - 1 + 2 * reach

    def greet(g, t):
        pl.semaphore_signal(barrier, inc=1, device_id=(g.device(g.peer(t)),), device_id_type=MESH)

    def greet_wide(t, _):
        greet(wide, t)
        return 0

    for t in range(reach, 0, -1):
        greet(ring, t)
        greet(ring, ring.size - t)
    lax.fori_loop(1, wide.size, greet_wide, 0)

    def vouch():
        for j, t in enumerate((reach, ring.size - reach)):
            pl.semaphore_signal(
                vouched.at[j], inc=1, device_id=(ring.device(ring.peer(t)),), device_id_type=MESH
            )

    def fetch(j):
        src = (x_in, p_in, own_in, oth_in, mass_in, cols_in, deg_in, send_in, pair_in, part_in)[j]
        dst = (x_ref, p_ref, own_ref, oth_ref, mass_ref, cols_ref, deg_ref, send_ref, pair_ref, part_ref)[j]
        return pltpu.make_async_copy(src, dst, in_sems.at[j])

    for j in (5, 9, 7, 8, 6, 3, 2, 0, 1, 4):
        fetch(j).start()

    def pair_copies(snd, rcv, ss, rs, idx, far_idx=None):
        out = []
        devices = (lower, upper) if far_idx is None else (lower2, upper2)
        src_idx = idx
        if far_idx is not None:
            idx = far_idx
        for side, (src, dst, dev) in enumerate(((0, 16, devices[0]), (16, 0, devices[1]))):
            out.append(
                pltpu.make_async_remote_copy(
                    snd.at[src_idx + (pl.ds(src, 16),)],
                    rcv.at[idx + (pl.ds(dst, 16),)],
                    ss.at[idx + (side,)],
                    rs.at[idx + (side,)],
                    device_id=(dev,),
                    device_id_type=MESH,
                )
            )
        return out

    def start(*args):
        for c in pair_copies(*args):
            c.start()

    def wait_recv(*args):
        for c in pair_copies(*args):
            c.wait_recv()

    def wait_send(*args):
        for c in pair_copies(*args):
            c.wait_send()

    def both_copies(ref, ss, rs):
        return [
            pltpu.make_async_remote_copy(
                ref.at[0], ref.at[at], ss.at[at], rs.at[at], device_id=(dev,), device_id_type=MESH
            )
            for at, dev in ((1, upper), (2, lower))
        ]

    def ar_copy(slot, stage, t, receive):
        g = groups[slot][stage]
        peer = g.peer(t)
        buf = ar_bufs[slot][stage]
        at = peer if receive else g.pos
        return pltpu.make_async_remote_copy(
            buf.at[g.pos],
            buf.at[at],
            ar_ss[slot][stage].at[peer],
            ar_rs[slot][stage].at[at],
            device_id=(g.device(peer),),
            device_id_type=MESH,
        )

    def ar_start(slot, stage, value):
        g = groups[slot][stage]
        ar_bufs[slot][stage][g.pos] = value

        def go(t, _):
            ar_copy(slot, stage, t, False).start()
            return 0

        lax.fori_loop(1, g.size, go, 0)

    def ar_finish(slot, stage):
        g = groups[slot][stage]

        def go(t, _):
            ar_copy(slot, stage, t, True).wait_recv()
            return 0

        lax.fori_loop(1, g.size, go, 0)
        buf = ar_bufs[slot][stage]
        total = buf[0]
        for j in range(1, g.size):
            total = total + buf[j]
        return total

    def ar_drain(slot, stage):
        g = groups[slot][stage]

        def go(t, _):
            ar_copy(slot, stage, t, False).wait_send()
            return 0

        lax.fori_loop(1, g.size, go, 0)

    for j in (5, 9, 7, 8, 6):
        fetch(j).wait()
    for k in range(K):
        at_k = pl.ds(k * N, N)
        hot = one_hot(iota((N, N), 0) == cols_ref[k : k + 1, :]).astype(bf16)
        halo = one_hot(iota((H, N), 0) + N == cols_ref[k : k + 1, :]).astype(bf16)
        for t in range(T):
            Gl[pl.ds(t * N, N), at_k] = hot
            GS[0:N, pl.ds((k * T + t) * N, N)] = hot
            GS[N : N + H, pl.ds((k * T + t) * N, N)] = halo
            GHs[pl.ds(t * H, H), at_k] = halo
            GH2[pl.ds(t * 2 * H, H), at_k] = halo
    hot = one_hot(iota((N, N), 0) == part_ref[...]).astype(bf16)
    halo = one_hot(iota((H, N), 0) + N == part_ref[...]).astype(bf16)
    for t in range(T):
        Ql[pl.ds(t * N, N), :] = hot
        Qh[pl.ds(t * H, H), :] = halo

    def column(ref):
        square = jnp.where(iota((H, H), 0) == iota((H, H), 1), ref[...].astype(f32), 0.0)
        return jnp.sum(square, axis=1, keepdims=True)

    lanes = iota((H, N), 1).astype(f32)
    sel = one_hot(lanes == column(send_ref)).astype(bf16)
    psel = one_hot(lanes == column(pair_ref)).astype(bf16)
    for t in range(T):
        Pn[0, :, pl.ds(t * N, N)] = sel
        Pn[1, :, pl.ds(t * N, N)] = psel
        for k in range(K):
            PK[:, pl.ds((k * T + t) * N, N)] = jnp.zeros((N, N), bf16)
            PK[pl.ds(k * H, H), pl.ds((k * T + t) * N, N)] = psel
            near_pair = dot_nn(psel, GS[0:N, (k * T) * N : (k * T + 1) * N]).astype(bf16)
            GH2[pl.ds(t * 2 * H + H, H), pl.ds(k * N, N)] = near_pair
        Pr[pl.ds(t * H, H), :] = sel

    def bcast_rows(ref, idx, r):
        return ref[idx + (slice(r, r + 1), slice(None))]

    def store_split_w(k, b, value):
        for t, term in enumerate(split(value)):
            wcat[pl.ds(b * C, C), pl.ds((k * T + t) * N, N)] = term

    def store_split_v(ref):
        for b in range(S):
            for t, term in enumerate(split(ref[b])):
                vcat[pl.ds(b * C, C), pl.ds(t * N, N)] = term

    def scatter_slot(k, total):
        at_k = slice(k * T * N, (k + 1) * T * N)
        part = dot_nt(GS[:, at_k], wcat[:, at_k])
        return part if total is None else total + part

    def turned_rows(rows):
        return jnp.concatenate([rows[0:N, 0:N].T, rows[0:N, N : 2 * N].T], axis=0).reshape(S, C, N)

    def from_halo(rows, matrix):
        return dot_tn(jnp.concatenate(split(rows), axis=0), matrix[...])

    def reverse(ref):
        rows = None
        for k in range(K):
            for half in range(2):
                total = [jnp.zeros((C, N), f32)] * 8
                for a in range(S):
                    value = ref[a]
                    for j in range(8):
                        total[j] = total[j] + bcast_rows(B, (k, a), half * 8 + j) * value
                for j in range(8):
                    store_split_w(k, half * 8 + j, total[j])
            rows = scatter_slot(k, rows)
        return rows

    def far(near, rows, half_way=None, table=None):
        rows = jnp.concatenate(split(rows), axis=0).T
        table = GHs if table is None else table
        total = [jnp.zeros((C, N), f32)] * S
        for k in range(K):
            if k % 2 == 0:
                got = dot_nn(rows, table[:, k * N : (k + 2) * N])
            if k == 2 and half_way is not None:
                half_way()
            part = got[:, (k % 2) * N : (k % 2 + 1) * N].reshape(S, C, N)
            near[k] = near[k] + part
            for b in range(S):
                value = near[k, b]
                for a in range(S):
                    total[a] = total[a] + bcast_rows(B, (k, a), b) * value
        return total

    def own(ref, D):
        total = [jnp.zeros((C, N), f32)] * S
        for b in range(S):
            value = ref[b]
            for a in range(S):
                total[a] = total[a] + bcast_rows(D, (a,), b) * value
        return total

    def gather_local(dst):
        rows = dot_nn(vcat[...], Gl[...])
        for k in range(K):
            dst[k] = rows[:, k * N : (k + 1) * N].reshape(S, C, N)

    def send_rows(i, ch, which):
        sndh[i, ch] = dot_nt(Pn[which], vcat[...])
        start(sndh, rcvh, hs, hr, (i, ch))

    def a_rest(i, ch, enter=None):
        src = v.at[ch]
        rows = reverse(src)
        sndc[i, ch] = rows[N : N + H]
        if enter is not None:
            enter()
        start(sndc, rcvc, cs, cr, (i, ch))
        gather_local(vv.at[ch])
        back = turned_rows(rows)
        total = own(src, D)
        for a in range(S):
            acc[ch, a] = total[a] - back[a]

    def a_finish(i, ch):
        wait_recv(sndh, rcvh, hs, hr, (i, ch))
        total = far(
            vv.at[ch], rcvh[i, ch], lambda: wait_recv(sndc, rcvc, cs, cr, (i, ch))
        )
        got = from_halo(rcvc[i, ch], Pr).reshape(S, C, N)
        return [y[ch, a] - acc[ch, a] + got[a] + total[a] for a in range(S)]

    def split_pair(b, value):
        for t, term in enumerate(split(value)):
            vcat[pl.ds(b * C, C), pl.ds(t * N, N)] = term

    def k_finish(i, ch):
        m = i - 3
        wait_recv(sndh, rcvh, hs, hr, (i, ch))
        wait_recv(sndh, rcvq, qs, qr, (i, ch), (m, ch))
        mine, near, beyond = sndh[i, ch], rcvh[i, ch], rcvq[m, ch]
        own_c = near * hdcT[0]
        lower_c = jnp.concatenate([beyond[0:16], mine[0:16]], axis=0) * hdcT[1]
        upper_c = jnp.concatenate([mine[16:32], beyond[16:32]], axis=0) * hdcT[2]
        terms = split(jnp.concatenate([own_c, lower_c, upper_c], axis=0))
        rep = dot_nn(jnp.concatenate(terms, axis=0).T, REP[...])
        for j in range(3):
            repv[j] = rep[:, j * N : (j + 1) * N].reshape(S, C, N)
        for j in range(3):
            for half in range(2):
                total = [jnp.zeros((C, N), f32)] * 8
                for a in range(S):
                    value = repv[j, a]
                    for b in range(8):
                        total[b] = total[b] + bcast_rows(BP, (j, a), half * 8 + b) * value
                for b in range(8):
                    for t, term in enumerate(split(total[b])):
                        wcat2[pl.ds((half * 8 + b) * C, C), pl.ds((j * T + t) * N, N)] = term
        back = turned_rows(dot_nt(TG[...], wcat2[...]))
        w_ref[...] = from_halo(own_c, Qh).reshape(S, C, N)
        e[ch] = e[ch] + w_ref[...]
        mid = own(w_ref, D)
        for a in range(S):
            acc[ch, a] = acc[ch, a] + mid[a] - back[a]
        wait_recv(sndk, rcvk, ks, kr, (m, ch))
        others = jnp.concatenate([term[H : 3 * H] for term in terms], axis=0)
        rows = rcvk[m, ch] + dot_nn(SEL[...], others)
        total = far(
            vv.at[ch],
            jnp.concatenate([rows, own_c], axis=0),
            lambda: wait_recv(sndc, rcvc, cs, cr, (i, ch)),
            GH2,
        )
        got = from_halo(rcvc[i, ch], Pr).reshape(S, C, N)
        return [y[ch, a] - acc[ch, a] + got[a] + total[a] for a in range(S)]

    def advance(i, ch, coarse_start, values, first):
        which = coarse_start.astype(jnp.int32)
        scale = jnp.where(coarse_start, 1.0, hd[...])
        keep = jnp.where(coarse_start, 0.0, 1.0)
        for b, value in enumerate(values):
            if first is not None:
                raw[b] = value
                value = jnp.where(first, x_ref[b], value)
            y[ch, b] = value
            value = value * scale[b : b + 1, :]
            v[ch, b] = value
            e[ch, b] = e[ch, b] + keep * value
            split_pair(b, value)
        send_rows(i, ch, which)

    def coarse_rest(i, ch):
        m = i - 3
        start(sndh, rcvq, qs, qr, (i, ch), (m, ch))
        pairs = dot_nn(vcat[...], Ql[...]).reshape(S, C, N)
        for b in range(S):
            value = (y[ch, b] + pairs[b]) * hdc[b : b + 1, :]
            v[ch, b] = value
            e[ch, b] = e[ch, b] + value
            split_pair(b, value)
        sndk[m, ch] = dot_nt(Pn[0], vcat[...])
        start(sndk, rcvk, ks, kr, (m, ch))

    def rr_store(row, ref, sign=1.0):
        for b in range(S):
            for t, term in enumerate(split(sign * ref[b])):
                rr[pl.ds(t * 128 + row, C), pl.ds(b * N, N)] = term

    live = [jnp.where(deg_ref[...] > k, 1.0, 0.0).astype(f32) for k in range(K)]

    def outer(left, right, k):
        def body(s, total):
            value = right[k, s]
            return tuple(total[a] + left[k, s, a : a + 1, :] * value for a in range(S))

        return lax.fori_loop(0, S, body, tuple(jnp.zeros((S, N), f32) for _ in range(S)), unroll=4)

    rr[...] = jnp.zeros_like(rr)
    e[...] = jnp.zeros_like(e)
    y[...] = jnp.zeros_like(y)
    fetch(3).wait()
    rows = None
    for k in range(K):
        for a, value in enumerate(outer(oth_ref, oth_ref, k)):
            store_split_w(k, a, value * live[k])
        rows = scatter_slot(k, rows)
    sndc[LAST, 0] = rows[N : N + H]
    D[...] = turned_rows(rows)
    fetch(2).wait()
    for k in range(K):
        for a, value in enumerate(outer(own_ref, oth_ref, k)):
            B[k, a] = value * live[k]
    fetch(0).wait()
    v[1] = x_ref[...]

    def enter():
        pl.semaphore_wait(barrier, n_bar)
        vouch()
        start(sndc, rcvc, cs, cr, (LAST, 0))

    for k in range(K):
        for t, term in enumerate(split(B[k].reshape(S * S, N))):
            wcat[:, pl.ds((k * T + t) * N, N)] = term
    BP[0] = dot_nt(wcat[...], PK[...]).reshape(S, S, N)
    targets = dot_nt(GS[...], PK[...]) * 0.5
    for t in range(T):
        TG[:, pl.ds(t * N, N)] = targets[0:N].astype(bf16)
    sndm[...] = jnp.zeros_like(sndm)
    sndm[:, 0:N] = targets[N : N + H]
    sndm[:, N : 2 * N] = dot_nt(sel, jnp.concatenate([psel, jnp.zeros((N - H, N), bf16)], axis=0))
    for t in range(T):
        for j in range(3):
            row = iota((H, 3 * N), 0)
            col = iota((H, 3 * N), 1)
            hit = (lax.div(col, N) == j) & (lax.rem(col, H) == row)
            REP[pl.ds((t * 3 + j) * H, H), :] = one_hot(hit).astype(bf16)

    for k in range(K):
        for a, value in enumerate(outer(own_ref, own_ref, k)):
            D[a] = D[a] + value * live[k]
    fetch(4).wait()
    for b in range(S):
        D[b, b : b + 1, :] = D[b, b : b + 1, :] + mass_ref[b : b + 1, :]
    store_split_v(x_ref)
    sndh[0, 1] = dot_nt(Pn[0], vcat[...])

    def enter_and_send():
        enter()
        start(sndh, rcvh, hs, hr, (0, 1))

    a_rest(0, 1, enter_and_send)
    fetch(1).wait()
    v[0] = p_ref[...]
    store_split_v(p_ref)
    send_rows(0, 0, 0)
    a_rest(0, 0)
    start(sndm, rcvm, ms, mr, ())
    for c in both_copies(BP, bs, br):
        c.start()
    rr_store(0, x_ref)
    rr_store(16, p_ref)

    wait_recv(sndc, rcvc, cs, cr, (LAST, 0))
    w_ref[...] = from_halo(rcvc[LAST, 0], Pr).reshape(S, S, N)
    for ch in (1, 0):
        total = own(v.at[ch], w_ref)
        for a in range(S):
            acc[ch, a] = acc[ch, a] + total[a]
    D[...] = D[...] + w_ref[...]
    for b in range(S):
        diag[b : b + 1, :] = D[b, b : b + 1, :]
    hd[...] = 0.5 / diag[...]
    dcat = jnp.concatenate(split(diag[...]), axis=1)
    sndd[...] = jnp.zeros_like(sndd)
    sndd[:, 0:S] = dot_nt(Pn[1], dcat)
    start(sndd, rcvd, ds, dr, ())

    def event(g, _):
        i = 1 + lax.div(g, 2)
        ch = 1 - lax.rem(g, 2)
        coarse_end = (i == 4) | (i == 5)
        coarse_start = (i == 3) | (i == 4)

        @pl.when(jnp.logical_not(coarse_end))
        def _():
            advance(i, ch, coarse_start, a_finish(i - 1, ch), (i == 1) & (ch == 0))

        @pl.when(coarse_end)
        def _():
            advance(i, ch, coarse_start, k_finish(i - 1, ch), None)

        @pl.when(coarse_start)
        def _():
            coarse_rest(i, ch)

        a_rest(i, ch)

        @pl.when((i == 1) & (ch == 1))
        def _():
            rr_store(32, raw, -1.0)

        @pl.when((i == 1) & (ch == 0))
        def _():
            rr_store(48, raw, -1.0)

        late = ch == 0

        @pl.when(late & (i == 1))
        def _():
            left = jnp.concatenate([rr[0:32, :], rr[128:160, :]], axis=0)
            parts = dot_nt(left, rr[...])
            parts = parts[:, 0:128] + parts[:, 128:256]
            parts = (parts[0:32] + parts[32:64]) * (1.0 / (N * S * n_dom))
            rolled = pltpu.roll(parts[16:32], 64, 1)
            ar_start(0, 0, jnp.where(iota((C, 128), 1) < 64, parts[0:16], rolled))
            for j in range(2):
                pl.semaphore_wait(vouched.at[j], 1)

        @pl.when(late & (i == 2))
        def _():
            wait_recv(sndd, rcvd, ds, dr, ())
            dcat = jnp.concatenate(split(diag[...]), axis=1)
            far_diag = from_halo(rcvd[...], Qh)[0:S]
            hdc[...] = 0.5 / (diag[...] + dot_nn(dcat, Ql[...]) + far_diag)
            for b in range(S):
                split_pair(b, jnp.broadcast_to(hdc[b : b + 1, :], (C, N)))
            hdcT[0] = dot_nt(Pn[1], vcat[...])
            for c in both_copies(hdcT, ts, tr):
                c.start()

        @pl.when(late & (i == 3))
        def _():
            wait_recv(sndm, rcvm, ms, mr, ())
            for c in both_copies(BP, bs, br):
                c.wait_recv()
            row = iota((H, N), 0)
            for j, keep in ((1, row < 16), (2, row >= 16)):
                there = jnp.where(keep, rcvm[:, 0:N], 0.0).astype(bf16)
                target = dot_tn(Pr[0:H, :], there).astype(bf16)
                for t in range(T):
                    TG[:, pl.ds((j * T + t) * N, N)] = target
            same = rcvm[:, N : 2 * N]
            half = jnp.where(row < 16, same, pltpu.roll(same, H, 1))
            SEL[...] = (half + pltpu.roll(half, 2 * H, 1)).astype(bf16)
            for c in both_copies(hdcT, ts, tr):
                c.wait_recv()

        stages = len(groups[0])
        for s in range(stages):

            @pl.when(late & (i == 2 + s))
            def _(s=s):
                total = ar_finish(0, s)
                if s + 1 < stages:
                    ar_start(0, s + 1, total)
                else:
                    gram1[...] = total
                    lane = iota((C, 128), 1)
                    work = jnp.where(lane < 16, total, jnp.where(lane < 32, pltpu.roll(total, 112, 1), 0.0))
                    for j in range(C):
                        col = jnp.sum(jnp.where(lane == j, work, 0.0), axis=1, keepdims=True)
                        row = work[j : j + 1, :] / col[j : j + 1, :]
                        unit = jnp.where(iota((C, 1), 0) == j, 1.0, 0.0)
                        work = work - (col - unit) * row
                    square = jnp.concatenate([work, jnp.zeros((128 - C, 128), f32)], axis=0).T
                    quot_t = square[16:32, :]
                    for j in range(C):
                        col = jnp.sum(jnp.where(lane == j, quot_t, 0.0), axis=1, keepdims=True)
                        qb[j] = jnp.broadcast_to(col, (C, 128))

        return 0

    lax.fori_loop(0, 2 * (LAST - 1), event, 0)

    def last_event(g, _):
        ch = g
        for b, value in enumerate(a_finish(LAST - 1, ch)):
            e[ch, b] = e[ch, b] + value * hd[b : b + 1, :]
        return 0

    lax.fori_loop(0, 2, last_event, 0)

    def combine(b, _):
        total = -e[1, b]
        for j in range(C):
            total = total - qb[j] * e[0, b, j : j + 1, :]
        w_ref[b] = total
        return 0

    lax.fori_loop(0, S, combine, 0)

    result = pltpu.make_async_copy(w_ref, out_ref, in_sems.at[10])
    result.start()
    store_split_v(w_ref)
    sndh[LAST, 0] = dot_nt(Pn[0], vcat[...])
    start(sndh, rcvh, hs, hr, (LAST, 0))
    rr_store(64, w_ref)
    lane = iota((C, 128), 1)
    scale = 1.0 / (N * S * n_dom)
    left = jnp.concatenate([rr[64:80, :], rr[192:208, :]], axis=0)
    parts = dot_nt(left, rr[...])
    parts = (parts[0:16, 0:128] + parts[0:16, 128:256] + parts[16:32, 0:128] + parts[16:32, 128:256]) * scale
    low = jnp.where(lane < 64, parts, 0.0)
    ar_start(1, 0, low[0:8] + pltpu.roll(low[8:16], 64, 1))

    diagonal = lax.div(lane, 16) == lax.rem(iota((C, 128), 0), 8)

    def pack_block(block):
        for shift in (16, 32, 64):
            block = block + pltpu.roll(block, shift, 1)
        block = jnp.where(diagonal, block, 0.0)
        top = jnp.sum(block[0:8], axis=0, keepdims=True)
        return jnp.concatenate([top, jnp.sum(block[8:16], axis=0, keepdims=True)], axis=0)

    def unpack_block(pair):
        wide = jnp.concatenate(
            [jnp.broadcast_to(pair[0:1], (8, 128)), jnp.broadcast_to(pair[1:2], (8, 128))], axis=0
        )
        wide = jnp.where(diagonal, wide, 0.0)
        for shift in (16, 32, 64):
            wide = wide + pltpu.roll(wide, shift, 1)
        return wide

    def lanes_from(value, source):
        return jnp.where(lane < 16, pltpu.roll(value, 128 - source, 1), 0.0)

    gram2[0:2, :] = pack_block(lanes_from(parts, 64))
    gather_local(vv.at[0])
    total = own(w_ref, D)
    for a in range(S):
        acc[0, a] = 0.5 * total[a]
    wait_recv(sndh, rcvh, hs, hr, (LAST, 0))
    total = far(vv.at[0], rcvh[LAST, 0])
    for a in range(S):
        v[0, a] = acc[0, a] - total[a]
    rr_store(80, v.at[0])
    images = jnp.concatenate([rr[80:96, :], rr[208:224, :]], axis=0)
    left = jnp.concatenate([rr[64:80, :], rr[192:208, :]], axis=0)
    parts = dot_nt(jnp.concatenate([left, images], axis=0), rr[...])
    parts = parts[:, 0:128] + parts[:, 128:256]
    both = lanes_from(parts[0:16] + parts[16:32], 80) + lanes_from(parts[32:48] + parts[48:64], 64)
    ar_start(2, 0, jnp.concatenate([pack_block(both * scale), gram2[0:2, :]], axis=0))

    def drain(g, _):
        i, ch = lax.div(g, 2), lax.rem(g, 2)
        wait_send(sndh, rcvh, hs, hr, (i, ch))
        wait_send(sndc, rcvc, cs, cr, (i, ch))
        return 0

    def drain_coarse(g, _):
        m, ch = lax.div(g, 2), lax.rem(g, 2)
        wait_send(sndk, rcvk, ks, kr, (m, ch))
        wait_send(sndh, rcvq, qs, qr, (m + 3, ch), (m, ch))
        return 0

    ar_start(1, 1, ar_finish(1, 0))
    lax.fori_loop(0, 2 * LAST, drain, 0)
    wait_send(sndh, rcvh, hs, hr, (LAST, 0))
    wait_send(sndc, rcvc, cs, cr, (LAST, 0))
    wait_send(sndd, rcvd, ds, dr, ())
    lax.fori_loop(0, 4, drain_coarse, 0)
    wait_send(sndm, rcvm, ms, mr, ())
    for c in both_copies(BP, bs, br) + both_copies(hdcT, ts, tr):
        c.wait_send()
    ar_start(2, 1, ar_finish(2, 0))
    for s in range(len(groups[0])):
        ar_drain(0, s)
    ar_drain(1, 0)
    ar_drain(2, 0)
    half = ar_finish(1, 1)
    high = pltpu.roll(half, 64, 1)
    g2 = jnp.where(lane < 64, jnp.concatenate([half, high], axis=0), 0.0)

    def place(value, source, target):
        shift = (target - source) % 128
        moved = pltpu.roll(value, shift, 1) if shift else value
        return jnp.where((lane >= target) & (lane < target + 16), moved, 0.0)

    g1 = gram1[...]
    turned = jnp.concatenate([g2, jnp.zeros((128 - C, 128), f32)], axis=0).T
    xw, pw, xaw, paw = [turned[16 * j : 16 * j + 16, :] for j in range(4)]
    gb_ref[0:16, :] = (place(g1, 0, 0) + place(xw, 0, 16) + place(g1, 16, 32))[:, 0:48]
    gb_ref[32:48, :] = (place(g1, 64, 0) + place(pw, 0, 16) + place(g1, 80, 32))[:, 0:48]
    ga_ref[0:16, :] = (place(g1, 32, 0) + place(xaw, 0, 16) + place(g1, 48, 32))[:, 0:48]
    ga_ref[32:48, :] = (place(g1, 96, 0) + place(paw, 0, 16) + place(g1, 112, 32))[:, 0:48]
    wide_a = place(g2, 32, 0) + place(g2, 48, 32)
    wide_b = place(g2, 0, 0) + place(g2, 16, 32)
    ar_drain(1, 1)
    last = ar_finish(2, 1)
    ga_ref[16:32, :] = (wide_a + place(unpack_block(last[0:2]), 16, 16))[:, 0:48]
    gb_ref[16:32, :] = (wide_b + place(unpack_block(last[2:4]), 16, 16))[:, 0:48]
    ar_drain(2, 1)
    result.wait()


def shards(n_dom, ar_dims, x, p, f_own, f_other, mass, cols, degree, send, pair, partner):
    vm = pltpu.VMEM
    dma = pltpu.SemaphoreType.DMA

    def size(dims):
        total = 1
        for _, g in dims:
            total *= g
        return total

    rows = (16, 8, 4)
    i32 = jnp.int32
    scratch = [
        vm((S, C, N), f32),
        vm((S, C, N), f32),
        vm((K, S, S, N), f32),
        vm((K, S, S, N), f32),
        vm((S, N), f32),
        vm((K, N), i32),
        vm((1, N), i32),
        vm((1, H), i32),
        vm((1, H), i32),
        vm((1, N), i32),
        dma((11,)),
        vm((K, S, S, N), f32),
        vm((S, S, N), f32),
        vm((S, N), f32),
        vm((S, N), f32),
        vm((S, N), f32),
        vm((2, S, C, N), f32),
        vm((2, S, C, N), f32),
        vm((2, S, C, N), f32),
        vm((2, S, C, N), f32),
        vm((2, K, S, C, N), f32),
        vm((S, C, N), f32),
        vm((C, C, 128), f32),
        vm((C, 128), f32),
        vm((C, 128), f32),
        vm((S * C, T * N), bf16),
        vm((S * C, T * K * N), bf16),
        vm((256, S * N), bf16),
        vm((T * N, K * N), bf16),
        vm((N + H, T * K * N), bf16),
        vm((T * H, K * N), bf16),
        vm((2, H, T * N), bf16),
        vm((T * H, N), bf16),
        vm((T * N, N), bf16),
        vm((T * H, N), bf16),
        vm((S, C, N), f32),
        vm((N, T * K * N), bf16),
        vm((T * 2 * H, K * N), bf16),
        vm((T * 3 * H, 3 * N), bf16),
        vm((3, S, S, N), f32),
        vm((3, H, S * C), f32),
        vm((N, 3 * T * N), bf16),
        vm((H, N), bf16),
        vm((3, S, C, N), f32),
        vm((S * C, 3 * T * N), bf16),
        vm((LAST + 1, 2, H, S * C), f32),
        vm((LAST + 1, 2, H, S * C), f32),
        vm((LAST + 1, 2, H, S * C), f32),
        vm((LAST + 1, 2, H, S * C), f32),
        vm((H, 128), f32),
        vm((H, 128), f32),
        vm((2, 2, H, S * C), f32),
        vm((2, 2, H, S * C), f32),
        vm((2, 2, H, S * C), f32),
        vm((H, 2 * N), f32),
        vm((H, 2 * N), f32),
        [[vm((size(d), rows[j], 128), f32) for d in st] for j, st in enumerate(ar_dims)],
        dma((LAST + 1, 2, 2)),
        dma((LAST + 1, 2, 2)),
        dma((LAST + 1, 2, 2)),
        dma((LAST + 1, 2, 2)),
        dma((2,)),
        dma((2,)),
        dma((2, 2, 2)),
        dma((2, 2, 2)),
        dma((2, 2, 2)),
        dma((2, 2, 2)),
        dma((2,)),
        dma((2,)),
        dma((3,)),
        dma((3,)),
        dma((3,)),
        dma((3,)),
        [[dma((size(d),)) for d in st] for st in ar_dims],
        [[dma((size(d),)) for d in st] for st in ar_dims],
        pltpu.SemaphoreType.REGULAR((2,)),
    ]
    whole = pl.BlockSpec(memory_space=pltpu.VMEM)
    return pl.pallas_call(
        functools.partial(kernel, n_dom, ar_dims),
        out_shape=(
            jax.ShapeDtypeStruct((S, C, N), f32),
            jax.ShapeDtypeStruct((3 * C, 3 * C), f32),
            jax.ShapeDtypeStruct((3 * C, 3 * C), f32),
        ),
        in_specs=[pl.BlockSpec(memory_space=pl.ANY)] * 10,
        out_specs=(pl.BlockSpec(memory_space=pl.ANY), whole, whole),
        scratch_shapes=scratch,
        compiler_params=pltpu.CompilerParams(
            collective_id=0, has_side_effects=True, vmem_limit_bytes=56 * 1024 * 1024
        ),
    )(
        x, p, f_own, f_other, mass, cols,
        degree.reshape(1, N), send.reshape(1, H), pair.reshape(1, H), partner.reshape(1, N),
    )


def solution(mesh):
    n_dom = mesh.shape["dom"]
    if n_dom == 512:
        near = [[(1, 8)], [(128, 4)], [(8, 4)], [(32, 4)]]
        quick = [[(128, 4), (1, 8)], [(8, 16)]]
    else:
        near = [[(1, 2)], [(2, n_dom // 2)]]
        quick = [[(1, 2)], [(2, n_dom // 2)]]
    row = P(None, "dom")
    return jax.shard_map(
        functools.partial(shards, n_dom, (near, quick, quick)),
        mesh=mesh,
        in_specs=(
            P(None, None, "dom"),
            P(None, None, "dom"),
            P(None, None, None, "dom"),
            P(None, None, None, "dom"),
            row, row, P("dom"), P("dom"), P("dom"), P("dom"),
        ),
        out_specs=(P(None, None, "dom"), P(), P()),
        check_vma=False,
    )
```

```python
import functools

import jax
import jax.numpy as jnp
from jax import lax
from jax.experimental import pallas as pl
from jax.experimental.pallas import tpu as pltpu
from jax.sharding import PartitionSpec as P

MESH = pl.DeviceIdType.MESH
f32 = jnp.float32
bf16 = jnp.bfloat16
S = 16
C = 16
K = 4
N = 128
H = 32
T = 2
LAST = 6


def iota(shape, dim):
    return lax.broadcasted_iota(jnp.int32, shape, dim)


def one_hot(mask):
    return jnp.where(mask, 1.0, 0.0).astype(f32)


def split(value):
    terms = []
    for t in range(T):
        term = value.astype(bf16)
        terms.append(term)
        if t + 1 < T:
            value = value - term.astype(f32)
    return terms


def dot_nn(a, b):
    return jnp.dot(a, b, preferred_element_type=f32)


def dot_nt(a, b):
    return lax.dot_general(a, b, (((1,), (1,)), ((), ())), preferred_element_type=f32)


def dot_tn(a, b):
    return lax.dot_general(a, b, (((0,), (0,)), ((), ())), preferred_element_type=f32)


class Groups:
    def __init__(self, me, dims):
        self.me, self.dims = me, dims
        self.size = 1
        for _, g in dims:
            self.size *= g
        self.pos = 0
        self.base = me
        for s, g in dims:
            p = lax.rem(lax.div(me, s), g)
            self.pos = self.pos * g + p
            self.base = self.base - p * s

    def device(self, pos):
        d = self.base
        for s, g in reversed(self.dims):
            d = d + lax.rem(pos, g) * s
            pos = lax.div(pos, g)
        return d

    def peer(self, t):
        return lax.rem(self.pos + t, self.size)


def kernel(
    n_dom, ar_dims,
    x_in, p_in, own_in, oth_in, mass_in, cols_in, deg_in, send_in, pair_in, part_in,
    out_ref, ga_ref, gb_ref,
    x_ref, p_ref, own_ref, oth_ref, mass_ref, cols_ref, deg_ref, send_ref, pair_ref, part_ref, in_sems,
    B, D, hd, hdc, diag, v, y, e, acc, vv, w_ref, qb, gram1, gram2,
    vcat, wcat, rr, Gl, GS, GHs, Pn, Pr, Ql, Qh, raw, PK, GH2, REP, BP, hdcT, TG, SEL, repv, wcat2, zcat,
    sndh, rcvh, sndc, rcvc, sndd, rcvd, sndk, rcvk, rcvq, sndm, rcvm, ar_bufs,
    hs, hr, cs, cr, ds, dr, ks, kr, qs, qr, ms, mr, bs, br, ts, tr, ar_ss, ar_rs, vouched,
):
    me = lax.axis_index("dom")
    lower = lax.rem(me + n_dom - 1, n_dom)
    upper = lax.rem(me + 1, n_dom)
    lower2 = lax.rem(me + n_dom - 2, n_dom)
    upper2 = lax.rem(me + 2, n_dom)
    groups = [[Groups(me, dims) for dims in stages] for stages in ar_dims]
    bar_groups = groups[1]

    barrier = pltpu.get_barrier_semaphore()
    for d in (lower, upper, lower2, upper2):
        pl.semaphore_signal(barrier, inc=1, device_id=(d,), device_id_type=MESH)
    wide, ring = bar_groups
    reach = 4
    n_bar = 4 + wide.size - 1 + 2 * reach

    def greet(g, t):
        pl.semaphore_signal(barrier, inc=1, device_id=(g.device(g.peer(t)),), device_id_type=MESH)

    def greet_wide(t, _):
        greet(wide, t)
        return 0

    for t in range(reach, 0, -1):
        greet(ring, t)
        greet(ring, ring.size - t)
    lax.fori_loop(1, wide.size, greet_wide, 0)

    def vouch():
        for j, t in enumerate((reach, ring.size - reach)):
            pl.semaphore_signal(
                vouched.at[j], inc=1, device_id=(ring.device(ring.peer(t)),), device_id_type=MESH
            )

    def fetch(j):
        src = (x_in, p_in, own_in, oth_in, mass_in, cols_in, deg_in, send_in, pair_in, part_in)[j]
        dst = (x_ref, p_ref, own_ref, oth_ref, mass_ref, cols_ref, deg_ref, send_ref, pair_ref, part_ref)[j]
        return pltpu.make_async_copy(src, dst, in_sems.at[j])

    for j in (5, 9, 7, 8, 6, 3, 2, 0, 1, 4):
        fetch(j).start()

    def pair_copies(snd, rcv, ss, rs, idx, far_idx=None):
        out = []
        devices = (lower, upper) if far_idx is None else (lower2, upper2)
        src_idx = idx
        if far_idx is not None:
            idx = far_idx
        for side, (src, dst, dev) in enumerate(((0, 16, devices[0]), (16, 0, devices[1]))):
            out.append(
                pltpu.make_async_remote_copy(
                    snd.at[src_idx + (pl.ds(src, 16),)],
                    rcv.at[idx + (pl.ds(dst, 16),)],
                    ss.at[idx + (side,)],
                    rs.at[idx + (side,)],
                    device_id=(dev,),
                    device_id_type=MESH,
                )
            )
        return out

    def start(*args):
        for c in pair_copies(*args):
            c.start()

    def wait_recv(*args):
        for c in pair_copies(*args):
            c.wait_recv()

    def wait_send(*args):
        for c in pair_copies(*args):
            c.wait_send()

    def both_copies(ref, ss, rs):
        return [
            pltpu.make_async_remote_copy(
                ref.at[0], ref.at[at], ss.at[at], rs.at[at], device_id=(dev,), device_id_type=MESH
            )
            for at, dev in ((1, upper), (2, lower))
        ]

    def ar_copy(slot, stage, t, receive):
        g = groups[slot][stage]
        peer = g.peer(t)
        buf = ar_bufs[slot][stage]
        at = peer if receive else g.pos
        return pltpu.make_async_remote_copy(
            buf.at[g.pos],
            buf.at[at],
            ar_ss[slot][stage].at[peer],
            ar_rs[slot][stage].at[at],
            device_id=(g.device(peer),),
            device_id_type=MESH,
        )

    def ar_start(slot, stage, value):
        g = groups[slot][stage]
        ar_bufs[slot][stage][g.pos] = value

        if slot == 2:
            for t in range(1, g.size):
                ar_copy(slot, stage, t, False).start()
            return

        def go(t, _):
            ar_copy(slot, stage, t, False).start()
            return 0

        lax.fori_loop(1, g.size, go, 0)

    def ar_finish(slot, stage):
        g = groups[slot][stage]

        def go(t, _):
            ar_copy(slot, stage, t, True).wait_recv()
            return 0

        if slot == 2:
            for t in range(1, g.size):
                go(t, 0)
        else:
            lax.fori_loop(1, g.size, go, 0)
        buf = ar_bufs[slot][stage]
        total = buf[0]
        for j in range(1, g.size):
            total = total + buf[j]
        return total

    def ar_drain(slot, stage):
        g = groups[slot][stage]

        def go(t, _):
            ar_copy(slot, stage, t, False).wait_send()
            return 0

        lax.fori_loop(1, g.size, go, 0)

    for j in (5, 9, 7, 8, 6):
        fetch(j).wait()
    for k in range(K):
        at_k = pl.ds(k * N, N)
        hot = one_hot(iota((N, N), 0) == cols_ref[k : k + 1, :]).astype(bf16)
        halo = one_hot(iota((H, N), 0) + N == cols_ref[k : k + 1, :]).astype(bf16)
        for t in range(T):
            Gl[pl.ds(t * N, N), at_k] = hot
            GS[0:N, pl.ds((k * T + t) * N, N)] = hot
            GS[N : N + H, pl.ds((k * T + t) * N, N)] = halo
            GHs[pl.ds(t * H, H), at_k] = halo
            GH2[pl.ds(t * 2 * H, H), at_k] = halo
    def column(ref):
        square = jnp.where(iota((H, H), 0) == iota((H, H), 1), ref[...].astype(f32), 0.0)
        return jnp.sum(square, axis=1, keepdims=True)

    lanes = iota((H, N), 1).astype(f32)
    sel = one_hot(lanes == column(send_ref)).astype(bf16)
    for t in range(T):
        Pn[0, :, pl.ds(t * N, N)] = sel

    def bcast_rows(ref, idx, r):
        return ref[idx + (slice(r, r + 1), slice(None))]

    def store_split_w(k, b, value):
        for t, term in enumerate(split(value)):
            wcat[pl.ds(b * C, C), pl.ds((k * T + t) * N, N)] = term

    def store_split_v(ref):
        for b in range(S):
            for t, term in enumerate(split(ref[b])):
                vcat[pl.ds(b * C, C), pl.ds(t * N, N)] = term

    def scatter_slot(k, total):
        at_k = slice(k * T * N, (k + 1) * T * N)
        part = dot_nt(GS[:, at_k], wcat[:, at_k])
        return part if total is None else total + part

    def turned_rows(rows):
        return jnp.concatenate([rows[0:N, 0:N].T, rows[0:N, N : 2 * N].T], axis=0).reshape(S, C, N)

    def from_halo(rows, matrix):
        return dot_tn(jnp.concatenate(split(rows), axis=0), matrix[...])

    def reverse(ref):
        rows = None
        for k in range(K):
            for half in range(2):
                total = [jnp.zeros((C, N), f32)] * 8
                for a in range(S):
                    value = ref[a]
                    for j in range(8):
                        total[j] = total[j] + bcast_rows(B, (k, a), half * 8 + j) * value
                for j in range(8):
                    store_split_w(k, half * 8 + j, total[j])
            rows = scatter_slot(k, rows)
        return rows

    def far(near, rows, half_way=None, table=None):
        rows = jnp.concatenate(split(rows), axis=0).T
        table = GHs if table is None else table
        total = [jnp.zeros((C, N), f32)] * S
        for k in range(K):
            if k % 2 == 0:
                got = dot_nn(rows, table[:, k * N : (k + 2) * N])
            if k == 3 and half_way is not None:
                half_way()
            part = got[:, (k % 2) * N : (k % 2 + 1) * N].reshape(S, C, N)
            near[k] = near[k] + part
            for b in range(S):
                value = near[k, b]
                for a in range(S):
                    total[a] = total[a] + bcast_rows(B, (k, a), b) * value
        return total

    def own(ref, D):
        total = [jnp.zeros((C, N), f32)] * S
        for b in range(S):
            value = ref[b]
            for a in range(S):
                total[a] = total[a] + bcast_rows(D, (a,), b) * value
        return total

    def gather_local(dst):
        rows = dot_nn(vcat[...], Gl[...])
        for k in range(K):
            dst[k] = rows[:, k * N : (k + 1) * N].reshape(S, C, N)

    def send_rows(i, ch, which):
        sndh[i, ch] = dot_nt(Pn[which], vcat[...])
        start(sndh, rcvh, hs, hr, (i, ch))

    def a_rest(i, ch):
        src = v.at[ch]
        rows = reverse(src)
        sndc[i, ch] = rows[N : N + H]
        start(sndc, rcvc, cs, cr, (i, ch))
        a_local(ch, rows)

    def a_local(ch, rows):
        src = v.at[ch]
        gather_local(vv.at[ch])
        back = turned_rows(rows)
        total = own(src, D)
        for a in range(S):
            acc[ch, a] = total[a] - back[a]

    def a_finish(i, ch):
        wait_recv(sndh, rcvh, hs, hr, (i, ch))
        total = far(
            vv.at[ch], rcvh[i, ch], lambda: wait_recv(sndc, rcvc, cs, cr, (i, ch))
        )
        got = from_halo(rcvc[i, ch], Pr).reshape(S, C, N)
        return [y[ch, a] - acc[ch, a] + got[a] + total[a] for a in range(S)]

    def split_pair(b, value):
        for t, term in enumerate(split(value)):
            vcat[pl.ds(b * C, C), pl.ds(t * N, N)] = term

    def k_finish(i, ch):
        m = i - 3
        wait_recv(sndh, rcvh, hs, hr, (i, ch))
        wait_recv(sndh, rcvq, qs, qr, (i, ch), (m, ch))
        mine, near, beyond = sndh[i, ch], rcvh[i, ch], rcvq[m, ch]
        own_c = near * hdcT[0]
        lower_c = jnp.concatenate([beyond[0:16], mine[0:16]], axis=0) * hdcT[1]
        upper_c = jnp.concatenate([mine[16:32], beyond[16:32]], axis=0) * hdcT[2]
        terms = split(jnp.concatenate([own_c, lower_c, upper_c], axis=0))
        rep = dot_nn(jnp.concatenate(terms, axis=0).T, REP[...])
        for j in range(3):
            repv[j] = rep[:, j * N : (j + 1) * N].reshape(S, C, N)
        for j in range(3):
            for half in range(2):
                total = [jnp.zeros((C, N), f32)] * 8
                for a in range(S):
                    value = repv[j, a]
                    for b in range(8):
                        total[b] = total[b] + bcast_rows(BP, (j, a), half * 8 + b) * value
                for b in range(8):
                    for t, term in enumerate(split(total[b])):
                        wcat2[pl.ds((half * 8 + b) * C, C), pl.ds((j * T + t) * N, N)] = term
        back = turned_rows(dot_nt(TG[...], wcat2[...]))
        w_ref[...] = from_halo(own_c, Qh).reshape(S, C, N)
        e[ch] = e[ch] + w_ref[...]
        mid = own(w_ref, D)
        for a in range(S):
            acc[ch, a] = acc[ch, a] + mid[a] - back[a]
        wait_recv(sndk, rcvk, ks, kr, (m, ch))
        others = jnp.concatenate([term[H : 3 * H] for term in terms], axis=0)
        rows = rcvk[m, ch] + dot_nn(SEL[...], others)
        total = far(
            vv.at[ch],
            jnp.concatenate([rows, own_c], axis=0),
            lambda: wait_recv(sndc, rcvc, cs, cr, (i, ch)),
            GH2,
        )
        got = from_halo(rcvc[i, ch], Pr).reshape(S, C, N)
        return [y[ch, a] - acc[ch, a] + got[a] + total[a] for a in range(S)]

    def advance(i, ch, coarse_start, values, first):
        which = coarse_start.astype(jnp.int32)
        scale = jnp.where(coarse_start, 1.0, hd[...])
        keep = jnp.where(coarse_start, 0.0, 1.0)
        for b, value in enumerate(values):
            if first is not None:
                raw[b] = value
                value = jnp.where(first, x_ref[b], value)
            y[ch, b] = value
            value = value * scale[b : b + 1, :]
            v[ch, b] = value
            e[ch, b] = e[ch, b] + keep * value
            split_pair(b, value)
        send_rows(i, ch, which)

    def coarse_rest(i, ch):
        m = i - 3
        start(sndh, rcvq, qs, qr, (i, ch), (m, ch))
        pairs = dot_nn(vcat[...], Ql[...]).reshape(S, C, N)
        for b in range(S):
            value = (y[ch, b] + pairs[b]) * hdc[b : b + 1, :]
            v[ch, b] = value
            e[ch, b] = e[ch, b] + value
            split_pair(b, value)
        sndk[m, ch] = dot_nt(Pn[0], vcat[...])
        start(sndk, rcvk, ks, kr, (m, ch))

    def rr_store(row, ref, sign=1.0):
        for b in range(S):
            for t, term in enumerate(split(sign * ref[b])):
                rr[pl.ds(t * 128 + row, C), pl.ds(b * N, N)] = term

    def later_tables():
        hot = one_hot(iota((N, N), 0) == part_ref[...]).astype(bf16)
        halo = one_hot(iota((H, N), 0) + N == part_ref[...]).astype(bf16)
        for t in range(T):
            Ql[pl.ds(t * N, N), :] = hot
            Qh[pl.ds(t * H, H), :] = halo
        psel = one_hot(lanes == column(pair_ref)).astype(bf16)
        for t in range(T):
            Pn[1, :, pl.ds(t * N, N)] = psel
            for k in range(K):
                PK[:, pl.ds((k * T + t) * N, N)] = jnp.zeros((N, N), bf16)
                PK[pl.ds(k * H, H), pl.ds((k * T + t) * N, N)] = psel
                near_pair = dot_nn(psel, GS[0:N, (k * T) * N : (k * T + 1) * N]).astype(bf16)
                GH2[pl.ds(t * 2 * H + H, H), pl.ds(k * N, N)] = near_pair
            Pr[pl.ds(t * H, H), :] = sel
        for k in range(K):
            for t, term in enumerate(split(B[k].reshape(S * S, N))):
                wcat[:, pl.ds((k * T + t) * N, N)] = term
        BP[0] = dot_nt(wcat[...], PK[...]).reshape(S, S, N)
        targets = dot_nt(GS[...], PK[...]) * 0.5
        for t in range(T):
            TG[:, pl.ds(t * N, N)] = targets[0:N].astype(bf16)
        sndm[...] = jnp.zeros_like(sndm)
        sndm[:, 0:N] = targets[N : N + H]
        sndm[:, N : 2 * N] = dot_nt(sel, jnp.concatenate([psel, jnp.zeros((N - H, N), bf16)], axis=0))
        for t in range(T):
            for j in range(3):
                row = iota((H, 3 * N), 0)
                col = iota((H, 3 * N), 1)
                hit = (lax.div(col, N) == j) & (lax.rem(col, H) == row)
                REP[pl.ds((t * 3 + j) * H, H), :] = one_hot(hit).astype(bf16)

    live = [jnp.where(deg_ref[...] > k, 1.0, 0.0).astype(f32) for k in range(K)]

    def outer(left, right, k):
        def body(s, total):
            value = right[k, s]
            return tuple(total[a] + left[k, s, a : a + 1, :] * value for a in range(S))

        return lax.fori_loop(0, S, body, tuple(jnp.zeros((S, N), f32) for _ in range(S)), unroll=4)

    fetch(3).wait()
    rows = None
    for k in range(K):
        for a, value in enumerate(outer(oth_ref, oth_ref, k)):
            store_split_w(k, a, value * live[k])
        rows = scatter_slot(k, rows)
    sndc[LAST, 0] = rows[N : N + H]
    D[...] = turned_rows(rows)
    fetch(2).wait()
    for k in range(K):
        for a, value in enumerate(outer(own_ref, oth_ref, k)):
            B[k, a] = value * live[k]
    fetch(0).wait()
    v[1] = x_ref[...]
    store_split_v(x_ref)
    sndh[0, 1] = dot_nt(Pn[0], vcat[...])
    rows = reverse(v.at[1])
    sndc[0, 1] = rows[N : N + H]
    pl.semaphore_wait(barrier, n_bar)
    vouch()
    start(sndh, rcvh, hs, hr, (0, 1))
    start(sndc, rcvc, cs, cr, (LAST, 0))
    start(sndc, rcvc, cs, cr, (0, 1))
    for k in range(K):
        for a, value in enumerate(outer(own_ref, own_ref, k)):
            D[a] = D[a] + value * live[k]
    fetch(4).wait()
    for b in range(S):
        D[b, b : b + 1, :] = D[b, b : b + 1, :] + mass_ref[b : b + 1, :]
    a_local(1, rows)
    fetch(1).wait()
    v[0] = p_ref[...]
    store_split_v(p_ref)
    send_rows(0, 0, 0)
    a_rest(0, 0)
    e[...] = jnp.zeros_like(e)
    y[...] = jnp.zeros_like(y)
    rr[...] = jnp.zeros_like(rr)
    rr_store(0, x_ref)
    rr_store(16, p_ref)
    later_tables()
    start(sndm, rcvm, ms, mr, ())
    for c in both_copies(BP, bs, br):
        c.start()

    wait_recv(sndc, rcvc, cs, cr, (LAST, 0))
    w_ref[...] = from_halo(rcvc[LAST, 0], Pr).reshape(S, S, N)
    for ch in (1, 0):
        total = own(v.at[ch], w_ref)
        for a in range(S):
            acc[ch, a] = acc[ch, a] + total[a]
    D[...] = D[...] + w_ref[...]
    for b in range(S):
        diag[b : b + 1, :] = D[b, b : b + 1, :]
    hd[...] = 0.5 / diag[...]
    dcat = jnp.concatenate(split(diag[...]), axis=1)
    sndd[...] = jnp.zeros_like(sndd)
    sndd[:, 0:S] = dot_nt(Pn[1], dcat)
    start(sndd, rcvd, ds, dr, ())

    def event(g, _):
        i = 1 + lax.div(g, 2)
        ch = 1 - lax.rem(g, 2)
        coarse_end = (i == 4) | (i == 5)
        coarse_start = (i == 3) | (i == 4)

        @pl.when(jnp.logical_not(coarse_end))
        def _():
            advance(i, ch, coarse_start, a_finish(i - 1, ch), (i == 1) & (ch == 0))

        @pl.when(coarse_end)
        def _():
            advance(i, ch, coarse_start, k_finish(i - 1, ch), None)

        @pl.when(coarse_start)
        def _():
            coarse_rest(i, ch)

        a_rest(i, ch)

        @pl.when((i == 1) & (ch == 1))
        def _():
            rr_store(32, raw, -1.0)

        @pl.when((i == 1) & (ch == 0))
        def _():
            rr_store(48, raw, -1.0)

        late = ch == 0

        @pl.when(late & (i == 1))
        def _():
            left = jnp.concatenate([rr[0:32, :], rr[128:160, :]], axis=0)
            parts = dot_nt(left, rr[...])
            parts = parts[:, 0:128] + parts[:, 128:256]
            parts = (parts[0:32] + parts[32:64]) * (1.0 / (N * S * n_dom))
            rolled = pltpu.roll(parts[16:32], 64, 1)
            ar_start(0, 0, jnp.where(iota((C, 128), 1) < 64, parts[0:16], rolled))
            for j in range(2):
                pl.semaphore_wait(vouched.at[j], 1)

        @pl.when(late & (i == 2))
        def _():
            wait_recv(sndd, rcvd, ds, dr, ())
            dcat = jnp.concatenate(split(diag[...]), axis=1)
            far_diag = from_halo(rcvd[...], Qh)[0:S]
            hdc[...] = 0.5 / (diag[...] + dot_nn(dcat, Ql[...]) + far_diag)
            for b in range(S):
                split_pair(b, jnp.broadcast_to(hdc[b : b + 1, :], (C, N)))
            hdcT[0] = dot_nt(Pn[1], vcat[...])
            for c in both_copies(hdcT, ts, tr):
                c.start()

        @pl.when(late & (i == 3))
        def _():
            wait_recv(sndm, rcvm, ms, mr, ())
            for c in both_copies(BP, bs, br):
                c.wait_recv()
            row = iota((H, N), 0)
            for j, keep in ((1, row < 16), (2, row >= 16)):
                there = jnp.where(keep, rcvm[:, 0:N], 0.0).astype(bf16)
                target = dot_tn(Pr[0:H, :], there).astype(bf16)
                for t in range(T):
                    TG[:, pl.ds((j * T + t) * N, N)] = target
            same = rcvm[:, N : 2 * N]
            half = jnp.where(row < 16, same, pltpu.roll(same, H, 1))
            SEL[...] = (half + pltpu.roll(half, 2 * H, 1)).astype(bf16)
            for c in both_copies(hdcT, ts, tr):
                c.wait_recv()

        stages = len(groups[0])
        for s in range(stages):

            @pl.when(late & (i == 2 + s))
            def _(s=s):
                total = ar_finish(0, s)
                if s + 1 < stages:
                    ar_start(0, s + 1, total)
                else:
                    gram1[...] = total
                    lane = iota((C, 128), 1)
                    work = jnp.where(lane < 16, total, jnp.where(lane < 32, pltpu.roll(total, 112, 1), 0.0))
                    for j in range(C):
                        col = jnp.sum(jnp.where(lane == j, work, 0.0), axis=1, keepdims=True)
                        row = work[j : j + 1, :] / col[j : j + 1, :]
                        unit = jnp.where(iota((C, 1), 0) == j, 1.0, 0.0)
                        work = work - (col - unit) * row
                    square = jnp.concatenate([work, jnp.zeros((128 - C, 128), f32)], axis=0).T
                    quot_t = square[16:32, :]
                    for j in range(C):
                        col = jnp.sum(jnp.where(lane == j, quot_t, 0.0), axis=1, keepdims=True)
                        qb[j] = jnp.broadcast_to(col, (C, 128))

        return 0

    lax.fori_loop(0, 2 * (LAST - 1), event, 0)

    def last_event(g, _):
        ch = g
        for b, value in enumerate(a_finish(LAST - 1, ch)):
            e[ch, b] = e[ch, b] + value * hd[b : b + 1, :]
        return 0

    lax.fori_loop(0, 2, last_event, 0)

    def combine(b, _):
        total = -e[1, b]
        for j in range(C):
            total = total - qb[j] * e[0, b, j : j + 1, :]
        w_ref[b] = total
        return 0

    lax.fori_loop(0, S, combine, 0)

    result = pltpu.make_async_copy(w_ref, out_ref, in_sems.at[10])
    result.start()
    store_split_v(w_ref)
    sndh[LAST, 0] = dot_nt(Pn[0], vcat[...])
    start(sndh, rcvh, hs, hr, (LAST, 0))
    rr_store(64, w_ref)
    lane = iota((C, 128), 1)
    scale = 1.0 / (N * S * n_dom)
    left = jnp.concatenate([rr[64:80, :], rr[192:208, :]], axis=0)
    parts = dot_nt(left, rr[...])
    parts = (parts[0:16, 0:128] + parts[0:16, 128:256] + parts[16:32, 0:128] + parts[16:32, 128:256]) * scale
    low = jnp.where(lane < 64, parts, 0.0)
    ar_start(1, 0, low[0:8] + pltpu.roll(low[8:16], 64, 1))

    diagonal = lax.div(lane, 16) == lax.rem(iota((C, 128), 0), 8)

    def pack_block(block):
        for shift in (16, 32, 64):
            block = block + pltpu.roll(block, shift, 1)
        block = jnp.where(diagonal, block, 0.0)
        top = jnp.sum(block[0:8], axis=0, keepdims=True)
        return jnp.concatenate([top, jnp.sum(block[8:16], axis=0, keepdims=True)], axis=0)

    def unpack_block(pair):
        wide = jnp.concatenate(
            [jnp.broadcast_to(pair[0:1], (8, 128)), jnp.broadcast_to(pair[1:2], (8, 128))], axis=0
        )
        wide = jnp.where(diagonal, wide, 0.0)
        for shift in (16, 32, 64):
            wide = wide + pltpu.roll(wide, shift, 1)
        return wide

    def lanes_from(value, source):
        return jnp.where(lane < 16, pltpu.roll(value, 128 - source, 1), 0.0)

    gram2[0:2, :] = pack_block(lanes_from(parts, 64))
    rows = reverse(w_ref)
    turned = jnp.concatenate([term[0 : 2 * H] for term in split(jnp.concatenate([rows[N : N + H], rows[N : N + H]], axis=0))], axis=0).T
    zcat[...] = turned
    gather_local(vv.at[0])
    back = turned_rows(rows)
    near = vv.at[0]
    mid = own(w_ref, D)
    for a in range(S):
        acc[0, a] = mid[a] - back[a]
    mid = far(near, jnp.zeros((H, S * C), f32))
    for a in range(S):
        v[0, a] = acc[0, a] - mid[a]
    rr_store(80, v.at[0])
    parts = dot_nt(left, rr[...])
    parts = parts[0:16, 0:128] + parts[0:16, 128:256] + parts[16:32, 0:128] + parts[16:32, 128:256]
    gram2[2:4, :] = pack_block(lanes_from(parts, 80) * scale)
    wait_recv(sndh, rcvh, hs, hr, (LAST, 0))
    terms = split(rcvh[LAST, 0])
    edges = dot_nn(zcat[...], jnp.concatenate([terms[0], terms[1], terms[0], terms[1]], axis=0))
    same = lax.div(iota((S * C, S * C), 0), C) == lax.div(iota((S * C, S * C), 1), C)
    edges = jnp.sum(jnp.where(same, edges, 0.0).reshape(S, C, S * C), axis=0)
    edges = edges[:, 0:128] + edges[:, 128:256]
    ar_start(2, 0, jnp.concatenate([gram2[2:4, :] - pack_block(edges * (2.0 * scale)), gram2[0:2, :]], axis=0))

    def drain(g, _):
        i, ch = lax.div(g, 2), lax.rem(g, 2)
        wait_send(sndh, rcvh, hs, hr, (i, ch))
        wait_send(sndc, rcvc, cs, cr, (i, ch))
        return 0

    def drain_coarse(g, _):
        m, ch = lax.div(g, 2), lax.rem(g, 2)
        wait_send(sndk, rcvk, ks, kr, (m, ch))
        wait_send(sndh, rcvq, qs, qr, (m + 3, ch), (m, ch))
        return 0

    ar_start(1, 1, ar_finish(1, 0))
    lax.fori_loop(0, 2 * LAST, drain, 0)
    wait_send(sndh, rcvh, hs, hr, (LAST, 0))
    wait_send(sndc, rcvc, cs, cr, (LAST, 0))
    wait_send(sndd, rcvd, ds, dr, ())
    lax.fori_loop(0, 4, drain_coarse, 0)
    wait_send(sndm, rcvm, ms, mr, ())
    for c in both_copies(BP, bs, br) + both_copies(hdcT, ts, tr):
        c.wait_send()
    ar_start(2, 1, ar_finish(2, 0))
    for s in range(len(groups[0])):
        ar_drain(0, s)
    ar_drain(1, 0)
    ar_drain(2, 0)
    half = ar_finish(1, 1)
    high = pltpu.roll(half, 64, 1)
    g2 = jnp.where(lane < 64, jnp.concatenate([half, high], axis=0), 0.0)

    def place(value, source, target):
        shift = (target - source) % 128
        moved = pltpu.roll(value, shift, 1) if shift else value
        return jnp.where((lane >= target) & (lane < target + 16), moved, 0.0)

    g1 = gram1[...]
    turned = jnp.concatenate([g2, jnp.zeros((128 - C, 128), f32)], axis=0).T
    xw, pw, xaw, paw = [turned[16 * j : 16 * j + 16, :] for j in range(4)]
    gb_ref[0:16, :] = (place(g1, 0, 0) + place(xw, 0, 16) + place(g1, 16, 32))[:, 0:48]
    gb_ref[32:48, :] = (place(g1, 64, 0) + place(pw, 0, 16) + place(g1, 80, 32))[:, 0:48]
    ga_ref[0:16, :] = (place(g1, 32, 0) + place(xaw, 0, 16) + place(g1, 48, 32))[:, 0:48]
    ga_ref[32:48, :] = (place(g1, 96, 0) + place(paw, 0, 16) + place(g1, 112, 32))[:, 0:48]
    wide_a = place(g2, 32, 0) + place(g2, 48, 32)
    wide_b = place(g2, 0, 0) + place(g2, 16, 32)
    ar_drain(1, 1)
    last = ar_finish(2, 1)
    image = unpack_block(last[0:2])
    square = jnp.concatenate([jnp.where(lane < 16, image, 0.0), jnp.zeros((128 - C, 128), f32)], axis=0).T
    image = 0.5 * (jnp.where(lane < 16, image, 0.0) + square[0:16, :])
    ga_ref[16:32, :] = (wide_a + place(image, 0, 16))[:, 0:48]
    gb_ref[16:32, :] = (wide_b + place(unpack_block(last[2:4]), 16, 16))[:, 0:48]
    ar_drain(2, 1)
    result.wait()


def move_results(a_in, b_in, c_in, a_out, b_out, c_out, sems):
    pairs = ((a_in, a_out), (b_in, b_out), (c_in, c_out))
    copies = [pltpu.make_async_copy(src, dst, sems.at[j]) for j, (src, dst) in enumerate(pairs)]
    for c in copies:
        c.start()
    for c in copies:
        c.wait()


def shards(n_dom, ar_dims, x, p, f_own, f_other, mass, cols, degree, send, pair, partner):
    vm = pltpu.VMEM
    dma = pltpu.SemaphoreType.DMA

    def size(dims):
        total = 1
        for _, g in dims:
            total *= g
        return total

    rows = (16, 8, 4)
    i32 = jnp.int32
    scratch = [
        vm((S, C, N), f32),
        vm((S, C, N), f32),
        vm((K, S, S, N), f32),
        vm((K, S, S, N), f32),
        vm((S, N), f32),
        vm((K, N), i32),
        vm((1, N), i32),
        vm((1, H), i32),
        vm((1, H), i32),
        vm((1, N), i32),
        dma((11,)),
        vm((K, S, S, N), f32),
        vm((S, S, N), f32),
        vm((S, N), f32),
        vm((S, N), f32),
        vm((S, N), f32),
        vm((2, S, C, N), f32),
        vm((2, S, C, N), f32),
        vm((2, S, C, N), f32),
        vm((2, S, C, N), f32),
        vm((2, K, S, C, N), f32),
        vm((S, C, N), f32),
        vm((C, C, 128), f32),
        vm((C, 128), f32),
        vm((C, 128), f32),
        vm((S * C, T * N), bf16),
        vm((S * C, T * K * N), bf16),
        vm((256, S * N), bf16),
        vm((T * N, K * N), bf16),
        vm((N + H, T * K * N), bf16),
        vm((T * H, K * N), bf16),
        vm((2, H, T * N), bf16),
        vm((T * H, N), bf16),
        vm((T * N, N), bf16),
        vm((T * H, N), bf16),
        vm((S, C, N), f32),
        vm((N, T * K * N), bf16),
        vm((T * 2 * H, K * N), bf16),
        vm((T * 3 * H, 3 * N), bf16),
        vm((3, S, S, N), f32),
        vm((3, H, S * C), f32),
        vm((N, 3 * T * N), bf16),
        vm((H, N), bf16),
        vm((3, S, C, N), f32),
        vm((S * C, 3 * T * N), bf16),
        vm((S * C, 2 * T * H), bf16),
        vm((LAST + 1, 2, H, S * C), f32),
        vm((LAST + 1, 2, H, S * C), f32),
        vm((LAST + 1, 2, H, S * C), f32),
        vm((LAST + 1, 2, H, S * C), f32),
        vm((H, 128), f32),
        vm((H, 128), f32),
        vm((2, 2, H, S * C), f32),
        vm((2, 2, H, S * C), f32),
        vm((2, 2, H, S * C), f32),
        vm((H, 2 * N), f32),
        vm((H, 2 * N), f32),
        [[vm((size(d), rows[j], 128), f32) for d in st] for j, st in enumerate(ar_dims)],
        dma((LAST + 1, 2, 2)),
        dma((LAST + 1, 2, 2)),
        dma((LAST + 1, 2, 2)),
        dma((LAST + 1, 2, 2)),
        dma((2,)),
        dma((2,)),
        dma((2, 2, 2)),
        dma((2, 2, 2)),
        dma((2, 2, 2)),
        dma((2, 2, 2)),
        dma((2,)),
        dma((2,)),
        dma((3,)),
        dma((3,)),
        dma((3,)),
        dma((3,)),
        [[dma((size(d),)) for d in st] for st in ar_dims],
        [[dma((size(d),)) for d in st] for st in ar_dims],
        pltpu.SemaphoreType.REGULAR((2,)),
    ]
    whole = pl.BlockSpec(memory_space=pltpu.VMEM)
    results = pl.pallas_call(
        functools.partial(kernel, n_dom, ar_dims),
        out_shape=(
            jax.ShapeDtypeStruct((S, C, N), f32),
            jax.ShapeDtypeStruct((3 * C, 3 * C), f32),
            jax.ShapeDtypeStruct((3 * C, 3 * C), f32),
        ),
        in_specs=[pl.BlockSpec(memory_space=pl.ANY)] * 10,
        out_specs=(pl.BlockSpec(memory_space=pl.ANY), whole, whole),
        scratch_shapes=scratch,
        compiler_params=pltpu.CompilerParams(
            collective_id=0, has_side_effects=True, vmem_limit_bytes=56 * 1024 * 1024
        ),
    )(
        x, p, f_own, f_other, mass, cols,
        degree.reshape(1, N), send.reshape(1, H), pair.reshape(1, H), partner.reshape(1, N),
    )
    any_space = pl.BlockSpec(memory_space=pl.ANY)
    return pl.pallas_call(
        move_results,
        out_shape=tuple(jax.ShapeDtypeStruct(r.shape, r.dtype) for r in results),
        in_specs=[any_space] * 3,
        out_specs=(any_space,) * 3,
        scratch_shapes=[dma((3,))],
    )(*results)


def solution(mesh):
    n_dom = mesh.shape["dom"]
    if n_dom == 512:
        near = [[(1, 8)], [(128, 4)], [(8, 4)], [(32, 4)]]
        quick = [[(128, 4), (1, 8)], [(8, 16)]]
    else:
        near = [[(1, 2)], [(2, n_dom // 2)]]
        quick = [[(1, 2)], [(2, n_dom // 2)]]
    row = P(None, "dom")
    return jax.shard_map(
        functools.partial(shards, n_dom, (near, quick, quick)),
        mesh=mesh,
        in_specs=(
            P(None, None, "dom"),
            P(None, None, "dom"),
            P(None, None, None, "dom"),
            P(None, None, None, "dom"),
            row, row, P("dom"), P("dom"), P("dom"), P("dom"),
        ),
        out_specs=(P(None, None, "dom"), P(), P()),
        check_vma=False,
    )
```

```python
import functools

import jax
import jax.numpy as jnp
from jax import lax
from jax.experimental import pallas as pl
from jax.experimental.pallas import tpu as pltpu
from jax.sharding import PartitionSpec as P

MESH = pl.DeviceIdType.MESH
f32 = jnp.float32
bf16 = jnp.bfloat16
S = 16
C = 16
K = 4
N = 128
H = 32
T = 2
LAST = 6


def iota(shape, dim):
    return lax.broadcasted_iota(jnp.int32, shape, dim)


def one_hot(mask):
    return jnp.where(mask, 1.0, 0.0).astype(f32)


def split(value):
    terms = []
    for t in range(T):
        term = value.astype(bf16)
        terms.append(term)
        if t + 1 < T:
            value = value - term.astype(f32)
    return terms


def dot_nn(a, b):
    return jnp.dot(a, b, preferred_element_type=f32)


def dot_nt(a, b):
    return lax.dot_general(a, b, (((1,), (1,)), ((), ())), preferred_element_type=f32)


def dot_tn(a, b):
    return lax.dot_general(a, b, (((0,), (0,)), ((), ())), preferred_element_type=f32)


class Groups:
    def __init__(self, me, dims):
        self.me, self.dims = me, dims
        self.size = 1
        for _, g in dims:
            self.size *= g
        self.pos = 0
        self.base = me
        for s, g in dims:
            p = lax.rem(lax.div(me, s), g)
            self.pos = self.pos * g + p
            self.base = self.base - p * s

    def device(self, pos):
        d = self.base
        for s, g in reversed(self.dims):
            d = d + lax.rem(pos, g) * s
            pos = lax.div(pos, g)
        return d

    def peer(self, t):
        return lax.rem(self.pos + t, self.size)


def kernel(
    n_dom, ar_dims,
    x_in, p_in, own_in, oth_in, mass_in, cols_in, deg_in, send_in, pair_in, part_in,
    out_ref, ga_ref, gb_ref,
    x_ref, p_ref, own_ref, oth_ref, mass_ref, cols_ref, deg_ref, send_ref, pair_ref, part_ref, in_sems,
    B, D, hd, hdc, diag, v, y, e, acc, vv, w_ref, qb, gram1, gram2,
    vcat, wcat, rr, Gl, GS, GHs, Pn, Pr, Ql, Qh, raw, PK, GH2, REP, BP, hdcT, TG, SEL, repv, wcat2, zcat,
    sndh, rcvh, sndc, rcvc, sndd, rcvd, sndk, rcvk, rcvq, sndm, rcvm, ar_bufs,
    hs, hr, cs, cr, ds, dr, ks, kr, qs, qr, ms, mr, bs, br, ts, tr, ar_ss, ar_rs, vouched,
):
    me = lax.axis_index("dom")
    lower = lax.rem(me + n_dom - 1, n_dom)
    upper = lax.rem(me + 1, n_dom)
    lower2 = lax.rem(me + n_dom - 2, n_dom)
    upper2 = lax.rem(me + 2, n_dom)
    groups = [[Groups(me, dims) for dims in stages] for stages in ar_dims]
    bar_groups = groups[1]

    barrier = pltpu.get_barrier_semaphore()
    for d in (lower, upper, lower2, upper2):
        pl.semaphore_signal(barrier, inc=1, device_id=(d,), device_id_type=MESH)
    wide, ring = bar_groups
    reach = 4
    n_bar = 4 + wide.size - 1 + 2 * reach

    def greet(g, t):
        pl.semaphore_signal(barrier, inc=1, device_id=(g.device(g.peer(t)),), device_id_type=MESH)

    def greet_wide(t, _):
        greet(wide, t)
        return 0

    for t in range(reach, 0, -1):
        greet(ring, t)
        greet(ring, ring.size - t)
    lax.fori_loop(1, wide.size, greet_wide, 0)

    def vouch():
        for j, t in enumerate((reach, ring.size - reach)):
            pl.semaphore_signal(
                vouched.at[j], inc=1, device_id=(ring.device(ring.peer(t)),), device_id_type=MESH
            )

    def fetch(j):
        src = (x_in, p_in, own_in, oth_in, mass_in, cols_in, deg_in, send_in, pair_in, part_in)[j]
        dst = (x_ref, p_ref, own_ref, oth_ref, mass_ref, cols_ref, deg_ref, send_ref, pair_ref, part_ref)[j]
        return pltpu.make_async_copy(src, dst, in_sems.at[j])

    for j in (5, 9, 7, 8, 6, 3, 2, 0, 1, 4):
        fetch(j).start()

    def pair_copies(snd, rcv, ss, rs, idx, far_idx=None):
        out = []
        devices = (lower, upper) if far_idx is None else (lower2, upper2)
        src_idx = idx
        if far_idx is not None:
            idx = far_idx
        for side, (src, dst, dev) in enumerate(((0, 16, devices[0]), (16, 0, devices[1]))):
            out.append(
                pltpu.make_async_remote_copy(
                    snd.at[src_idx + (pl.ds(src, 16),)],
                    rcv.at[idx + (pl.ds(dst, 16),)],
                    ss.at[idx + (side,)],
                    rs.at[idx + (side,)],
                    device_id=(dev,),
                    device_id_type=MESH,
                )
            )
        return out

    def start(*args):
        for c in pair_copies(*args):
            c.start()

    def wait_recv(*args):
        for c in pair_copies(*args):
            c.wait_recv()

    def wait_send(*args):
        for c in pair_copies(*args):
            c.wait_send()

    def both_copies(ref, ss, rs):
        return [
            pltpu.make_async_remote_copy(
                ref.at[0], ref.at[at], ss.at[at], rs.at[at], device_id=(dev,), device_id_type=MESH
            )
            for at, dev in ((1, upper), (2, lower))
        ]

    def ar_copy(slot, stage, t, receive):
        g = groups[slot][stage]
        peer = g.peer(t)
        buf = ar_bufs[slot][stage]
        at = peer if receive else g.pos
        return pltpu.make_async_remote_copy(
            buf.at[g.pos],
            buf.at[at],
            ar_ss[slot][stage].at[peer],
            ar_rs[slot][stage].at[at],
            device_id=(g.device(peer),),
            device_id_type=MESH,
        )

    def ar_start(slot, stage, value):
        g = groups[slot][stage]
        ar_bufs[slot][stage][g.pos] = value

        if slot == 2:
            for t in range(1, g.size):
                ar_copy(slot, stage, t, False).start()
            return

        def go(t, _):
            ar_copy(slot, stage, t, False).start()
            return 0

        lax.fori_loop(1, g.size, go, 0)

    def ar_finish(slot, stage):
        g = groups[slot][stage]

        def go(t, _):
            ar_copy(slot, stage, t, True).wait_recv()
            return 0

        if slot == 2:
            for t in range(1, g.size):
                go(t, 0)
        else:
            lax.fori_loop(1, g.size, go, 0)
        buf = ar_bufs[slot][stage]
        total = buf[0]
        for j in range(1, g.size):
            total = total + buf[j]
        return total

    def ar_drain(slot, stage):
        g = groups[slot][stage]

        def go(t, _):
            ar_copy(slot, stage, t, False).wait_send()
            return 0

        lax.fori_loop(1, g.size, go, 0)

    for j in (5, 9, 7, 8, 6):
        fetch(j).wait()
    for k in range(K):
        at_k = pl.ds(k * N, N)
        hot = one_hot(iota((N, N), 0) == cols_ref[k : k + 1, :]).astype(bf16)
        halo = one_hot(iota((H, N), 0) + N == cols_ref[k : k + 1, :]).astype(bf16)
        for t in range(T):
            Gl[pl.ds(t * N, N), at_k] = hot
            GS[0:N, pl.ds((k * T + t) * N, N)] = hot
            GS[N : N + H, pl.ds((k * T + t) * N, N)] = halo
            GHs[pl.ds(t * H, H), at_k] = halo
            GH2[pl.ds(t * 2 * H, H), at_k] = halo
    def column(ref):
        square = jnp.where(iota((H, H), 0) == iota((H, H), 1), ref[...].astype(f32), 0.0)
        return jnp.sum(square, axis=1, keepdims=True)

    lanes = iota((H, N), 1).astype(f32)
    sel = one_hot(lanes == column(send_ref)).astype(bf16)
    for t in range(T):
        Pn[0, :, pl.ds(t * N, N)] = sel

    def bcast_rows(ref, idx, r):
        return ref[idx + (slice(r, r + 1), slice(None))]

    def store_split_w(k, b, value):
        for t, term in enumerate(split(value)):
            wcat[pl.ds(b * C, C), pl.ds((k * T + t) * N, N)] = term

    def store_split_v(ref):
        for b in range(S):
            for t, term in enumerate(split(ref[b])):
                vcat[pl.ds(b * C, C), pl.ds(t * N, N)] = term

    def scatter_slot(k, total):
        at_k = slice(k * T * N, (k + 1) * T * N)
        part = dot_nt(GS[:, at_k], wcat[:, at_k])
        return part if total is None else total + part

    def turned_rows(rows):
        return jnp.concatenate([rows[0:N, 0:N].T, rows[0:N, N : 2 * N].T], axis=0).reshape(S, C, N)

    def from_halo(rows, matrix):
        return dot_tn(jnp.concatenate(split(rows), axis=0), matrix[...])

    def reverse(ref):
        rows = None
        for k in range(K):
            for half in range(2):
                total = [jnp.zeros((C, N), f32)] * 8
                for a in range(S):
                    value = ref[a]
                    for j in range(8):
                        total[j] = total[j] + bcast_rows(B, (k, a), half * 8 + j) * value
                for j in range(8):
                    store_split_w(k, half * 8 + j, total[j])
            rows = scatter_slot(k, rows)
        return rows

    def far(near, rows, half_way=None, table=None):
        rows = jnp.concatenate(split(rows), axis=0).T
        table = GHs if table is None else table
        total = [jnp.zeros((C, N), f32)] * S
        for k in range(K):
            if k % 2 == 0:
                got = dot_nn(rows, table[:, k * N : (k + 2) * N])
            if k == 3 and half_way is not None:
                half_way()
            part = got[:, (k % 2) * N : (k % 2 + 1) * N].reshape(S, C, N)
            near[k] = near[k] + part
            for b in range(S):
                value = near[k, b]
                for a in range(S):
                    total[a] = total[a] + bcast_rows(B, (k, a), b) * value
        return total

    def own(ref, D):
        total = [jnp.zeros((C, N), f32)] * S
        for b in range(S):
            value = ref[b]
            for a in range(S):
                total[a] = total[a] + bcast_rows(D, (a,), b) * value
        return total

    def gather_local(dst):
        rows = dot_nn(vcat[...], Gl[...])
        for k in range(K):
            dst[k] = rows[:, k * N : (k + 1) * N].reshape(S, C, N)

    def send_rows(i, ch, which):
        sndh[i, ch] = dot_nt(Pn[which], vcat[...])
        start(sndh, rcvh, hs, hr, (i, ch))

    def a_rest(i, ch):
        src = v.at[ch]
        rows = reverse(src)
        sndc[i, ch] = rows[N : N + H]
        start(sndc, rcvc, cs, cr, (i, ch))
        a_local(ch, rows)

    def a_local(ch, rows):
        src = v.at[ch]
        gather_local(vv.at[ch])
        back = turned_rows(rows)
        total = own(src, D)
        for a in range(S):
            acc[ch, a] = total[a] - back[a]

    def a_finish(i, ch):
        wait_recv(sndh, rcvh, hs, hr, (i, ch))
        total = far(
            vv.at[ch], rcvh[i, ch], lambda: wait_recv(sndc, rcvc, cs, cr, (i, ch))
        )
        got = from_halo(rcvc[i, ch], Pr).reshape(S, C, N)
        return [y[ch, a] - acc[ch, a] + got[a] + total[a] for a in range(S)]

    def split_pair(b, value):
        for t, term in enumerate(split(value)):
            vcat[pl.ds(b * C, C), pl.ds(t * N, N)] = term

    def k_finish(i, ch):
        m = i - 3
        wait_recv(sndh, rcvh, hs, hr, (i, ch))
        wait_recv(sndh, rcvq, qs, qr, (i, ch), (m, ch))
        mine, near, beyond = sndh[i, ch], rcvh[i, ch], rcvq[m, ch]
        own_c = near * hdcT[0]
        lower_c = jnp.concatenate([beyond[0:16], mine[0:16]], axis=0) * hdcT[1]
        upper_c = jnp.concatenate([mine[16:32], beyond[16:32]], axis=0) * hdcT[2]
        terms = split(jnp.concatenate([own_c, lower_c, upper_c], axis=0))
        rep = dot_nn(jnp.concatenate(terms, axis=0).T, REP[...])
        for j in range(3):
            repv[j] = rep[:, j * N : (j + 1) * N].reshape(S, C, N)
        for j in range(3):
            for half in range(2):
                total = [jnp.zeros((C, N), f32)] * 8
                for a in range(S):
                    value = repv[j, a]
                    for b in range(8):
                        total[b] = total[b] + bcast_rows(BP, (j, a), half * 8 + b) * value
                for b in range(8):
                    for t, term in enumerate(split(total[b])):
                        wcat2[pl.ds((half * 8 + b) * C, C), pl.ds((j * T + t) * N, N)] = term
        back = turned_rows(dot_nt(TG[...], wcat2[...]))
        w_ref[...] = from_halo(own_c, Qh).reshape(S, C, N)
        e[ch] = e[ch] + w_ref[...]
        mid = own(w_ref, D)
        for a in range(S):
            acc[ch, a] = acc[ch, a] + mid[a] - back[a]
        wait_recv(sndk, rcvk, ks, kr, (m, ch))
        others = jnp.concatenate([term[H : 3 * H] for term in terms], axis=0)
        rows = rcvk[m, ch] + dot_nn(SEL[...], others)
        total = far(
            vv.at[ch],
            jnp.concatenate([rows, own_c], axis=0),
            lambda: wait_recv(sndc, rcvc, cs, cr, (i, ch)),
            GH2,
        )
        got = from_halo(rcvc[i, ch], Pr).reshape(S, C, N)
        return [y[ch, a] - acc[ch, a] + got[a] + total[a] for a in range(S)]

    def advance(i, ch, coarse_start, values, first):
        which = coarse_start.astype(jnp.int32)
        scale = jnp.where(coarse_start, 1.0, hd[...])
        keep = jnp.where(coarse_start, 0.0, 1.0)
        for b, value in enumerate(values):
            if first is not None:
                raw[b] = value
                value = jnp.where(first, x_ref[b], value)
            y[ch, b] = value
            value = value * scale[b : b + 1, :]
            v[ch, b] = value
            e[ch, b] = e[ch, b] + keep * value
            split_pair(b, value)
        send_rows(i, ch, which)

    def coarse_rest(i, ch):
        m = i - 3
        start(sndh, rcvq, qs, qr, (i, ch), (m, ch))
        pairs = dot_nn(vcat[...], Ql[...]).reshape(S, C, N)
        for b in range(S):
            value = (y[ch, b] + pairs[b]) * hdc[b : b + 1, :]
            v[ch, b] = value
            e[ch, b] = e[ch, b] + value
            split_pair(b, value)
        sndk[m, ch] = dot_nt(Pn[0], vcat[...])
        start(sndk, rcvk, ks, kr, (m, ch))

    def rr_store(row, ref, sign=1.0):
        for b in range(S):
            for t, term in enumerate(split(sign * ref[b])):
                rr[pl.ds(t * 128 + row, C), pl.ds(b * N, N)] = term

    def later_tables():
        hot = one_hot(iota((N, N), 0) == part_ref[...]).astype(bf16)
        halo = one_hot(iota((H, N), 0) + N == part_ref[...]).astype(bf16)
        for t in range(T):
            Ql[pl.ds(t * N, N), :] = hot
            Qh[pl.ds(t * H, H), :] = halo
        psel = one_hot(lanes == column(pair_ref)).astype(bf16)
        for t in range(T):
            Pn[1, :, pl.ds(t * N, N)] = psel
            for k in range(K):
                PK[:, pl.ds((k * T + t) * N, N)] = jnp.zeros((N, N), bf16)
                PK[pl.ds(k * H, H), pl.ds((k * T + t) * N, N)] = psel
                near_pair = dot_nn(psel, GS[0:N, (k * T) * N : (k * T + 1) * N]).astype(bf16)
                GH2[pl.ds(t * 2 * H + H, H), pl.ds(k * N, N)] = near_pair
            Pr[pl.ds(t * H, H), :] = sel
        for k in range(K):
            for t, term in enumerate(split(B[k].reshape(S * S, N))):
                wcat[:, pl.ds((k * T + t) * N, N)] = term
        BP[0] = dot_nt(wcat[...], PK[...]).reshape(S, S, N)
        targets = dot_nt(GS[...], PK[...]) * 0.5
        for t in range(T):
            TG[:, pl.ds(t * N, N)] = targets[0:N].astype(bf16)
        sndm[...] = jnp.zeros_like(sndm)
        sndm[:, 0:N] = targets[N : N + H]
        sndm[:, N : 2 * N] = dot_nt(sel, jnp.concatenate([psel, jnp.zeros((N - H, N), bf16)], axis=0))
        for t in range(T):
            for j in range(3):
                row = iota((H, 3 * N), 0)
                col = iota((H, 3 * N), 1)
                hit = (lax.div(col, N) == j) & (lax.rem(col, H) == row)
                REP[pl.ds((t * 3 + j) * H, H), :] = one_hot(hit).astype(bf16)

    live = [jnp.where(deg_ref[...] > k, 1.0, 0.0).astype(f32) for k in range(K)]

    def outer(left, right, k):
        def body(s, total):
            value = right[k, s]
            return tuple(total[a] + left[k, s, a : a + 1, :] * value for a in range(S))

        return lax.fori_loop(0, S, body, tuple(jnp.zeros((S, N), f32) for _ in range(S)), unroll=4)

    fetch(3).wait()
    rows = None
    for k in range(K):
        for a, value in enumerate(outer(oth_ref, oth_ref, k)):
            store_split_w(k, a, value * live[k])
        rows = scatter_slot(k, rows)
    sndc[LAST, 0] = rows[N : N + H]
    D[...] = turned_rows(rows)
    fetch(2).wait()
    for k in range(K):
        for a, value in enumerate(outer(own_ref, oth_ref, k)):
            B[k, a] = value * live[k]
    fetch(0).wait()
    v[1] = x_ref[...]
    store_split_v(x_ref)
    sndh[0, 1] = dot_nt(Pn[0], vcat[...])
    rows = reverse(v.at[1])
    sndc[0, 1] = rows[N : N + H]
    pl.semaphore_wait(barrier, n_bar)
    vouch()
    start(sndh, rcvh, hs, hr, (0, 1))
    start(sndc, rcvc, cs, cr, (LAST, 0))
    start(sndc, rcvc, cs, cr, (0, 1))
    for k in range(K):
        for a, value in enumerate(outer(own_ref, own_ref, k)):
            D[a] = D[a] + value * live[k]
    fetch(4).wait()
    for b in range(S):
        D[b, b : b + 1, :] = D[b, b : b + 1, :] + mass_ref[b : b + 1, :]
    a_local(1, rows)
    fetch(1).wait()
    v[0] = p_ref[...]
    store_split_v(p_ref)
    send_rows(0, 0, 0)
    a_rest(0, 0)
    e[...] = jnp.zeros_like(e)
    y[...] = jnp.zeros_like(y)
    rr[...] = jnp.zeros_like(rr)
    rr_store(0, x_ref)
    rr_store(16, p_ref)
    later_tables()
    start(sndm, rcvm, ms, mr, ())
    for c in both_copies(BP, bs, br):
        c.start()

    wait_recv(sndc, rcvc, cs, cr, (LAST, 0))
    w_ref[...] = from_halo(rcvc[LAST, 0], Pr).reshape(S, S, N)
    for ch in (1, 0):
        total = own(v.at[ch], w_ref)
        for a in range(S):
            acc[ch, a] = acc[ch, a] + total[a]
    D[...] = D[...] + w_ref[...]
    for b in range(S):
        diag[b : b + 1, :] = D[b, b : b + 1, :]
    hd[...] = 0.5 / diag[...]
    dcat = jnp.concatenate(split(diag[...]), axis=1)
    sndd[...] = jnp.zeros_like(sndd)
    sndd[:, 0:S] = dot_nt(Pn[1], dcat)
    start(sndd, rcvd, ds, dr, ())

    def event(g, _):
        i = 1 + lax.div(g, 2)
        ch = 1 - lax.rem(g, 2)
        coarse_end = (i == 4) | (i == 5)
        coarse_start = (i == 3) | (i == 4)

        @pl.when(jnp.logical_not(coarse_end))
        def _():
            advance(i, ch, coarse_start, a_finish(i - 1, ch), (i == 1) & (ch == 0))

        @pl.when(coarse_end)
        def _():
            advance(i, ch, coarse_start, k_finish(i - 1, ch), None)

        @pl.when(coarse_start)
        def _():
            coarse_rest(i, ch)

        a_rest(i, ch)

        @pl.when((i == 1) & (ch == 1))
        def _():
            rr_store(32, raw, -1.0)

        @pl.when((i == 1) & (ch == 0))
        def _():
            rr_store(48, raw, -1.0)

        late = ch == 0

        @pl.when(late & (i == 1))
        def _():
            left = jnp.concatenate([rr[0:32, :], rr[128:160, :]], axis=0)
            parts = dot_nt(left, rr[...])
            parts = parts[:, 0:128] + parts[:, 128:256]
            parts = (parts[0:32] + parts[32:64]) * (1.0 / (N * S * n_dom))
            rolled = pltpu.roll(parts[16:32], 64, 1)
            ar_start(0, 0, jnp.where(iota((C, 128), 1) < 64, parts[0:16], rolled))
            for j in range(2):
                pl.semaphore_wait(vouched.at[j], 1)

        @pl.when(late & (i == 2))
        def _():
            wait_recv(sndd, rcvd, ds, dr, ())
            dcat = jnp.concatenate(split(diag[...]), axis=1)
            far_diag = from_halo(rcvd[...], Qh)[0:S]
            hdc[...] = 0.5 / (diag[...] + dot_nn(dcat, Ql[...]) + far_diag)
            for b in range(S):
                split_pair(b, jnp.broadcast_to(hdc[b : b + 1, :], (C, N)))
            hdcT[0] = dot_nt(Pn[1], vcat[...])
            for c in both_copies(hdcT, ts, tr):
                c.start()

        @pl.when(late & (i == 3))
        def _():
            wait_recv(sndm, rcvm, ms, mr, ())
            for c in both_copies(BP, bs, br):
                c.wait_recv()
            row = iota((H, N), 0)
            for j, keep in ((1, row < 16), (2, row >= 16)):
                there = jnp.where(keep, rcvm[:, 0:N], 0.0).astype(bf16)
                target = dot_tn(Pr[0:H, :], there).astype(bf16)
                for t in range(T):
                    TG[:, pl.ds((j * T + t) * N, N)] = target
            same = rcvm[:, N : 2 * N]
            half = jnp.where(row < 16, same, pltpu.roll(same, H, 1))
            SEL[...] = (half + pltpu.roll(half, 2 * H, 1)).astype(bf16)
            for c in both_copies(hdcT, ts, tr):
                c.wait_recv()

        stages = len(groups[0])
        for s in range(stages):

            @pl.when(late & (i == 2 + s))
            def _(s=s):
                total = ar_finish(0, s)
                if s + 1 < stages:
                    ar_start(0, s + 1, total)
                else:
                    gram1[...] = total
                    lane = iota((C, 128), 1)
                    work = jnp.where(lane < 16, total, jnp.where(lane < 32, pltpu.roll(total, 112, 1), 0.0))
                    for j in range(C):
                        col = jnp.sum(jnp.where(lane == j, work, 0.0), axis=1, keepdims=True)
                        row = work[j : j + 1, :] / col[j : j + 1, :]
                        unit = jnp.where(iota((C, 1), 0) == j, 1.0, 0.0)
                        work = work - (col - unit) * row
                    square = jnp.concatenate([work, jnp.zeros((128 - C, 128), f32)], axis=0).T
                    quot_t = square[16:32, :]
                    for j in range(C):
                        col = jnp.sum(jnp.where(lane == j, quot_t, 0.0), axis=1, keepdims=True)
                        qb[j] = jnp.broadcast_to(col, (C, 128))

        return 0

    lax.fori_loop(0, 2 * (LAST - 1), event, 0)

    def last_event(g, _):
        ch = 1 - g
        for b, value in enumerate(a_finish(LAST - 1, ch)):
            e[ch, b] = e[ch, b] + value * hd[b : b + 1, :]
        return 0

    lax.fori_loop(0, 2, last_event, 0)

    def combine(b, _):
        total = -e[1, b]
        for j in range(C):
            total = total - qb[j] * e[0, b, j : j + 1, :]
        w_ref[b] = total
        return 0

    lax.fori_loop(0, S, combine, 0)

    result = pltpu.make_async_copy(w_ref, out_ref, in_sems.at[10])
    result.start()
    store_split_v(w_ref)
    sndh[LAST, 0] = dot_nt(Pn[0], vcat[...])
    start(sndh, rcvh, hs, hr, (LAST, 0))
    rr_store(64, w_ref)
    lane = iota((C, 128), 1)
    scale = 1.0 / (N * S * n_dom)
    left = jnp.concatenate([rr[64:80, :], rr[192:208, :]], axis=0)
    parts = dot_nt(left, rr[...])
    parts = (parts[0:16, 0:128] + parts[0:16, 128:256] + parts[16:32, 0:128] + parts[16:32, 128:256]) * scale
    low = jnp.where(lane < 64, parts, 0.0)
    ar_start(1, 0, low[0:8] + pltpu.roll(low[8:16], 64, 1))

    diagonal = lax.div(lane, 16) == lax.rem(iota((C, 128), 0), 8)

    def pack_block(block):
        for shift in (16, 32, 64):
            block = block + pltpu.roll(block, shift, 1)
        block = jnp.where(diagonal, block, 0.0)
        top = jnp.sum(block[0:8], axis=0, keepdims=True)
        return jnp.concatenate([top, jnp.sum(block[8:16], axis=0, keepdims=True)], axis=0)

    def unpack_block(pair):
        wide = jnp.concatenate(
            [jnp.broadcast_to(pair[0:1], (8, 128)), jnp.broadcast_to(pair[1:2], (8, 128))], axis=0
        )
        wide = jnp.where(diagonal, wide, 0.0)
        for shift in (16, 32, 64):
            wide = wide + pltpu.roll(wide, shift, 1)
        return wide

    def lanes_from(value, source):
        return jnp.where(lane < 16, pltpu.roll(value, 128 - source, 1), 0.0)

    gram2[0:2, :] = pack_block(lanes_from(parts, 64))
    rows = reverse(w_ref)
    turned = jnp.concatenate([term[0 : 2 * H] for term in split(jnp.concatenate([rows[N : N + H], rows[N : N + H]], axis=0))], axis=0).T
    zcat[...] = turned
    gather_local(vv.at[0])
    back = turned_rows(rows)
    near = vv.at[0]
    mid = own(w_ref, D)
    for a in range(S):
        acc[0, a] = mid[a] - back[a]
    mid = far(near, jnp.zeros((H, S * C), f32))
    for a in range(S):
        v[0, a] = acc[0, a] - mid[a]
    rr_store(80, v.at[0])
    parts = dot_nt(left, rr[...])
    parts = parts[0:16, 0:128] + parts[0:16, 128:256] + parts[16:32, 0:128] + parts[16:32, 128:256]
    gram2[2:4, :] = pack_block(lanes_from(parts, 80) * scale)
    wait_recv(sndh, rcvh, hs, hr, (LAST, 0))
    terms = split(rcvh[LAST, 0])
    edges = dot_nn(zcat[...], jnp.concatenate([terms[0], terms[1], terms[0], terms[1]], axis=0))
    same = lax.div(iota((S * C, S * C), 0), C) == lax.div(iota((S * C, S * C), 1), C)
    edges = jnp.sum(jnp.where(same, edges, 0.0).reshape(S, C, S * C), axis=0)
    edges = edges[:, 0:128] + edges[:, 128:256]
    ar_start(2, 0, jnp.concatenate([gram2[2:4, :] - pack_block(edges * (2.0 * scale)), gram2[0:2, :]], axis=0))

    def drain(g, _):
        i, ch = lax.div(g, 2), lax.rem(g, 2)
        wait_send(sndh, rcvh, hs, hr, (i, ch))
        wait_send(sndc, rcvc, cs, cr, (i, ch))
        return 0

    def drain_coarse(g, _):
        m, ch = lax.div(g, 2), lax.rem(g, 2)
        wait_send(sndk, rcvk, ks, kr, (m, ch))
        wait_send(sndh, rcvq, qs, qr, (m + 3, ch), (m, ch))
        return 0

    ar_start(1, 1, ar_finish(1, 0))
    lax.fori_loop(0, 2 * LAST, drain, 0)
    wait_send(sndh, rcvh, hs, hr, (LAST, 0))
    wait_send(sndc, rcvc, cs, cr, (LAST, 0))
    wait_send(sndd, rcvd, ds, dr, ())
    lax.fori_loop(0, 4, drain_coarse, 0)
    wait_send(sndm, rcvm, ms, mr, ())
    for c in both_copies(BP, bs, br) + both_copies(hdcT, ts, tr):
        c.wait_send()
    ar_start(2, 1, ar_finish(2, 0))
    for s in range(len(groups[0])):
        ar_drain(0, s)
    ar_drain(1, 0)
    ar_drain(2, 0)
    half = ar_finish(1, 1)
    high = pltpu.roll(half, 64, 1)
    g2 = jnp.where(lane < 64, jnp.concatenate([half, high], axis=0), 0.0)

    def place(value, source, target):
        shift = (target - source) % 128
        moved = pltpu.roll(value, shift, 1) if shift else value
        return jnp.where((lane >= target) & (lane < target + 16), moved, 0.0)

    g1 = gram1[...]
    turned = jnp.concatenate([g2, jnp.zeros((128 - C, 128), f32)], axis=0).T
    xw, pw, xaw, paw = [turned[16 * j : 16 * j + 16, :] for j in range(4)]
    gb_ref[0:16, :] = (place(g1, 0, 0) + place(xw, 0, 16) + place(g1, 16, 32))[:, 0:48]
    gb_ref[32:48, :] = (place(g1, 64, 0) + place(pw, 0, 16) + place(g1, 80, 32))[:, 0:48]
    ga_ref[0:16, :] = (place(g1, 32, 0) + place(xaw, 0, 16) + place(g1, 48, 32))[:, 0:48]
    ga_ref[32:48, :] = (place(g1, 96, 0) + place(paw, 0, 16) + place(g1, 112, 32))[:, 0:48]
    wide_a = place(g2, 32, 0) + place(g2, 48, 32)
    wide_b = place(g2, 0, 0) + place(g2, 16, 32)
    ar_drain(1, 1)
    last = ar_finish(2, 1)
    image = unpack_block(last[0:2])
    square = jnp.concatenate([jnp.where(lane < 16, image, 0.0), jnp.zeros((128 - C, 128), f32)], axis=0).T
    image = 0.5 * (jnp.where(lane < 16, image, 0.0) + square[0:16, :])
    ga_ref[16:32, :] = (wide_a + place(image, 0, 16))[:, 0:48]
    gb_ref[16:32, :] = (wide_b + place(unpack_block(last[2:4]), 16, 16))[:, 0:48]
    ar_drain(2, 1)
    result.wait()


def move_results(a_in, b_in, c_in, a_out, b_out, c_out, a_mid, b_mid, c_mid, sems):
    sets = ((a_in, a_mid, a_out), (b_in, b_mid, b_out), (c_in, c_mid, c_out))
    first = [pltpu.make_async_copy(src, mid, sems.at[j]) for j, (src, mid, _) in enumerate(sets)]
    second = [pltpu.make_async_copy(mid, dst, sems.at[3 + j]) for j, (_, mid, dst) in enumerate(sets)]
    for c in first:
        c.start()
    for before, after in zip(first, second):
        before.wait()
        after.start()
    for c in second:
        c.wait()


def shards(n_dom, ar_dims, x, p, f_own, f_other, mass, cols, degree, send, pair, partner):
    vm = pltpu.VMEM
    dma = pltpu.SemaphoreType.DMA

    def size(dims):
        total = 1
        for _, g in dims:
            total *= g
        return total

    rows = (16, 8, 4)
    i32 = jnp.int32
    scratch = [
        vm((S, C, N), f32),
        vm((S, C, N), f32),
        vm((K, S, S, N), f32),
        vm((K, S, S, N), f32),
        vm((S, N), f32),
        vm((K, N), i32),
        vm((1, N), i32),
        vm((1, H), i32),
        vm((1, H), i32),
        vm((1, N), i32),
        dma((11,)),
        vm((K, S, S, N), f32),
        vm((S, S, N), f32),
        vm((S, N), f32),
        vm((S, N), f32),
        vm((S, N), f32),
        vm((2, S, C, N), f32),
        vm((2, S, C, N), f32),
        vm((2, S, C, N), f32),
        vm((2, S, C, N), f32),
        vm((2, K, S, C, N), f32),
        vm((S, C, N), f32),
        vm((C, C, 128), f32),
        vm((C, 128), f32),
        vm((C, 128), f32),
        vm((S * C, T * N), bf16),
        vm((S * C, T * K * N), bf16),
        vm((256, S * N), bf16),
        vm((T * N, K * N), bf16),
        vm((N + H, T * K * N), bf16),
        vm((T * H, K * N), bf16),
        vm((2, H, T * N), bf16),
        vm((T * H, N), bf16),
        vm((T * N, N), bf16),
        vm((T * H, N), bf16),
        vm((S, C, N), f32),
        vm((N, T * K * N), bf16),
        vm((T * 2 * H, K * N), bf16),
        vm((T * 3 * H, 3 * N), bf16),
        vm((3, S, S, N), f32),
        vm((3, H, S * C), f32),
        vm((N, 3 * T * N), bf16),
        vm((H, N), bf16),
        vm((3, S, C, N), f32),
        vm((S * C, 3 * T * N), bf16),
        vm((S * C, 2 * T * H), bf16),
        vm((LAST + 1, 2, H, S * C), f32),
        vm((LAST + 1, 2, H, S * C), f32),
        vm((LAST + 1, 2, H, S * C), f32),
        vm((LAST + 1, 2, H, S * C), f32),
        vm((H, 128), f32),
        vm((H, 128), f32),
        vm((2, 2, H, S * C), f32),
        vm((2, 2, H, S * C), f32),
        vm((2, 2, H, S * C), f32),
        vm((H, 2 * N), f32),
        vm((H, 2 * N), f32),
        [[vm((size(d), rows[j], 128), f32) for d in st] for j, st in enumerate(ar_dims)],
        dma((LAST + 1, 2, 2)),
        dma((LAST + 1, 2, 2)),
        dma((LAST + 1, 2, 2)),
        dma((LAST + 1, 2, 2)),
        dma((2,)),
        dma((2,)),
        dma((2, 2, 2)),
        dma((2, 2, 2)),
        dma((2, 2, 2)),
        dma((2, 2, 2)),
        dma((2,)),
        dma((2,)),
        dma((3,)),
        dma((3,)),
        dma((3,)),
        dma((3,)),
        [[dma((size(d),)) for d in st] for st in ar_dims],
        [[dma((size(d),)) for d in st] for st in ar_dims],
        pltpu.SemaphoreType.REGULAR((2,)),
    ]
    whole = pl.BlockSpec(memory_space=pltpu.VMEM)
    results = pl.pallas_call(
        functools.partial(kernel, n_dom, ar_dims),
        out_shape=(
            jax.ShapeDtypeStruct((S, C, N), f32),
            jax.ShapeDtypeStruct((3 * C, 3 * C), f32),
            jax.ShapeDtypeStruct((3 * C, 3 * C), f32),
        ),
        in_specs=[pl.BlockSpec(memory_space=pl.ANY)] * 10,
        out_specs=(pl.BlockSpec(memory_space=pl.ANY), whole, whole),
        scratch_shapes=scratch,
        compiler_params=pltpu.CompilerParams(
            collective_id=0, has_side_effects=True, vmem_limit_bytes=56 * 1024 * 1024
        ),
    )(
        x, p, f_own, f_other, mass, cols,
        degree.reshape(1, N), send.reshape(1, H), pair.reshape(1, H), partner.reshape(1, N),
    )
    any_space = pl.BlockSpec(memory_space=pl.ANY)
    return pl.pallas_call(
        move_results,
        out_shape=tuple(jax.ShapeDtypeStruct(r.shape, r.dtype) for r in results),
        in_specs=[any_space] * 3,
        out_specs=(any_space,) * 3,
        scratch_shapes=[vm(r.shape, r.dtype) for r in results] + [dma((6,))],
    )(*results)


def solution(mesh):
    n_dom = mesh.shape["dom"]
    if n_dom == 512:
        near = [[(1, 8)], [(128, 4)], [(8, 4)], [(32, 4)]]
        quick = [[(128, 4), (1, 8)], [(8, 16)]]
    else:
        near = [[(1, 2)], [(2, n_dom // 2)]]
        quick = [[(1, 2)], [(2, n_dom // 2)]]
    row = P(None, "dom")
    return jax.shard_map(
        functools.partial(shards, n_dom, (near, quick, quick)),
        mesh=mesh,
        in_specs=(
            P(None, None, "dom"),
            P(None, None, "dom"),
            P(None, None, None, "dom"),
            P(None, None, None, "dom"),
            row, row, P("dom"), P("dom"), P("dom"), P("dom"),
        ),
        out_specs=(P(None, None, "dom"), P(), P()),
        check_vma=False,
    )
```

```python
import functools

import jax
import jax.numpy as jnp
from jax import lax
from jax.experimental import pallas as pl
from jax.experimental.pallas import tpu as pltpu
from jax.sharding import PartitionSpec as P

MESH = pl.DeviceIdType.MESH
f32 = jnp.float32
bf16 = jnp.bfloat16
S = 16
C = 16
K = 4
N = 128
H = 32
T = 2
LAST = 6


def iota(shape, dim):
    return lax.broadcasted_iota(jnp.int32, shape, dim)


def one_hot(mask):
    return jnp.where(mask, 1.0, 0.0).astype(f32)


def split(value):
    terms = []
    for t in range(T):
        term = value.astype(bf16)
        terms.append(term)
        if t + 1 < T:
            value = value - term.astype(f32)
    return terms


def dot_nn(a, b):
    return jnp.dot(a, b, preferred_element_type=f32)


def dot_nt(a, b):
    return lax.dot_general(a, b, (((1,), (1,)), ((), ())), preferred_element_type=f32)


def dot_tn(a, b):
    return lax.dot_general(a, b, (((0,), (0,)), ((), ())), preferred_element_type=f32)


class Groups:
    def __init__(self, me, dims):
        self.me, self.dims = me, dims
        self.size = 1
        for _, g in dims:
            self.size *= g
        self.pos = 0
        self.base = me
        for s, g in dims:
            p = lax.rem(lax.div(me, s), g)
            self.pos = self.pos * g + p
            self.base = self.base - p * s

    def device(self, pos):
        d = self.base
        for s, g in reversed(self.dims):
            d = d + lax.rem(pos, g) * s
            pos = lax.div(pos, g)
        return d

    def peer(self, t):
        return lax.rem(self.pos + t, self.size)


def kernel(
    n_dom, ar_dims,
    x_in, p_in, own_in, oth_in, mass_in, cols_in, deg_in, send_in, pair_in, part_in,
    out_ref, ga_ref, gb_ref,
    x_ref, p_ref, own_ref, oth_ref, mass_ref, cols_ref, deg_ref, send_ref, pair_ref, part_ref, in_sems,
    B, D, hd, hdc, diag, v, y, e, acc, vv, w_ref, qb, gram1, gram2,
    vcat, wcat, rr, Gl, GS, GHs, Pn, Pr, Ql, Qh, raw, PK, GH2, REP, BP, hdcT, TG, SEL, repv, wcat2, zcat, back_rows,
    sndh, rcvh, sndc, rcvc, sndd, rcvd, sndk, rcvk, rcvq, sndm, rcvm, ar_bufs,
    hs, hr, cs, cr, ds, dr, ks, kr, qs, qr, ms, mr, bs, br, ts, tr, ar_ss, ar_rs, vouched,
):
    me = lax.axis_index("dom")
    lower = lax.rem(me + n_dom - 1, n_dom)
    upper = lax.rem(me + 1, n_dom)
    lower2 = lax.rem(me + n_dom - 2, n_dom)
    upper2 = lax.rem(me + 2, n_dom)
    groups = [[Groups(me, dims) for dims in stages] for stages in ar_dims]
    bar_groups = groups[1]

    barrier = pltpu.get_barrier_semaphore()
    for d in (lower, upper, lower2, upper2):
        pl.semaphore_signal(barrier, inc=1, device_id=(d,), device_id_type=MESH)
    wide, ring = bar_groups
    reach = 4
    n_bar = 4 + wide.size - 1 + 2 * reach

    def greet(g, t):
        pl.semaphore_signal(barrier, inc=1, device_id=(g.device(g.peer(t)),), device_id_type=MESH)

    def greet_wide(t, _):
        greet(wide, t)
        return 0

    for t in range(reach, 0, -1):
        greet(ring, t)
        greet(ring, ring.size - t)
    lax.fori_loop(1, wide.size, greet_wide, 0)

    def vouch():
        for j, t in enumerate((reach, ring.size - reach)):
            pl.semaphore_signal(
                vouched.at[j], inc=1, device_id=(ring.device(ring.peer(t)),), device_id_type=MESH
            )

    def fetch(j):
        src = (x_in, p_in, own_in, oth_in, mass_in, cols_in, deg_in, send_in, pair_in, part_in)[j]
        dst = (x_ref, p_ref, own_ref, oth_ref, mass_ref, cols_ref, deg_ref, send_ref, pair_ref, part_ref)[j]
        return pltpu.make_async_copy(src, dst, in_sems.at[j])

    for j in (5, 9, 7, 8, 6, 3, 2, 0, 1, 4):
        fetch(j).start()

    def pair_copies(snd, rcv, ss, rs, idx, far_idx=None):
        out = []
        devices = (lower, upper) if far_idx is None else (lower2, upper2)
        src_idx = idx
        if far_idx is not None:
            idx = far_idx
        for side, (src, dst, dev) in enumerate(((0, 16, devices[0]), (16, 0, devices[1]))):
            out.append(
                pltpu.make_async_remote_copy(
                    snd.at[src_idx + (pl.ds(src, 16),)],
                    rcv.at[idx + (pl.ds(dst, 16),)],
                    ss.at[idx + (side,)],
                    rs.at[idx + (side,)],
                    device_id=(dev,),
                    device_id_type=MESH,
                )
            )
        return out

    def start(*args):
        for c in pair_copies(*args):
            c.start()

    def wait_recv(*args):
        for c in pair_copies(*args):
            c.wait_recv()

    def wait_send(*args):
        for c in pair_copies(*args):
            c.wait_send()

    def both_copies(ref, ss, rs):
        return [
            pltpu.make_async_remote_copy(
                ref.at[0], ref.at[at], ss.at[at], rs.at[at], device_id=(dev,), device_id_type=MESH
            )
            for at, dev in ((1, upper), (2, lower))
        ]

    def ar_copy(slot, stage, t, receive):
        g = groups[slot][stage]
        peer = g.peer(t)
        buf = ar_bufs[slot][stage]
        at = peer if receive else g.pos
        return pltpu.make_async_remote_copy(
            buf.at[g.pos],
            buf.at[at],
            ar_ss[slot][stage].at[peer],
            ar_rs[slot][stage].at[at],
            device_id=(g.device(peer),),
            device_id_type=MESH,
        )

    def ar_start(slot, stage, value):
        g = groups[slot][stage]
        ar_bufs[slot][stage][g.pos] = value

        if slot == 2:
            for t in range(1, g.size):
                ar_copy(slot, stage, t, False).start()
            return

        def go(t, _):
            ar_copy(slot, stage, t, False).start()
            return 0

        lax.fori_loop(1, g.size, go, 0)

    def ar_finish(slot, stage):
        g = groups[slot][stage]

        def go(t, _):
            ar_copy(slot, stage, t, True).wait_recv()
            return 0

        if slot == 2:
            for t in range(1, g.size):
                go(t, 0)
        else:
            lax.fori_loop(1, g.size, go, 0)
        buf = ar_bufs[slot][stage]
        total = buf[0]
        for j in range(1, g.size):
            total = total + buf[j]
        return total

    def ar_drain(slot, stage):
        g = groups[slot][stage]

        def go(t, _):
            ar_copy(slot, stage, t, False).wait_send()
            return 0

        lax.fori_loop(1, g.size, go, 0)

    for j in (5, 9, 7, 8, 6):
        fetch(j).wait()
    for k in range(K):
        at_k = pl.ds(k * N, N)
        hot = one_hot(iota((N, N), 0) == cols_ref[k : k + 1, :]).astype(bf16)
        halo = one_hot(iota((H, N), 0) + N == cols_ref[k : k + 1, :]).astype(bf16)
        for t in range(T):
            Gl[pl.ds(t * N, N), at_k] = hot
            GS[0:N, pl.ds((k * T + t) * N, N)] = hot
            GS[N : N + H, pl.ds((k * T + t) * N, N)] = halo
            GHs[pl.ds(t * H, H), at_k] = halo
            GH2[pl.ds(t * 2 * H, H), at_k] = halo
    def column(ref):
        square = jnp.where(iota((H, H), 0) == iota((H, H), 1), ref[...].astype(f32), 0.0)
        return jnp.sum(square, axis=1, keepdims=True)

    lanes = iota((H, N), 1).astype(f32)
    sel = one_hot(lanes == column(send_ref)).astype(bf16)
    for t in range(T):
        Pn[0, :, pl.ds(t * N, N)] = sel

    def bcast_rows(ref, idx, r):
        return ref[idx + (slice(r, r + 1), slice(None))]

    def store_split_w(k, b, value):
        for t, term in enumerate(split(value)):
            wcat[pl.ds(b * C, C), pl.ds((k * T + t) * N, N)] = term

    def store_split_v(ref, cur=0):
        for b in range(S):
            for t, term in enumerate(split(ref[b])):
                vcat[cur, pl.ds(b * C, C), pl.ds(t * N, N)] = term

    def scatter_slot(k, total):
        at_k = slice(k * T * N, (k + 1) * T * N)
        part = dot_nt(GS[:, at_k], wcat[:, at_k])
        return part if total is None else total + part

    def turned_rows(rows):
        return jnp.concatenate([rows[0:N, 0:N].T, rows[0:N, N : 2 * N].T], axis=0).reshape(S, C, N)

    def from_halo(rows, matrix):
        return dot_tn(jnp.concatenate(split(rows), axis=0), matrix[...])

    def reverse(ref):
        rows = None
        for k in range(K):
            for half in range(2):
                total = [jnp.zeros((C, N), f32)] * 8
                for a in range(S):
                    value = ref[a]
                    for j in range(8):
                        total[j] = total[j] + bcast_rows(B, (k, a), half * 8 + j) * value
                for j in range(8):
                    store_split_w(k, half * 8 + j, total[j])
            rows = scatter_slot(k, rows)
        return rows

    def far(near, rows, half_way=None, table=None):
        rows = jnp.concatenate(split(rows), axis=0).T
        table = GHs if table is None else table
        total = [jnp.zeros((C, N), f32)] * S
        for k in range(K):
            if k % 2 == 0:
                got = dot_nn(rows, table[:, k * N : (k + 2) * N])
            if k == 3 and half_way is not None:
                half_way()
            part = got[:, (k % 2) * N : (k % 2 + 1) * N].reshape(S, C, N)
            near[k] = near[k] + part
            for b in range(S):
                value = near[k, b]
                for a in range(S):
                    total[a] = total[a] + bcast_rows(B, (k, a), b) * value
        return total

    def own(ref, D):
        total = [jnp.zeros((C, N), f32)] * S
        for b in range(S):
            value = ref[b]
            for a in range(S):
                total[a] = total[a] + bcast_rows(D, (a,), b) * value
        return total

    def gather_local(dst, cur=0):
        rows = dot_nn(vcat[cur], Gl[...])
        for k in range(K):
            dst[k] = rows[:, k * N : (k + 1) * N].reshape(S, C, N)

    def send_rows(i, ch, which):
        cur = ch
        sndh[i, ch] = dot_nt(Pn[which], vcat[cur])
        start(sndh, rcvh, hs, hr, (i, ch))

    def a_send(i, ch):
        rows = reverse(v.at[ch])
        sndc[i, ch] = rows[N : N + H]
        start(sndc, rcvc, cs, cr, (i, ch))
        back_rows[ch] = rows[0:N]

    def a_local(ch):
        src = v.at[ch]
        rows = back_rows[ch]
        gather_local(vv.at[ch], ch)
        back = turned_rows(rows)
        total = own(src, D)
        for a in range(S):
            acc[ch, a] = total[a] - back[a]

    def a_finish(i, ch):
        wait_recv(sndh, rcvh, hs, hr, (i, ch))
        total = far(
            vv.at[ch], rcvh[i, ch], lambda: wait_recv(sndc, rcvc, cs, cr, (i, ch))
        )
        got = from_halo(rcvc[i, ch], Pr).reshape(S, C, N)
        return [y[ch, a] - acc[ch, a] + got[a] + total[a] for a in range(S)]

    def split_pair(b, value, cur):
        for t, term in enumerate(split(value)):
            vcat[cur, pl.ds(b * C, C), pl.ds(t * N, N)] = term

    def k_finish(i, ch):
        m = i - 3
        wait_recv(sndh, rcvh, hs, hr, (i, ch))
        wait_recv(sndh, rcvq, qs, qr, (i, ch), (m, ch))
        wait_recv(sndk, rcvk, ks, kr, (m, ch))
        mine, near, beyond = sndh[i, ch], rcvh[i, ch], rcvq[m, ch]
        own_c = near * hdcT[0]
        lower_c = jnp.concatenate([beyond[0:16], mine[0:16]], axis=0) * hdcT[1]
        upper_c = jnp.concatenate([mine[16:32], beyond[16:32]], axis=0) * hdcT[2]
        terms = split(jnp.concatenate([own_c, lower_c, upper_c], axis=0))
        rep = dot_nn(jnp.concatenate(terms, axis=0).T, REP[...])
        for j in range(3):
            repv[j] = rep[:, j * N : (j + 1) * N].reshape(S, C, N)
        for j in range(3):
            for half in range(2):
                total = [jnp.zeros((C, N), f32)] * 8
                for a in range(S):
                    value = repv[j, a]
                    for b in range(8):
                        total[b] = total[b] + bcast_rows(BP, (j, a), half * 8 + b) * value
                for b in range(8):
                    for t, term in enumerate(split(total[b])):
                        wcat2[pl.ds((half * 8 + b) * C, C), pl.ds((j * T + t) * N, N)] = term
        back = turned_rows(dot_nt(TG[...], wcat2[...]))
        w_ref[...] = from_halo(own_c, Qh).reshape(S, C, N)
        e[ch] = e[ch] + w_ref[...]
        mid = own(w_ref, D)
        for a in range(S):
            acc[ch, a] = acc[ch, a] + mid[a] - back[a]
        others = jnp.concatenate([term[H : 3 * H] for term in terms], axis=0)
        rows = rcvk[m, ch] + dot_nn(SEL[...], others)
        total = far(
            vv.at[ch],
            jnp.concatenate([rows, own_c], axis=0),
            lambda: wait_recv(sndc, rcvc, cs, cr, (i, ch)),
            GH2,
        )
        got = from_halo(rcvc[i, ch], Pr).reshape(S, C, N)
        return [y[ch, a] - acc[ch, a] + got[a] + total[a] for a in range(S)]

    def advance(i, ch, coarse_start, values, first):
        which = coarse_start.astype(jnp.int32)
        scale = jnp.where(coarse_start, 1.0, hd[...])
        keep = jnp.where(coarse_start, 0.0, 1.0)
        for b, value in enumerate(values):
            if first is not None:
                raw[b] = value
                value = jnp.where(first, x_ref[b], value)
            y[ch, b] = value
            value = value * scale[b : b + 1, :]
            v[ch, b] = value
            e[ch, b] = e[ch, b] + keep * value
            split_pair(b, value, ch)
        send_rows(i, ch, which)

    def coarse_rest(i, ch):
        m = i - 3
        cur = ch
        start(sndh, rcvq, qs, qr, (i, ch), (m, ch))
        pairs = dot_nn(vcat[cur], Ql[...]).reshape(S, C, N)
        for b in range(S):
            value = (y[ch, b] + pairs[b]) * hdc[b : b + 1, :]
            v[ch, b] = value
            e[ch, b] = e[ch, b] + value
            split_pair(b, value, ch)
        sndk[m, ch] = dot_nt(Pn[0], vcat[cur])
        start(sndk, rcvk, ks, kr, (m, ch))

    def rr_store(row, ref, sign=1.0):
        for b in range(S):
            for t, term in enumerate(split(sign * ref[b])):
                rr[pl.ds(t * 128 + row, C), pl.ds(b * N, N)] = term

    def later_tables():
        hot = one_hot(iota((N, N), 0) == part_ref[...]).astype(bf16)
        halo = one_hot(iota((H, N), 0) + N == part_ref[...]).astype(bf16)
        for t in range(T):
            Ql[pl.ds(t * N, N), :] = hot
            Qh[pl.ds(t * H, H), :] = halo
        psel = one_hot(lanes == column(pair_ref)).astype(bf16)
        for t in range(T):
            Pn[1, :, pl.ds(t * N, N)] = psel
            for k in range(K):
                PK[:, pl.ds((k * T + t) * N, N)] = jnp.zeros((N, N), bf16)
                PK[pl.ds(k * H, H), pl.ds((k * T + t) * N, N)] = psel
                near_pair = dot_nn(psel, GS[0:N, (k * T) * N : (k * T + 1) * N]).astype(bf16)
                GH2[pl.ds(t * 2 * H + H, H), pl.ds(k * N, N)] = near_pair
            Pr[pl.ds(t * H, H), :] = sel
        for k in range(K):
            for t, term in enumerate(split(B[k].reshape(S * S, N))):
                wcat[:, pl.ds((k * T + t) * N, N)] = term
        BP[0] = dot_nt(wcat[...], PK[...]).reshape(S, S, N)
        targets = dot_nt(GS[...], PK[...]) * 0.5
        for t in range(T):
            TG[:, pl.ds(t * N, N)] = targets[0:N].astype(bf16)
        sndm[...] = jnp.zeros_like(sndm)
        sndm[:, 0:N] = targets[N : N + H]
        sndm[:, N : 2 * N] = dot_nt(sel, jnp.concatenate([psel, jnp.zeros((N - H, N), bf16)], axis=0))
        for t in range(T):
            for j in range(3):
                row = iota((H, 3 * N), 0)
                col = iota((H, 3 * N), 1)
                hit = (lax.div(col, N) == j) & (lax.rem(col, H) == row)
                REP[pl.ds((t * 3 + j) * H, H), :] = one_hot(hit).astype(bf16)

    live = [jnp.where(deg_ref[...] > k, 1.0, 0.0).astype(f32) for k in range(K)]

    def outer(left, right, k):
        def body(s, total):
            value = right[k, s]
            return tuple(total[a] + left[k, s, a : a + 1, :] * value for a in range(S))

        return lax.fori_loop(0, S, body, tuple(jnp.zeros((S, N), f32) for _ in range(S)), unroll=4)

    fetch(3).wait()
    rows = None
    for k in range(K):
        for a, value in enumerate(outer(oth_ref, oth_ref, k)):
            store_split_w(k, a, value * live[k])
        rows = scatter_slot(k, rows)
    sndc[LAST, 0] = rows[N : N + H]
    D[...] = turned_rows(rows)
    fetch(2).wait()
    for k in range(K):
        for a, value in enumerate(outer(own_ref, oth_ref, k)):
            B[k, a] = value * live[k]
    fetch(0).wait()
    v[1] = x_ref[...]
    store_split_v(x_ref, 1)
    sndh[0, 1] = dot_nt(Pn[0], vcat[1])
    rows = reverse(v.at[1])
    sndc[0, 1] = rows[N : N + H]
    back_rows[1] = rows[0:N]
    pl.semaphore_wait(barrier, n_bar)
    vouch()
    start(sndh, rcvh, hs, hr, (0, 1))
    start(sndc, rcvc, cs, cr, (LAST, 0))
    start(sndc, rcvc, cs, cr, (0, 1))
    for k in range(K):
        for a, value in enumerate(outer(own_ref, own_ref, k)):
            D[a] = D[a] + value * live[k]
    fetch(4).wait()
    for b in range(S):
        D[b, b : b + 1, :] = D[b, b : b + 1, :] + mass_ref[b : b + 1, :]
    a_local(1)
    fetch(1).wait()
    v[0] = p_ref[...]
    store_split_v(p_ref)
    send_rows(0, 0, 0)
    a_send(0, 0)
    a_local(0)
    e[...] = jnp.zeros_like(e)
    y[...] = jnp.zeros_like(y)
    rr[...] = jnp.zeros_like(rr)
    rr_store(0, x_ref)
    rr_store(16, p_ref)
    later_tables()
    start(sndm, rcvm, ms, mr, ())
    for c in both_copies(BP, bs, br):
        c.start()

    wait_recv(sndc, rcvc, cs, cr, (LAST, 0))
    w_ref[...] = from_halo(rcvc[LAST, 0], Pr).reshape(S, S, N)
    for ch in (1, 0):
        total = own(v.at[ch], w_ref)
        for a in range(S):
            acc[ch, a] = acc[ch, a] + total[a]
    D[...] = D[...] + w_ref[...]
    for b in range(S):
        diag[b : b + 1, :] = D[b, b : b + 1, :]
    hd[...] = 0.5 / diag[...]
    dcat = jnp.concatenate(split(diag[...]), axis=1)
    sndd[...] = jnp.zeros_like(sndd)
    sndd[:, 0:S] = dot_nt(Pn[1], dcat)
    start(sndd, rcvd, ds, dr, ())

    def event(i, g):
        ch = 1 - g
        coarse_end = (i == 4) | (i == 5)
        coarse_start = (i == 3) | (i == 4)

        @pl.when(jnp.logical_not(coarse_end))
        def _():
            advance(i, ch, coarse_start, a_finish(i - 1, ch), (i == 1) & (ch == 0))

        @pl.when(coarse_end)
        def _():
            advance(i, ch, coarse_start, k_finish(i - 1, ch), None)

        @pl.when(coarse_start)
        def _():
            coarse_rest(i, ch)

        a_send(i, ch)
        return 0

    def both_chains(j, _):
        i = 1 + j
        lax.fori_loop(0, 2, lambda g, c: event(i, g), 0)

        @pl.when(i == 1)
        def _():
            rr_store(32, y.at[1], -1.0)
            rr_store(48, raw, -1.0)

        def rest(g, _):
            a_local(1 - g)
            return 0

        lax.fori_loop(0, 2, rest, 0)
        late = i > 0


        @pl.when(late & (i == 1))
        def _():
            left = jnp.concatenate([rr[0:32, :], rr[128:160, :]], axis=0)
            parts = dot_nt(left, rr[...])
            parts = parts[:, 0:128] + parts[:, 128:256]
            parts = (parts[0:32] + parts[32:64]) * (1.0 / (N * S * n_dom))
            rolled = pltpu.roll(parts[16:32], 64, 1)
            ar_start(0, 0, jnp.where(iota((C, 128), 1) < 64, parts[0:16], rolled))
            for j in range(2):
                pl.semaphore_wait(vouched.at[j], 1)

        @pl.when(late & (i == 2))
        def _():
            wait_recv(sndd, rcvd, ds, dr, ())
            dcat = jnp.concatenate(split(diag[...]), axis=1)
            far_diag = from_halo(rcvd[...], Qh)[0:S]
            hdc[...] = 0.5 / (diag[...] + dot_nn(dcat, Ql[...]) + far_diag)
            for b in range(S):
                split_pair(b, jnp.broadcast_to(hdc[b : b + 1, :], (C, N)), 0)
            hdcT[0] = dot_nt(Pn[1], vcat[0])
            for c in both_copies(hdcT, ts, tr):
                c.start()

        @pl.when(late & (i == 3))
        def _():
            wait_recv(sndm, rcvm, ms, mr, ())
            for c in both_copies(BP, bs, br):
                c.wait_recv()
            row = iota((H, N), 0)
            for j, keep in ((1, row < 16), (2, row >= 16)):
                there = jnp.where(keep, rcvm[:, 0:N], 0.0).astype(bf16)
                target = dot_tn(Pr[0:H, :], there).astype(bf16)
                for t in range(T):
                    TG[:, pl.ds((j * T + t) * N, N)] = target
            same = rcvm[:, N : 2 * N]
            half = jnp.where(row < 16, same, pltpu.roll(same, H, 1))
            SEL[...] = (half + pltpu.roll(half, 2 * H, 1)).astype(bf16)
            for c in both_copies(hdcT, ts, tr):
                c.wait_recv()

        stages = len(groups[0])
        for s in range(stages):

            @pl.when(late & (i == 2 + s))
            def _(s=s):
                total = ar_finish(0, s)
                if s + 1 < stages:
                    ar_start(0, s + 1, total)
                else:
                    gram1[...] = total
                    lane = iota((C, 128), 1)
                    work = jnp.where(lane < 16, total, jnp.where(lane < 32, pltpu.roll(total, 112, 1), 0.0))
                    for j in range(C):
                        col = jnp.sum(jnp.where(lane == j, work, 0.0), axis=1, keepdims=True)
                        row = work[j : j + 1, :] / col[j : j + 1, :]
                        unit = jnp.where(iota((C, 1), 0) == j, 1.0, 0.0)
                        work = work - (col - unit) * row
                    square = jnp.concatenate([work, jnp.zeros((128 - C, 128), f32)], axis=0).T
                    quot_t = square[16:32, :]
                    for j in range(C):
                        col = jnp.sum(jnp.where(lane == j, quot_t, 0.0), axis=1, keepdims=True)
                        qb[j] = jnp.broadcast_to(col, (C, 128))

        return 0

    lax.fori_loop(0, LAST - 1, both_chains, 0)

    def last_event(g, _):
        ch = 1 - g
        for b, value in enumerate(a_finish(LAST - 1, ch)):
            e[ch, b] = e[ch, b] + value * hd[b : b + 1, :]
        return 0

    lax.fori_loop(0, 2, last_event, 0)

    def combine(b, _):
        total = -e[1, b]
        for j in range(C):
            total = total - qb[j] * e[0, b, j : j + 1, :]
        w_ref[b] = total
        return 0

    lax.fori_loop(0, S, combine, 0)

    result = pltpu.make_async_copy(w_ref, out_ref, in_sems.at[10])
    result.start()
    store_split_v(w_ref)
    sndh[LAST, 0] = dot_nt(Pn[0], vcat[0])
    start(sndh, rcvh, hs, hr, (LAST, 0))
    rr_store(64, w_ref)
    lane = iota((C, 128), 1)
    scale = 1.0 / (N * S * n_dom)
    left = jnp.concatenate([rr[64:80, :], rr[192:208, :]], axis=0)
    parts = dot_nt(left, rr[...])
    parts = (parts[0:16, 0:128] + parts[0:16, 128:256] + parts[16:32, 0:128] + parts[16:32, 128:256]) * scale
    low = jnp.where(lane < 64, parts, 0.0)
    ar_start(1, 0, low[0:8] + pltpu.roll(low[8:16], 64, 1))

    diagonal = lax.div(lane, 16) == lax.rem(iota((C, 128), 0), 8)

    def pack_block(block):
        for shift in (16, 32, 64):
            block = block + pltpu.roll(block, shift, 1)
        block = jnp.where(diagonal, block, 0.0)
        top = jnp.sum(block[0:8], axis=0, keepdims=True)
        return jnp.concatenate([top, jnp.sum(block[8:16], axis=0, keepdims=True)], axis=0)

    def unpack_block(pair):
        wide = jnp.concatenate(
            [jnp.broadcast_to(pair[0:1], (8, 128)), jnp.broadcast_to(pair[1:2], (8, 128))], axis=0
        )
        wide = jnp.where(diagonal, wide, 0.0)
        for shift in (16, 32, 64):
            wide = wide + pltpu.roll(wide, shift, 1)
        return wide

    def lanes_from(value, source):
        return jnp.where(lane < 16, pltpu.roll(value, 128 - source, 1), 0.0)

    gram2[0:2, :] = pack_block(lanes_from(parts, 64))
    rows = reverse(w_ref)
    turned = jnp.concatenate([term[0 : 2 * H] for term in split(jnp.concatenate([rows[N : N + H], rows[N : N + H]], axis=0))], axis=0).T
    zcat[...] = turned
    gather_local(vv.at[0])
    back = turned_rows(rows)
    near = vv.at[0]
    mid = own(w_ref, D)
    for a in range(S):
        acc[0, a] = mid[a] - back[a]
    mid = far(near, jnp.zeros((H, S * C), f32))
    for a in range(S):
        v[0, a] = acc[0, a] - mid[a]
    rr_store(80, v.at[0])
    parts = dot_nt(left, rr[...])
    parts = parts[0:16, 0:128] + parts[0:16, 128:256] + parts[16:32, 0:128] + parts[16:32, 128:256]
    gram2[2:4, :] = pack_block(lanes_from(parts, 80) * scale)
    wait_recv(sndh, rcvh, hs, hr, (LAST, 0))
    terms = split(rcvh[LAST, 0])
    edges = dot_nn(zcat[...], jnp.concatenate([terms[0], terms[1], terms[0], terms[1]], axis=0))
    same = lax.div(iota((S * C, S * C), 0), C) == lax.div(iota((S * C, S * C), 1), C)
    edges = jnp.sum(jnp.where(same, edges, 0.0).reshape(S, C, S * C), axis=0)
    edges = edges[:, 0:128] + edges[:, 128:256]
    ar_start(2, 0, jnp.concatenate([gram2[2:4, :] - pack_block(edges * (2.0 * scale)), gram2[0:2, :]], axis=0))

    def drain(g, _):
        i, ch = lax.div(g, 2), lax.rem(g, 2)
        wait_send(sndh, rcvh, hs, hr, (i, ch))
        wait_send(sndc, rcvc, cs, cr, (i, ch))
        return 0

    def drain_coarse(g, _):
        m, ch = lax.div(g, 2), lax.rem(g, 2)
        wait_send(sndk, rcvk, ks, kr, (m, ch))
        wait_send(sndh, rcvq, qs, qr, (m + 3, ch), (m, ch))
        return 0

    ar_start(1, 1, ar_finish(1, 0))
    lax.fori_loop(0, 2 * LAST, drain, 0)
    wait_send(sndh, rcvh, hs, hr, (LAST, 0))
    wait_send(sndc, rcvc, cs, cr, (LAST, 0))
    wait_send(sndd, rcvd, ds, dr, ())
    ar_start(2, 1, ar_finish(2, 0))
    lax.fori_loop(0, 4, drain_coarse, 0)
    wait_send(sndm, rcvm, ms, mr, ())
    for c in both_copies(BP, bs, br) + both_copies(hdcT, ts, tr):
        c.wait_send()
    for s in range(len(groups[0])):
        ar_drain(0, s)
    ar_drain(1, 0)
    ar_drain(2, 0)
    half = ar_finish(1, 1)
    high = pltpu.roll(half, 64, 1)
    g2 = jnp.where(lane < 64, jnp.concatenate([half, high], axis=0), 0.0)

    def place(value, source, target):
        shift = (target - source) % 128
        moved = pltpu.roll(value, shift, 1) if shift else value
        return jnp.where((lane >= target) & (lane < target + 16), moved, 0.0)

    g1 = gram1[...]
    turned = jnp.concatenate([g2, jnp.zeros((128 - C, 128), f32)], axis=0).T
    xw, pw, xaw, paw = [turned[16 * j : 16 * j + 16, :] for j in range(4)]
    gb_ref[0:16, :] = (place(g1, 0, 0) + place(xw, 0, 16) + place(g1, 16, 32))[:, 0:48]
    gb_ref[32:48, :] = (place(g1, 64, 0) + place(pw, 0, 16) + place(g1, 80, 32))[:, 0:48]
    ga_ref[0:16, :] = (place(g1, 32, 0) + place(xaw, 0, 16) + place(g1, 48, 32))[:, 0:48]
    ga_ref[32:48, :] = (place(g1, 96, 0) + place(paw, 0, 16) + place(g1, 112, 32))[:, 0:48]
    wide_a = place(g2, 32, 0) + place(g2, 48, 32)
    wide_b = place(g2, 0, 0) + place(g2, 16, 32)
    ar_drain(1, 1)
    last = ar_finish(2, 1)
    image = unpack_block(last[0:2])
    square = jnp.concatenate([jnp.where(lane < 16, image, 0.0), jnp.zeros((128 - C, 128), f32)], axis=0).T
    image = 0.5 * (jnp.where(lane < 16, image, 0.0) + square[0:16, :])
    ga_ref[16:32, :] = (wide_a + place(image, 0, 16))[:, 0:48]
    gb_ref[16:32, :] = (wide_b + place(unpack_block(last[2:4]), 16, 16))[:, 0:48]
    ar_drain(2, 1)
    result.wait()


def move_results(a_in, b_in, c_in, a_out, b_out, c_out, a_mid, b_mid, c_mid, sems):
    sets = ((a_in, a_mid, a_out), (b_in, b_mid, b_out), (c_in, c_mid, c_out))
    first = [pltpu.make_async_copy(src, mid, sems.at[j]) for j, (src, mid, _) in enumerate(sets)]
    second = [pltpu.make_async_copy(mid, dst, sems.at[3 + j]) for j, (_, mid, dst) in enumerate(sets)]
    for c in first:
        c.start()
    for before, after in zip(first, second):
        before.wait()
        after.start()
    for c in second:
        c.wait()


def shards(n_dom, ar_dims, x, p, f_own, f_other, mass, cols, degree, send, pair, partner):
    vm = pltpu.VMEM
    dma = pltpu.SemaphoreType.DMA

    def size(dims):
        total = 1
        for _, g in dims:
            total *= g
        return total

    rows = (16, 8, 4)
    i32 = jnp.int32
    scratch = [
        vm((S, C, N), f32),
        vm((S, C, N), f32),
        vm((K, S, S, N), f32),
        vm((K, S, S, N), f32),
        vm((S, N), f32),
        vm((K, N), i32),
        vm((1, N), i32),
        vm((1, H), i32),
        vm((1, H), i32),
        vm((1, N), i32),
        dma((11,)),
        vm((K, S, S, N), f32),
        vm((S, S, N), f32),
        vm((S, N), f32),
        vm((S, N), f32),
        vm((S, N), f32),
        vm((2, S, C, N), f32),
        vm((2, S, C, N), f32),
        vm((2, S, C, N), f32),
        vm((2, S, C, N), f32),
        vm((2, K, S, C, N), f32),
        vm((S, C, N), f32),
        vm((C, C, 128), f32),
        vm((C, 128), f32),
        vm((C, 128), f32),
        vm((2, S * C, T * N), bf16),
        vm((S * C, T * K * N), bf16),
        vm((256, S * N), bf16),
        vm((T * N, K * N), bf16),
        vm((N + H, T * K * N), bf16),
        vm((T * H, K * N), bf16),
        vm((2, H, T * N), bf16),
        vm((T * H, N), bf16),
        vm((T * N, N), bf16),
        vm((T * H, N), bf16),
        vm((S, C, N), f32),
        vm((N, T * K * N), bf16),
        vm((T * 2 * H, K * N), bf16),
        vm((T * 3 * H, 3 * N), bf16),
        vm((3, S, S, N), f32),
        vm((3, H, S * C), f32),
        vm((N, 3 * T * N), bf16),
        vm((H, N), bf16),
        vm((3, S, C, N), f32),
        vm((S * C, 3 * T * N), bf16),
        vm((S * C, 2 * T * H), bf16),
        vm((2, N, S * C), f32),
        vm((LAST + 1, 2, H, S * C), f32),
        vm((LAST + 1, 2, H, S * C), f32),
        vm((LAST + 1, 2, H, S * C), f32),
        vm((LAST + 1, 2, H, S * C), f32),
        vm((H, 128), f32),
        vm((H, 128), f32),
        vm((2, 2, H, S * C), f32),
        vm((2, 2, H, S * C), f32),
        vm((2, 2, H, S * C), f32),
        vm((H, 2 * N), f32),
        vm((H, 2 * N), f32),
        [[vm((size(d), rows[j], 128), f32) for d in st] for j, st in enumerate(ar_dims)],
        dma((LAST + 1, 2, 2)),
        dma((LAST + 1, 2, 2)),
        dma((LAST + 1, 2, 2)),
        dma((LAST + 1, 2, 2)),
        dma((2,)),
        dma((2,)),
        dma((2, 2, 2)),
        dma((2, 2, 2)),
        dma((2, 2, 2)),
        dma((2, 2, 2)),
        dma((2,)),
        dma((2,)),
        dma((3,)),
        dma((3,)),
        dma((3,)),
        dma((3,)),
        [[dma((size(d),)) for d in st] for st in ar_dims],
        [[dma((size(d),)) for d in st] for st in ar_dims],
        pltpu.SemaphoreType.REGULAR((2,)),
    ]
    whole = pl.BlockSpec(memory_space=pltpu.VMEM)
    results = pl.pallas_call(
        functools.partial(kernel, n_dom, ar_dims),
        out_shape=(
            jax.ShapeDtypeStruct((S, C, N), f32),
            jax.ShapeDtypeStruct((3 * C, 3 * C), f32),
            jax.ShapeDtypeStruct((3 * C, 3 * C), f32),
        ),
        in_specs=[pl.BlockSpec(memory_space=pl.ANY)] * 10,
        out_specs=(pl.BlockSpec(memory_space=pl.ANY), whole, whole),
        scratch_shapes=scratch,
        compiler_params=pltpu.CompilerParams(
            collective_id=0, has_side_effects=True, vmem_limit_bytes=56 * 1024 * 1024
        ),
    )(
        x, p, f_own, f_other, mass, cols,
        degree.reshape(1, N), send.reshape(1, H), pair.reshape(1, H), partner.reshape(1, N),
    )
    any_space = pl.BlockSpec(memory_space=pl.ANY)
    return pl.pallas_call(
        move_results,
        out_shape=tuple(jax.ShapeDtypeStruct(r.shape, r.dtype) for r in results),
        in_specs=[any_space] * 3,
        out_specs=(any_space,) * 3,
        scratch_shapes=[vm(r.shape, r.dtype) for r in results] + [dma((6,))],
    )(*results)


def solution(mesh):
    n_dom = mesh.shape["dom"]
    if n_dom == 512:
        near = [[(1, 8)], [(128, 4)], [(8, 4)], [(32, 4)]]
        quick = [[(128, 4), (1, 8)], [(8, 16)]]
    else:
        near = [[(1, 2)], [(2, n_dom // 2)]]
        quick = [[(1, 2)], [(2, n_dom // 2)]]
    row = P(None, "dom")
    return jax.shard_map(
        functools.partial(shards, n_dom, (near, quick, quick)),
        mesh=mesh,
        in_specs=(
            P(None, None, "dom"),
            P(None, None, "dom"),
            P(None, None, None, "dom"),
            P(None, None, None, "dom"),
            row, row, P("dom"), P("dom"), P("dom"), P("dom"),
        ),
        out_specs=(P(None, None, "dom"), P(), P()),
        check_vma=False,
    )
```

```python
import functools

import jax
import jax.numpy as jnp
from jax import lax
from jax.experimental import pallas as pl
from jax.experimental.pallas import tpu as pltpu
from jax.sharding import PartitionSpec as P

MESH = pl.DeviceIdType.MESH
f32 = jnp.float32
bf16 = jnp.bfloat16
S = 16
C = 16
K = 4
N = 128
H = 32
T = 2
LAST = 6


def iota(shape, dim):
    return lax.broadcasted_iota(jnp.int32, shape, dim)


def one_hot(mask):
    return jnp.where(mask, 1.0, 0.0).astype(f32)


def split(value):
    terms = []
    for t in range(T):
        term = value.astype(bf16)
        terms.append(term)
        if t + 1 < T:
            value = value - term.astype(f32)
    return terms


def dot_nn(a, b):
    return jnp.dot(a, b, preferred_element_type=f32)


def dot_nt(a, b):
    return lax.dot_general(a, b, (((1,), (1,)), ((), ())), preferred_element_type=f32)


def dot_tn(a, b):
    return lax.dot_general(a, b, (((0,), (0,)), ((), ())), preferred_element_type=f32)


class Groups:
    def __init__(self, me, dims):
        self.me, self.dims = me, dims
        self.size = 1
        for _, g in dims:
            self.size *= g
        self.pos = 0
        self.base = me
        for s, g in dims:
            p = lax.rem(lax.div(me, s), g)
            self.pos = self.pos * g + p
            self.base = self.base - p * s

    def device(self, pos):
        d = self.base
        for s, g in reversed(self.dims):
            d = d + lax.rem(pos, g) * s
            pos = lax.div(pos, g)
        return d

    def peer(self, t):
        return lax.rem(self.pos + t, self.size)


def kernel(
    n_dom, ar_dims,
    x_in, p_in, own_in, oth_in, mass_in, cols_in, deg_in, send_in, pair_in, part_in,
    out_ref, ga_ref, gb_ref,
    x_ref, p_ref, own_ref, oth_ref, mass_ref, cols_ref, deg_ref, send_ref, pair_ref, part_ref, in_sems,
    B, D, hd, hdc, diag, v, y, e, acc, vv, w_ref, qb, gram1, gram2,
    vcat, wcat, rr, Gl, GS, GHs, Pn, Pr, Ql, Qh, raw, PK, GH2, REP, BP, hdcT, TG, SEL, repv, wcat2, zcat, back_rows,
    sndh, rcvh, sndc, rcvc, sndd, rcvd, sndk, rcvk, rcvq, sndm, rcvm, ar_bufs,
    hs, hr, cs, cr, ds, dr, ks, kr, qs, qr, ms, mr, bs, br, ts, tr, ar_ss, ar_rs, vouched,
):
    me = lax.axis_index("dom")
    lower = lax.rem(me + n_dom - 1, n_dom)
    upper = lax.rem(me + 1, n_dom)
    lower2 = lax.rem(me + n_dom - 2, n_dom)
    upper2 = lax.rem(me + 2, n_dom)
    groups = [[Groups(me, dims) for dims in stages] for stages in ar_dims]
    bar_groups = groups[1]

    barrier = pltpu.get_barrier_semaphore()
    for d in (lower, upper, lower2, upper2):
        pl.semaphore_signal(barrier, inc=1, device_id=(d,), device_id_type=MESH)
    wide, ring = bar_groups
    reach = 4
    n_bar = 4 + wide.size - 1 + 2 * reach

    def greet(g, t):
        pl.semaphore_signal(barrier, inc=1, device_id=(g.device(g.peer(t)),), device_id_type=MESH)

    def greet_wide(t, _):
        greet(wide, t)
        return 0

    for t in range(reach, 0, -1):
        greet(ring, t)
        greet(ring, ring.size - t)
    lax.fori_loop(1, wide.size, greet_wide, 0)

    def vouch():
        for j, t in enumerate((reach, ring.size - reach)):
            pl.semaphore_signal(
                vouched.at[j], inc=1, device_id=(ring.device(ring.peer(t)),), device_id_type=MESH
            )

    def fetch(j):
        src = (x_in, p_in, own_in, oth_in, mass_in, cols_in, deg_in, send_in, pair_in, part_in)[j]
        dst = (x_ref, p_ref, own_ref, oth_ref, mass_ref, cols_ref, deg_ref, send_ref, pair_ref, part_ref)[j]
        return pltpu.make_async_copy(src, dst, in_sems.at[j])

    for j in (5, 9, 7, 8, 6, 3, 2, 0, 1, 4):
        fetch(j).start()

    def pair_copies(snd, rcv, ss, rs, idx, far_idx=None):
        out = []
        devices = (lower, upper) if far_idx is None else (lower2, upper2)
        src_idx = idx
        if far_idx is not None:
            idx = far_idx
        for side, (src, dst, dev) in enumerate(((0, 16, devices[0]), (16, 0, devices[1]))):
            out.append(
                pltpu.make_async_remote_copy(
                    snd.at[src_idx + (pl.ds(src, 16),)],
                    rcv.at[idx + (pl.ds(dst, 16),)],
                    ss.at[idx + (side,)],
                    rs.at[idx + (side,)],
                    device_id=(dev,),
                    device_id_type=MESH,
                )
            )
        return out

    def start(*args):
        for c in pair_copies(*args):
            c.start()

    def wait_recv(*args):
        for c in pair_copies(*args):
            c.wait_recv()

    def wait_send(*args):
        for c in pair_copies(*args):
            c.wait_send()

    def both_copies(ref, ss, rs):
        return [
            pltpu.make_async_remote_copy(
                ref.at[0], ref.at[at], ss.at[at], rs.at[at], device_id=(dev,), device_id_type=MESH
            )
            for at, dev in ((1, upper), (2, lower))
        ]

    def ar_copy(slot, stage, t, receive):
        g = groups[slot][stage]
        peer = g.peer(t)
        buf = ar_bufs[slot][stage]
        at = peer if receive else g.pos
        return pltpu.make_async_remote_copy(
            buf.at[g.pos],
            buf.at[at],
            ar_ss[slot][stage].at[peer],
            ar_rs[slot][stage].at[at],
            device_id=(g.device(peer),),
            device_id_type=MESH,
        )

    def ar_start(slot, stage, value):
        g = groups[slot][stage]
        ar_bufs[slot][stage][g.pos] = value

        if slot == 2:
            for t in range(1, g.size):
                ar_copy(slot, stage, t, False).start()
            return

        def go(t, _):
            ar_copy(slot, stage, t, False).start()
            return 0

        lax.fori_loop(1, g.size, go, 0)

    def ar_finish(slot, stage):
        g = groups[slot][stage]

        def go(t, _):
            ar_copy(slot, stage, t, True).wait_recv()
            return 0

        if slot == 2:
            for t in range(1, g.size):
                go(t, 0)
        else:
            lax.fori_loop(1, g.size, go, 0)
        buf = ar_bufs[slot][stage]
        total = buf[0]
        for j in range(1, g.size):
            total = total + buf[j]
        return total

    def ar_drain(slot, stage):
        g = groups[slot][stage]

        def go(t, _):
            ar_copy(slot, stage, t, False).wait_send()
            return 0

        lax.fori_loop(1, g.size, go, 0)

    for j in (5, 9, 7, 8, 6):
        fetch(j).wait()
    for k in range(K):
        at_k = pl.ds(k * N, N)
        hot = one_hot(iota((N, N), 0) == cols_ref[k : k + 1, :]).astype(bf16)
        halo = one_hot(iota((H, N), 0) + N == cols_ref[k : k + 1, :]).astype(bf16)
        for t in range(T):
            Gl[pl.ds(t * N, N), at_k] = hot
            GS[0:N, pl.ds((k * T + t) * N, N)] = hot
            GS[N : N + H, pl.ds((k * T + t) * N, N)] = halo
            GHs[pl.ds(t * H, H), at_k] = halo
            GH2[pl.ds(t * 2 * H, H), at_k] = halo
    def column(ref):
        square = jnp.where(iota((H, H), 0) == iota((H, H), 1), ref[...].astype(f32), 0.0)
        return jnp.sum(square, axis=1, keepdims=True)

    lanes = iota((H, N), 1).astype(f32)
    sel = one_hot(lanes == column(send_ref)).astype(bf16)
    for t in range(T):
        Pn[0, :, pl.ds(t * N, N)] = sel

    def bcast_rows(ref, idx, r):
        return ref[idx + (slice(r, r + 1), slice(None))]

    def store_split_w(k, b, value):
        for t, term in enumerate(split(value)):
            wcat[pl.ds(b * C, C), pl.ds((k * T + t) * N, N)] = term

    def store_split_v(ref, cur=0):
        for b in range(S):
            for t, term in enumerate(split(ref[b])):
                vcat[cur, pl.ds(b * C, C), pl.ds(t * N, N)] = term

    def scatter_slot(k, total):
        at_k = slice(k * T * N, (k + 1) * T * N)
        part = dot_nt(GS[:, at_k], wcat[:, at_k])
        return part if total is None else total + part

    def turned_rows(rows):
        return jnp.concatenate([rows[0:N, 0:N].T, rows[0:N, N : 2 * N].T], axis=0).reshape(S, C, N)

    def from_halo(rows, matrix):
        return dot_tn(jnp.concatenate(split(rows), axis=0), matrix[...])

    def reverse(ref):
        rows = None
        for k in range(K):
            for half in range(2):
                total = [jnp.zeros((C, N), f32)] * 8
                for a in range(S):
                    value = ref[a]
                    for j in range(8):
                        total[j] = total[j] + bcast_rows(B, (k, a), half * 8 + j) * value
                for j in range(8):
                    store_split_w(k, half * 8 + j, total[j])
            rows = scatter_slot(k, rows)
        return rows

    def far(near, rows, half_way=None, table=None):
        rows = jnp.concatenate(split(rows), axis=0).T
        table = GHs if table is None else table
        total = [jnp.zeros((C, N), f32)] * S
        for k in range(K):
            if k % 2 == 0:
                got = dot_nn(rows, table[:, k * N : (k + 2) * N])
            if k == 3 and half_way is not None:
                half_way()
            part = got[:, (k % 2) * N : (k % 2 + 1) * N].reshape(S, C, N)
            near[k] = near[k] + part
            for b in range(S):
                value = near[k, b]
                for a in range(S):
                    total[a] = total[a] + bcast_rows(B, (k, a), b) * value
        return total

    def own(ref, D):
        total = [jnp.zeros((C, N), f32)] * S
        for b in range(S):
            value = ref[b]
            for a in range(S):
                total[a] = total[a] + bcast_rows(D, (a,), b) * value
        return total

    def gather_local(dst, cur=0):
        rows = dot_nn(vcat[cur], Gl[...])
        for k in range(K):
            dst[k] = rows[:, k * N : (k + 1) * N].reshape(S, C, N)

    def send_rows(i, ch, which):
        cur = ch
        sndh[i, ch] = dot_nt(Pn[which], vcat[cur])
        start(sndh, rcvh, hs, hr, (i, ch))

    def a_send(i, ch):
        rows = reverse(v.at[ch])
        sndc[i, ch] = rows[N : N + H]
        start(sndc, rcvc, cs, cr, (i, ch))
        back_rows[ch] = rows[0:N]

    def a_local(ch):
        src = v.at[ch]
        rows = back_rows[ch]
        gather_local(vv.at[ch], ch)
        back = turned_rows(rows)
        total = own(src, D)
        for a in range(S):
            acc[ch, a] = total[a] - back[a]

    def a_finish(i, ch):
        wait_recv(sndh, rcvh, hs, hr, (i, ch))
        total = far(
            vv.at[ch], rcvh[i, ch], lambda: wait_recv(sndc, rcvc, cs, cr, (i, ch))
        )
        got = from_halo(rcvc[i, ch], Pr).reshape(S, C, N)
        return [y[ch, a] - acc[ch, a] + got[a] + total[a] for a in range(S)]

    def split_pair(b, value, cur):
        for t, term in enumerate(split(value)):
            vcat[cur, pl.ds(b * C, C), pl.ds(t * N, N)] = term

    def k_finish(i, ch):
        m = i - 3
        wait_recv(sndh, rcvh, hs, hr, (i, ch))
        wait_recv(sndh, rcvq, qs, qr, (i, ch), (m, ch))
        wait_recv(sndk, rcvk, ks, kr, (m, ch))
        mine, near, beyond = sndh[i, ch], rcvh[i, ch], rcvq[m, ch]
        own_c = near * hdcT[0]
        lower_c = jnp.concatenate([beyond[0:16], mine[0:16]], axis=0) * hdcT[1]
        upper_c = jnp.concatenate([mine[16:32], beyond[16:32]], axis=0) * hdcT[2]
        terms = split(jnp.concatenate([own_c, lower_c, upper_c], axis=0))
        rep = dot_nn(jnp.concatenate(terms, axis=0).T, REP[...])
        for j in range(3):
            repv[j] = rep[:, j * N : (j + 1) * N].reshape(S, C, N)
        for j in range(3):
            for half in range(2):
                total = [jnp.zeros((C, N), f32)] * 8
                for a in range(S):
                    value = repv[j, a]
                    for b in range(8):
                        total[b] = total[b] + bcast_rows(BP, (j, a), half * 8 + b) * value
                for b in range(8):
                    for t, term in enumerate(split(total[b])):
                        wcat2[pl.ds((half * 8 + b) * C, C), pl.ds((j * T + t) * N, N)] = term
        back = turned_rows(dot_nt(TG[...], wcat2[...]))
        w_ref[...] = from_halo(own_c, Qh).reshape(S, C, N)
        e[ch] = e[ch] + w_ref[...]
        mid = own(w_ref, D)
        for a in range(S):
            acc[ch, a] = acc[ch, a] + mid[a] - back[a]
        others = jnp.concatenate([term[H : 3 * H] for term in terms], axis=0)
        rows = rcvk[m, ch] + dot_nn(SEL[...], others)
        total = far(
            vv.at[ch],
            jnp.concatenate([rows, own_c], axis=0),
            lambda: wait_recv(sndc, rcvc, cs, cr, (i, ch)),
            GH2,
        )
        got = from_halo(rcvc[i, ch], Pr).reshape(S, C, N)
        return [y[ch, a] - acc[ch, a] + got[a] + total[a] for a in range(S)]

    def advance(i, ch, coarse_start, values, first):
        which = coarse_start.astype(jnp.int32)
        scale = jnp.where(coarse_start, 1.0, hd[...])
        keep = jnp.where(coarse_start, 0.0, 1.0)
        for b, value in enumerate(values):
            if first is not None:
                raw[b] = value
                value = jnp.where(first, x_ref[b], value)
            y[ch, b] = value
            value = value * scale[b : b + 1, :]
            v[ch, b] = value
            e[ch, b] = e[ch, b] + keep * value
            split_pair(b, value, ch)
        send_rows(i, ch, which)

    def coarse_rest(i, ch):
        m = i - 3
        cur = ch
        start(sndh, rcvq, qs, qr, (i, ch), (m, ch))
        pairs = dot_nn(vcat[cur], Ql[...]).reshape(S, C, N)
        for b in range(S):
            value = (y[ch, b] + pairs[b]) * hdc[b : b + 1, :]
            v[ch, b] = value
            e[ch, b] = e[ch, b] + value
            split_pair(b, value, ch)
        sndk[m, ch] = dot_nt(Pn[0], vcat[cur])
        start(sndk, rcvk, ks, kr, (m, ch))

    def rr_store(row, ref, sign=1.0):
        for b in range(S):
            for t, term in enumerate(split(sign * ref[b])):
                rr[pl.ds(t * 128 + row, C), pl.ds(b * N, N)] = term

    def later_tables():
        hot = one_hot(iota((N, N), 0) == part_ref[...]).astype(bf16)
        halo = one_hot(iota((H, N), 0) + N == part_ref[...]).astype(bf16)
        for t in range(T):
            Ql[pl.ds(t * N, N), :] = hot
            Qh[pl.ds(t * H, H), :] = halo
        psel = one_hot(lanes == column(pair_ref)).astype(bf16)
        for t in range(T):
            Pn[1, :, pl.ds(t * N, N)] = psel
            for k in range(K):
                PK[:, pl.ds((k * T + t) * N, N)] = jnp.zeros((N, N), bf16)
                PK[pl.ds(k * H, H), pl.ds((k * T + t) * N, N)] = psel
                near_pair = dot_nn(psel, GS[0:N, (k * T) * N : (k * T + 1) * N]).astype(bf16)
                GH2[pl.ds(t * 2 * H + H, H), pl.ds(k * N, N)] = near_pair
            Pr[pl.ds(t * H, H), :] = sel
        for k in range(K):
            for t, term in enumerate(split(B[k].reshape(S * S, N))):
                wcat[:, pl.ds((k * T + t) * N, N)] = term
        BP[0] = dot_nt(wcat[...], PK[...]).reshape(S, S, N)
        targets = dot_nt(GS[...], PK[...]) * 0.5
        for t in range(T):
            TG[:, pl.ds(t * N, N)] = targets[0:N].astype(bf16)
        sndm[...] = jnp.zeros_like(sndm)
        sndm[:, 0:N] = targets[N : N + H]
        sndm[:, N : 2 * N] = dot_nt(sel, jnp.concatenate([psel, jnp.zeros((N - H, N), bf16)], axis=0))
        for t in range(T):
            for j in range(3):
                row = iota((H, 3 * N), 0)
                col = iota((H, 3 * N), 1)
                hit = (lax.div(col, N) == j) & (lax.rem(col, H) == row)
                REP[pl.ds((t * 3 + j) * H, H), :] = one_hot(hit).astype(bf16)

    live = [jnp.where(deg_ref[...] > k, 1.0, 0.0).astype(f32) for k in range(K)]

    def outer(left, right, k):
        def body(s, total):
            value = right[k, s]
            return tuple(total[a] + left[k, s, a : a + 1, :] * value for a in range(S))

        return lax.fori_loop(0, S, body, tuple(jnp.zeros((S, N), f32) for _ in range(S)), unroll=4)

    fetch(3).wait()
    rows = None
    for k in range(K):
        for a, value in enumerate(outer(oth_ref, oth_ref, k)):
            store_split_w(k, a, value * live[k])
        rows = scatter_slot(k, rows)
    sndc[LAST, 0] = rows[N : N + H]
    D[...] = turned_rows(rows)
    fetch(2).wait()
    for k in range(K):
        for a, value in enumerate(outer(own_ref, oth_ref, k)):
            B[k, a] = value * live[k]
    fetch(0).wait()
    v[1] = x_ref[...]
    store_split_v(x_ref, 1)
    sndh[0, 1] = dot_nt(Pn[0], vcat[1])
    rows = reverse(v.at[1])
    sndc[0, 1] = rows[N : N + H]
    back_rows[1] = rows[0:N]
    pl.semaphore_wait(barrier, n_bar)
    vouch()
    start(sndh, rcvh, hs, hr, (0, 1))
    start(sndc, rcvc, cs, cr, (LAST, 0))
    start(sndc, rcvc, cs, cr, (0, 1))
    for k in range(K):
        for a, value in enumerate(outer(own_ref, own_ref, k)):
            D[a] = D[a] + value * live[k]
    fetch(4).wait()
    for b in range(S):
        D[b, b : b + 1, :] = D[b, b : b + 1, :] + mass_ref[b : b + 1, :]
    a_local(1)
    fetch(1).wait()
    v[0] = p_ref[...]
    store_split_v(p_ref)
    send_rows(0, 0, 0)
    a_send(0, 0)
    a_local(0)
    e[...] = jnp.zeros_like(e)
    y[...] = jnp.zeros_like(y)
    rr[...] = jnp.zeros_like(rr)
    rr_store(0, x_ref)
    rr_store(16, p_ref)
    later_tables()
    start(sndm, rcvm, ms, mr, ())
    for c in both_copies(BP, bs, br):
        c.start()

    wait_recv(sndc, rcvc, cs, cr, (LAST, 0))
    w_ref[...] = from_halo(rcvc[LAST, 0], Pr).reshape(S, S, N)
    for ch in (1, 0):
        total = own(v.at[ch], w_ref)
        for a in range(S):
            acc[ch, a] = acc[ch, a] + total[a]
    D[...] = D[...] + w_ref[...]
    for b in range(S):
        diag[b : b + 1, :] = D[b, b : b + 1, :]
    hd[...] = 0.5 / diag[...]
    dcat = jnp.concatenate(split(diag[...]), axis=1)
    sndd[...] = jnp.zeros_like(sndd)
    sndd[:, 0:S] = dot_nt(Pn[1], dcat)
    start(sndd, rcvd, ds, dr, ())

    def event(i, g):
        ch = 1 - g
        coarse_end = (i == 4) | (i == 5)
        coarse_start = (i == 3) | (i == 4)

        @pl.when(jnp.logical_not(coarse_end))
        def _():
            advance(i, ch, coarse_start, a_finish(i - 1, ch), (i == 1) & (ch == 0))

        @pl.when(coarse_end)
        def _():
            advance(i, ch, coarse_start, k_finish(i - 1, ch), None)

        @pl.when(coarse_start)
        def _():
            coarse_rest(i, ch)

        a_send(i, ch)
        return 0

    def both_chains(j, _):
        i = 1 + j
        lax.fori_loop(0, 2, lambda g, c: event(i, g), 0)

        @pl.when(i == 1)
        def _():
            rr_store(32, y.at[1], -1.0)
            rr_store(48, raw, -1.0)

        def rest(g, _):
            a_local(1 - g)
            return 0

        lax.fori_loop(0, 2, rest, 0)
        late = i > 0


        @pl.when(late & (i == 1))
        def _():
            left = jnp.concatenate([rr[0:32, :], rr[128:160, :]], axis=0)
            parts = dot_nt(left, rr[...])
            parts = parts[:, 0:128] + parts[:, 128:256]
            parts = (parts[0:32] + parts[32:64]) * (1.0 / (N * S * n_dom))
            rolled = pltpu.roll(parts[16:32], 64, 1)
            ar_start(0, 0, jnp.where(iota((C, 128), 1) < 64, parts[0:16], rolled))
            for j in range(2):
                pl.semaphore_wait(vouched.at[j], 1)

        @pl.when(late & (i == 2))
        def _():
            wait_recv(sndd, rcvd, ds, dr, ())
            dcat = jnp.concatenate(split(diag[...]), axis=1)
            far_diag = from_halo(rcvd[...], Qh)[0:S]
            hdc[...] = 0.5 / (diag[...] + dot_nn(dcat, Ql[...]) + far_diag)
            for b in range(S):
                split_pair(b, jnp.broadcast_to(hdc[b : b + 1, :], (C, N)), 0)
            hdcT[0] = dot_nt(Pn[1], vcat[0])
            for c in both_copies(hdcT, ts, tr):
                c.start()

        @pl.when(late & (i == 3))
        def _():
            wait_recv(sndm, rcvm, ms, mr, ())
            for c in both_copies(BP, bs, br):
                c.wait_recv()
            row = iota((H, N), 0)
            for j, keep in ((1, row < 16), (2, row >= 16)):
                there = jnp.where(keep, rcvm[:, 0:N], 0.0).astype(bf16)
                target = dot_tn(Pr[0:H, :], there).astype(bf16)
                for t in range(T):
                    TG[:, pl.ds((j * T + t) * N, N)] = target
            same = rcvm[:, N : 2 * N]
            half = jnp.where(row < 16, same, pltpu.roll(same, H, 1))
            SEL[...] = (half + pltpu.roll(half, 2 * H, 1)).astype(bf16)
            for c in both_copies(hdcT, ts, tr):
                c.wait_recv()

        stages = len(groups[0])
        for s in range(stages):

            @pl.when(late & (i == 2 + s))
            def _(s=s):
                total = ar_finish(0, s)
                if s + 1 < stages:
                    ar_start(0, s + 1, total)
                else:
                    gram1[...] = total
                    lane = iota((C, 128), 1)
                    work = jnp.where(lane < 16, total, jnp.where(lane < 32, pltpu.roll(total, 112, 1), 0.0))
                    for j in range(C):
                        col = jnp.sum(jnp.where(lane == j, work, 0.0), axis=1, keepdims=True)
                        row = work[j : j + 1, :] / col[j : j + 1, :]
                        unit = jnp.where(iota((C, 1), 0) == j, 1.0, 0.0)
                        work = work - (col - unit) * row
                    square = jnp.concatenate([work, jnp.zeros((128 - C, 128), f32)], axis=0).T
                    quot_t = square[16:32, :]
                    for j in range(C):
                        col = jnp.sum(jnp.where(lane == j, quot_t, 0.0), axis=1, keepdims=True)
                        qb[j] = jnp.broadcast_to(col, (C, 128))

        return 0

    lax.fori_loop(0, LAST - 1, both_chains, 0)

    def last_event(g, _):
        ch = 1 - g
        for b, value in enumerate(a_finish(LAST - 1, ch)):
            e[ch, b] = e[ch, b] + value * hd[b : b + 1, :]
        return 0

    lax.fori_loop(0, 2, last_event, 0)

    def combine(b, _):
        total = -e[1, b]
        for j in range(C):
            total = total - qb[j] * e[0, b, j : j + 1, :]
        w_ref[b] = total
        return 0

    lax.fori_loop(0, S, combine, 0)

    result = pltpu.make_async_copy(w_ref, out_ref, in_sems.at[10])
    result.start()
    store_split_v(w_ref)
    sndh[LAST, 0] = dot_nt(Pn[0], vcat[0])
    start(sndh, rcvh, hs, hr, (LAST, 0))
    rr_store(64, w_ref)
    lane = iota((C, 128), 1)
    scale = 1.0 / (N * S * n_dom)
    left = jnp.concatenate([rr[64:80, :], rr[192:208, :]], axis=0)
    parts = dot_nt(left, rr[...])
    parts = (parts[0:16, 0:128] + parts[0:16, 128:256] + parts[16:32, 0:128] + parts[16:32, 128:256]) * scale
    low = jnp.where(lane < 64, parts, 0.0)
    ar_start(1, 0, low[0:8] + pltpu.roll(low[8:16], 64, 1))

    diagonal = lax.div(lane, 16) == lax.rem(iota((C, 128), 0), 8)

    def pack_block(block):
        for shift in (16, 32, 64):
            block = block + pltpu.roll(block, shift, 1)
        block = jnp.where(diagonal, block, 0.0)
        top = jnp.sum(block[0:8], axis=0, keepdims=True)
        return jnp.concatenate([top, jnp.sum(block[8:16], axis=0, keepdims=True)], axis=0)

    def unpack_block(pair):
        wide = jnp.concatenate(
            [jnp.broadcast_to(pair[0:1], (8, 128)), jnp.broadcast_to(pair[1:2], (8, 128))], axis=0
        )
        wide = jnp.where(diagonal, wide, 0.0)
        for shift in (16, 32, 64):
            wide = wide + pltpu.roll(wide, shift, 1)
        return wide

    def lanes_from(value, source):
        return jnp.where(lane < 16, pltpu.roll(value, 128 - source, 1), 0.0)

    gram2[0:2, :] = pack_block(lanes_from(parts, 64))
    rows = reverse(w_ref)
    turned = jnp.concatenate([term[0 : 2 * H] for term in split(jnp.concatenate([rows[N : N + H], rows[N : N + H]], axis=0))], axis=0).T
    zcat[...] = turned
    gather_local(vv.at[0])
    back = turned_rows(rows)
    near = vv.at[0]
    mid = own(w_ref, D)
    for a in range(S):
        acc[0, a] = mid[a] - back[a]
    mid = far(near, jnp.zeros((H, S * C), f32))
    for a in range(S):
        v[0, a] = acc[0, a] - mid[a]
    rr_store(80, v.at[0])
    parts = dot_nt(left, rr[...])
    parts = parts[0:16, 0:128] + parts[0:16, 128:256] + parts[16:32, 0:128] + parts[16:32, 128:256]
    gram2[2:4, :] = pack_block(lanes_from(parts, 80) * scale)
    wait_recv(sndh, rcvh, hs, hr, (LAST, 0))
    terms = split(rcvh[LAST, 0])
    edges = dot_nn(zcat[...], jnp.concatenate([terms[0], terms[1], terms[0], terms[1]], axis=0))
    same = lax.div(iota((S * C, S * C), 0), C) == lax.div(iota((S * C, S * C), 1), C)
    edges = jnp.sum(jnp.where(same, edges, 0.0).reshape(S, C, S * C), axis=0)
    edges = edges[:, 0:128] + edges[:, 128:256]
    ar_start(2, 0, jnp.concatenate([gram2[2:4, :] - pack_block(edges * (2.0 * scale)), gram2[0:2, :]], axis=0))

    def drain(g, _):
        i, ch = lax.div(g, 2), lax.rem(g, 2)
        wait_send(sndh, rcvh, hs, hr, (i, ch))
        wait_send(sndc, rcvc, cs, cr, (i, ch))
        return 0

    def drain_coarse(g, _):
        m, ch = lax.div(g, 2), lax.rem(g, 2)
        wait_send(sndk, rcvk, ks, kr, (m, ch))
        wait_send(sndh, rcvq, qs, qr, (m + 3, ch), (m, ch))
        return 0

    ar_start(1, 1, ar_finish(1, 0))
    wait_send(sndh, rcvh, hs, hr, (LAST, 0))
    wait_send(sndc, rcvc, cs, cr, (LAST, 0))
    wait_send(sndd, rcvd, ds, dr, ())
    ar_start(2, 1, ar_finish(2, 0))
    lax.fori_loop(0, 2 * LAST, drain, 0)
    lax.fori_loop(0, 4, drain_coarse, 0)
    wait_send(sndm, rcvm, ms, mr, ())
    for c in both_copies(BP, bs, br) + both_copies(hdcT, ts, tr):
        c.wait_send()
    for s in range(len(groups[0])):
        ar_drain(0, s)
    ar_drain(1, 0)
    ar_drain(2, 0)
    half = ar_finish(1, 1)
    high = pltpu.roll(half, 64, 1)
    g2 = jnp.where(lane < 64, jnp.concatenate([half, high], axis=0), 0.0)

    def place(value, source, target):
        shift = (target - source) % 128
        moved = pltpu.roll(value, shift, 1) if shift else value
        return jnp.where((lane >= target) & (lane < target + 16), moved, 0.0)

    g1 = gram1[...]
    turned = jnp.concatenate([g2, jnp.zeros((128 - C, 128), f32)], axis=0).T
    xw, pw, xaw, paw = [turned[16 * j : 16 * j + 16, :] for j in range(4)]
    gb_ref[0:16, :] = (place(g1, 0, 0) + place(xw, 0, 16) + place(g1, 16, 32))[:, 0:48]
    gb_ref[32:48, :] = (place(g1, 64, 0) + place(pw, 0, 16) + place(g1, 80, 32))[:, 0:48]
    ga_ref[0:16, :] = (place(g1, 32, 0) + place(xaw, 0, 16) + place(g1, 48, 32))[:, 0:48]
    ga_ref[32:48, :] = (place(g1, 96, 0) + place(paw, 0, 16) + place(g1, 112, 32))[:, 0:48]
    wide_a = place(g2, 32, 0) + place(g2, 48, 32)
    wide_b = place(g2, 0, 0) + place(g2, 16, 32)
    ar_drain(1, 1)
    last = ar_finish(2, 1)
    image = unpack_block(last[0:2])
    square = jnp.concatenate([jnp.where(lane < 16, image, 0.0), jnp.zeros((128 - C, 128), f32)], axis=0).T
    image = 0.5 * (jnp.where(lane < 16, image, 0.0) + square[0:16, :])
    ga_ref[16:32, :] = (wide_a + place(image, 0, 16))[:, 0:48]
    gb_ref[16:32, :] = (wide_b + place(unpack_block(last[2:4]), 16, 16))[:, 0:48]
    ar_drain(2, 1)
    result.wait()


def move_results(a_in, b_in, c_in, a_out, b_out, c_out, a_mid, b_mid, c_mid, sems):
    sets = ((a_in, a_mid, a_out), (b_in, b_mid, b_out), (c_in, c_mid, c_out))
    first = [pltpu.make_async_copy(src, mid, sems.at[j]) for j, (src, mid, _) in enumerate(sets)]
    second = [pltpu.make_async_copy(mid, dst, sems.at[3 + j]) for j, (_, mid, dst) in enumerate(sets)]
    for c in first:
        c.start()
    for before, after in zip(first, second):
        before.wait()
        after.start()
    for c in second:
        c.wait()


def shards(n_dom, ar_dims, x, p, f_own, f_other, mass, cols, degree, send, pair, partner):
    vm = pltpu.VMEM
    dma = pltpu.SemaphoreType.DMA

    def size(dims):
        total = 1
        for _, g in dims:
            total *= g
        return total

    rows = (16, 8, 4)
    i32 = jnp.int32
    scratch = [
        vm((S, C, N), f32),
        vm((S, C, N), f32),
        vm((K, S, S, N), f32),
        vm((K, S, S, N), f32),
        vm((S, N), f32),
        vm((K, N), i32),
        vm((1, N), i32),
        vm((1, H), i32),
        vm((1, H), i32),
        vm((1, N), i32),
        dma((11,)),
        vm((K, S, S, N), f32),
        vm((S, S, N), f32),
        vm((S, N), f32),
        vm((S, N), f32),
        vm((S, N), f32),
        vm((2, S, C, N), f32),
        vm((2, S, C, N), f32),
        vm((2, S, C, N), f32),
        vm((2, S, C, N), f32),
        vm((2, K, S, C, N), f32),
        vm((S, C, N), f32),
        vm((C, C, 128), f32),
        vm((C, 128), f32),
        vm((C, 128), f32),
        vm((2, S * C, T * N), bf16),
        vm((S * C, T * K * N), bf16),
        vm((256, S * N), bf16),
        vm((T * N, K * N), bf16),
        vm((N + H, T * K * N), bf16),
        vm((T * H, K * N), bf16),
        vm((2, H, T * N), bf16),
        vm((T * H, N), bf16),
        vm((T * N, N), bf16),
        vm((T * H, N), bf16),
        vm((S, C, N), f32),
        vm((N, T * K * N), bf16),
        vm((T * 2 * H, K * N), bf16),
        vm((T * 3 * H, 3 * N), bf16),
        vm((3, S, S, N), f32),
        vm((3, H, S * C), f32),
        vm((N, 3 * T * N), bf16),
        vm((H, N), bf16),
        vm((3, S, C, N), f32),
        vm((S * C, 3 * T * N), bf16),
        vm((S * C, 2 * T * H), bf16),
        vm((2, N, S * C), f32),
        vm((LAST + 1, 2, H, S * C), f32),
        vm((LAST + 1, 2, H, S * C), f32),
        vm((LAST + 1, 2, H, S * C), f32),
        vm((LAST + 1, 2, H, S * C), f32),
        vm((H, 128), f32),
        vm((H, 128), f32),
        vm((2, 2, H, S * C), f32),
        vm((2, 2, H, S * C), f32),
        vm((2, 2, H, S * C), f32),
        vm((H, 2 * N), f32),
        vm((H, 2 * N), f32),
        [[vm((size(d), rows[j], 128), f32) for d in st] for j, st in enumerate(ar_dims)],
        dma((LAST + 1, 2, 2)),
        dma((LAST + 1, 2, 2)),
        dma((LAST + 1, 2, 2)),
        dma((LAST + 1, 2, 2)),
        dma((2,)),
        dma((2,)),
        dma((2, 2, 2)),
        dma((2, 2, 2)),
        dma((2, 2, 2)),
        dma((2, 2, 2)),
        dma((2,)),
        dma((2,)),
        dma((3,)),
        dma((3,)),
        dma((3,)),
        dma((3,)),
        [[dma((size(d),)) for d in st] for st in ar_dims],
        [[dma((size(d),)) for d in st] for st in ar_dims],
        pltpu.SemaphoreType.REGULAR((2,)),
    ]
    whole = pl.BlockSpec(memory_space=pltpu.VMEM)
    results = pl.pallas_call(
        functools.partial(kernel, n_dom, ar_dims),
        out_shape=(
            jax.ShapeDtypeStruct((S, C, N), f32),
            jax.ShapeDtypeStruct((3 * C, 3 * C), f32),
            jax.ShapeDtypeStruct((3 * C, 3 * C), f32),
        ),
        in_specs=[pl.BlockSpec(memory_space=pl.ANY)] * 10,
        out_specs=(pl.BlockSpec(memory_space=pl.ANY), whole, whole),
        scratch_shapes=scratch,
        compiler_params=pltpu.CompilerParams(
            collective_id=0, has_side_effects=True, vmem_limit_bytes=56 * 1024 * 1024
        ),
    )(
        x, p, f_own, f_other, mass, cols,
        degree.reshape(1, N), send.reshape(1, H), pair.reshape(1, H), partner.reshape(1, N),
    )
    any_space = pl.BlockSpec(memory_space=pl.ANY)
    return pl.pallas_call(
        move_results,
        out_shape=tuple(jax.ShapeDtypeStruct(r.shape, r.dtype) for r in results),
        in_specs=[any_space] * 3,
        out_specs=(any_space,) * 3,
        scratch_shapes=[vm(r.shape, r.dtype) for r in results] + [dma((6,))],
    )(*results)


def solution(mesh):
    n_dom = mesh.shape["dom"]
    if n_dom == 512:
        near = [[(1, 8)], [(128, 4)], [(8, 4)], [(32, 4)]]
        quick = [[(128, 4), (1, 8)], [(8, 16)]]
    else:
        near = [[(1, 2)], [(2, n_dom // 2)]]
        quick = [[(1, 2)], [(2, n_dom // 2)]]
    row = P(None, "dom")
    return jax.shard_map(
        functools.partial(shards, n_dom, (near, quick, quick)),
        mesh=mesh,
        in_specs=(
            P(None, None, "dom"),
            P(None, None, "dom"),
            P(None, None, None, "dom"),
            P(None, None, None, "dom"),
            row, row, P("dom"), P("dom"), P("dom"), P("dom"),
        ),
        out_specs=(P(None, None, "dom"), P(), P()),
        check_vma=False,
    )
```
